32 devices in a mesh: ctx: 16 (over z, x, core), wsh: 2 (over y).
Axes of the slice: x: 2, y: 2, z: 4, core: 2. Of those that a mesh axis runs over, the one named last changes fastest.
Arguments:
- tokens: bfloat16 [2, 2048, 1024], P('wsh', 'ctx'), may hold values from -6 to 6
- out_cotangent: bfloat16 [2, 2048, 1024], P('wsh', 'ctx'), may hold values from -6 to 6
- norm_gains: float32 [2, 1024], replicated, may hold values from 0.5 to 1.5
- norm_biases: float32 [2, 1024], replicated, may hold values from -2 to 2
- qkv_weight: bfloat16 [1024, 3072], P('wsh'), may hold values from -0.1875 to 0.1875
- out_weight: bfloat16 [1024, 1024], P('wsh'), may hold values from -0.75 to 0.75
- up_weight: bfloat16 [1024, 4096], P('wsh'), may hold values from -0.1875 to 0.1875
- down_weight: bfloat16 [4096, 1024], P('wsh'), may hold values from -0.09375 to 0.09375
- proj_biases: float32 [9216], replicated, may hold values from -2 to 2
- adapters: float32 [8, 16, 16384], P(None, None, ('ctx', 'wsh')), may hold values from -0.12 to 0.12
- first_moment: float32 [8, 16, 16384], P(None, None, ('ctx', 'wsh')), may hold values from -64 to 64
- second_moment: float32 [8, 16, 16384], P(None, None, ('ctx', 'wsh')), may hold values from 6400 to 102400
- doc_starts: int32 [2, 1], P('wsh'), may hold values from 0 to 0, as said below
- doc_adapter: int32 [2, 1, 8], P('wsh'), may hold values from 0 to 1, as said below
- block_order: int32 [2, 32], P('wsh'), may hold values from 0 to 31, each once within a row
Outputs:
- block_out: bfloat16 [2, 2048, 1024], P('wsh', 'ctx')
- tokens_grad: float32 [2, 2048, 1024], P('wsh', 'ctx')
- adapter_grad: float32 [8, 16, 16384], P(None, None, ('ctx', 'wsh'))
- new_adapters: float32 [8, 16, 16384], P(None, None, ('ctx', 'wsh'))
- new_first: float32 [8, 16, 16384], P(None, None, ('ctx', 'wsh'))
- new_second: float32 [8, 16, 16384], P(None, None, ('ctx', 'wsh'))
- adapters_low: bfloat16 [8, 16, 16384], P(None, None, ('ctx', 'wsh'))
The draws below stay inside these ranges and needn't reach their ends.
Inputs may be any that keep to these rules, and one draw needn't show every extreme that they name: `doc_starts`: per stream: ascending and starting at 0; a document runs from its start to the next start (the last to 2048) and has 1024 to 2048 tokens; one has exactly 2048; where a stream has several documents, the last has exactly 1024. `doc_adapter`: each document's row is one-hot. Each stream's row is a permutation; the device of ctx index c holds the stream's blocks block_order[2c] and block_order[2c + 1] of 64 tokens, in this order.
All inputs are finite; a program needn't handle non-finite values.
Results may differ from the reference program's by a relative error of at most 0.014.
Values may be sent and summed in bfloat16 or wider, within the bound.
No kernel may reach another device: no remote copies, remote signals or barrier semaphores. Data moves between devices by JAX's collectives and lax.ppermute only.
A program may use at most 384 MiB of HBM per device.

```python
import math
import jax
import jax.numpy as jnp
from jax import lax

D = 1024
HEADS = 16
FF = 4096
HEAD_DIM = 64
ROT = 16
ADAPTERS = 8
RANK = 16
TOK_DEV = 128
BLK = 64
TOKENS = 2048
STREAMS = 2
DOC_MIN = 1024
LONGEST = 2048
NDOC = 1
KEY_BLOCK = 512
STEP = 8
N_CTX = 16


def stream_lengths(length_key):
    others = NDOC - 2
    spare = TOKENS - LONGEST - DOC_MIN
    if others <= 0:
        return jnp.full((1,), LONGEST, jnp.int32)
    pair_count = others // 2
    offsets = jax.random.randint(length_key, (max(pair_count, 1),), -DOC_MIN, DOC_MIN + 1, dtype=jnp.int32)[:pair_count]
    deltas = jnp.stack([offsets, -offsets], axis=1).reshape(-1)
    if others % 2 == 1:
        deltas = jnp.concatenate([deltas, jnp.zeros((1,), jnp.int32)])
    remain = spare - 2 * DOC_MIN * others
    lengths = 2 * DOC_MIN + deltas
    lengths = lengths.at[0].add(remain // 2)
    lengths = lengths.at[others - 1].add(remain - remain // 2)
    return jnp.concatenate([jnp.full((1,), LONGEST, jnp.int32), lengths])


def draw_doc_starts(key, part):
    key = jax.random.fold_in(key, 7)
    start_rows = []
    for stream in range(STREAMS):
        stream_key = jax.random.fold_in(key, stream)
        length_key, shuffle_key = jax.random.split(stream_key)
        lengths = stream_lengths(length_key)
        shuffle = jax.random.permutation(shuffle_key, lengths.shape[0])
        lengths = lengths[shuffle]
        if NDOC > 1:
            lengths = jnp.concatenate([lengths, jnp.full((1,), DOC_MIN, jnp.int32)])
        start_rows.append(jnp.cumsum(lengths) - lengths)
    return jnp.stack(start_rows).astype(jnp.int32)


def draw_doc_adapter(key, part):
    key = jax.random.fold_in(key, 9)
    picked = jax.random.randint(key, (STREAMS, NDOC), 0, ADAPTERS, dtype=jnp.int32)
    return (picked[:, :, None] == jnp.arange(ADAPTERS, dtype=jnp.int32)[None, None, :]).astype(jnp.int32)


def level_of(key, extent, cuts, smallest, high):
    factor_of = 1.0
    for position, shards_of in cuts:
        steps = jax.random.uniform(jax.random.fold_in(jax.random.fold_in(key, 6), position), (shards_of,), jnp.float32, smallest / len(cuts), high / len(cuts))
        factor_of = factor_of * jnp.repeat(jnp.exp(steps), extent[position] // shards_of).reshape((-1,) + (1,) * (len(extent) - 1 - position))
    return factor_of


def gaussian(own_key, shape, deviation, most, shards=(), held_as=jnp.bfloat16):
    drawn = jax.random.normal(own_key, shape, jnp.float32) * deviation
    if len(shards) > 0:
        drawn = level_of(own_key, shape, shards, -0.22, 0.18) * drawn
    return jnp.clip(drawn, min=-most, max=most).astype(held_as)


def setup_inputs(seed: int = 0) -> dict:
    arg_keys = jax.random.split(jax.random.key(seed), 16)
    return {
        "tokens": gaussian(arg_keys[0], (STREAMS, TOKENS, D), 1.0, 6.0, ((0, 2), (1, 16))),
        "out_cotangent": gaussian(arg_keys[1], (STREAMS, TOKENS, D), 1.0, 6.0, ((0, 2), (1, 16))),
        "norm_gains": jnp.clip(1.0 + 0.1 * jax.random.normal(arg_keys[2], (2, D), jnp.float32), 0.5, 1.5),
        "norm_biases": gaussian(arg_keys[3], (2, D), 0.3, 2.0, (), jnp.float32),
        "qkv_weight": gaussian(arg_keys[4], (D, 3 * D), D ** -0.5, 0.1875, ((0, 2),)),
        "out_weight": gaussian(arg_keys[5], (D, D), (D // 16) ** -0.5, 0.75, ((0, 2),)),
        "up_weight": gaussian(arg_keys[6], (D, FF), D ** -0.5, 0.1875, ((0, 2),)),
        "down_weight": gaussian(arg_keys[7], (FF, D), FF ** -0.5, 0.09375, ((0, 2),)),
        "proj_biases": gaussian(arg_keys[8], (5 * D + FF,), 0.3, 2.0, (), jnp.float32),
        "adapters": gaussian(arg_keys[9], (ADAPTERS, RANK, 8 * D + 2 * FF), 0.02, 0.12, ((2, 32),), jnp.float32),
        "first_moment": jnp.clip(jax.random.uniform(arg_keys[10], (ADAPTERS, RANK, 8 * D + 2 * FF), jnp.float32, -64.0, 64.0) * level_of(arg_keys[10], (ADAPTERS, RANK, 8 * D + 2 * FF), ((2, 32),), -0.4, 0.0), -64.0, 64.0),
        "second_moment": jnp.clip(jnp.exp(math.log(102400.0) - 2.7725887 * jax.random.uniform(arg_keys[11], (ADAPTERS, RANK, 8 * D + 2 * FF), jnp.float32) ** level_of(arg_keys[11], (ADAPTERS, RANK, 8 * D + 2 * FF), ((2, 32),), -0.2, 0.2)), 6400.0, 102400.0),
        "doc_starts": draw_doc_starts(jax.random.fold_in(arg_keys[15], 71), 0),
        "doc_adapter": draw_doc_adapter(jax.random.fold_in(arg_keys[15], 71), 0),
        "block_order": jax.vmap(lambda own: jax.random.permutation(own, 2 * N_CTX))(jax.random.split(arg_keys[14], STREAMS)).reshape((STREAMS, 2 * N_CTX)).astype(jnp.int32),
    }


@jax.custom_vjp
def low(v):
    return lax.optimization_barrier(v.astype(jnp.bfloat16)).astype(jnp.float32)

@jax.custom_vjp
def low_back(v):
    return v

def low_keep(v):
    return (low(v), None)

def low_pass(kept, grad):
    return (grad,)

def back_keep(v):
    return (v, None)

def back_low(kept, grad):
    return (low(grad),)
low.defvjp(low_keep, low_pass)
low_back.defvjp(back_keep, back_low)
exact_precision = lax.Precision.HIGHEST
epsilon = 1e-05
adapter_scale = 8.0
rope_base = 10000.0
learn_rate = 0.02
beta_first = 0.5
beta_second = 0.5
weight_decay = 0.01
adam_epsilon = 1e-08
masked_value = -1e+30

def layer_norm(values, gain_row, shift_row):
    center = values - lax.optimization_barrier(jnp.mean(values, axis=-1, keepdims=True))
    spread = lax.optimization_barrier(jnp.mean(center * center, axis=-1, keepdims=True))
    return center * lax.rsqrt(spread + epsilon) * gain_row + shift_row

def rotate_half(values):
    half_size = values.shape[-1] // 2
    return jnp.concatenate([-values[..., half_size:], values[..., :half_size]], axis=-1)

def rotary(values, cosine_table, sine_table):
    turned = values[..., :ROT]
    turned = turned * cosine_table[:, None, :] + rotate_half(turned) * sine_table[:, None, :]
    return jnp.concatenate([turned, values[..., ROT:]], axis=-1)

def rope_tables(place_rows):
    frequency = rope_base ** (-jnp.arange(0, ROT, 2, dtype=jnp.float32) / ROT)
    angles = place_rows.astype(jnp.float32)[:, None] * frequency[None, :]
    angles = jnp.concatenate([angles, angles], axis=1)
    return (jnp.cos(angles), jnp.sin(angles))

def token_layout(order_row, starts_row, adapter_rows):
    held_rows = jnp.arange(TOKENS, dtype=jnp.int32)
    owner_dev = held_rows // TOK_DEV
    within = held_rows % TOK_DEV
    block_id = order_row[(2 * owner_dev + within // BLK).astype(jnp.int32)]
    stream_pos = block_id * BLK + within % BLK
    finish = jnp.concatenate([starts_row[1:], jnp.full((1,), TOKENS, jnp.int32)])
    inside = ((stream_pos[:, None] >= starts_row[None, :]) & (stream_pos[:, None] < finish[None, :])).astype(jnp.int32)
    doc_index = lax.optimization_barrier(jnp.sum(inside * jnp.arange(NDOC, dtype=jnp.int32)[None, :], axis=1))
    doc_place = stream_pos - lax.optimization_barrier(jnp.sum(inside * starts_row[None, :], axis=1))
    chosen = lax.optimization_barrier(jnp.sum(inside[:, :, None] * adapter_rows[None, :, :], axis=1))
    return (stream_pos, doc_index, doc_place, chosen)

def adapter_pair(low_adapters, in_start, in_width, out_start, out_width):
    down_part = low_adapters[:, :, in_start:in_start + in_width]
    up_term = low_adapters[:, :, out_start:out_start + out_width].reshape(ADAPTERS * RANK, out_width)
    return (down_part, up_term)

def adapted(inputs, weight, bias_vector, pair, column_mask):
    down_part, up_term = pair
    frozen_term = jnp.dot(inputs, weight, precision=exact_precision)
    inner_product_rows = jnp.einsum('ti,ari->tar', inputs, down_part, precision=exact_precision).reshape(inputs.shape[0], ADAPTERS * RANK)
    inner_product_rows = low(low_back(inner_product_rows * column_mask))
    return frozen_term + bias_vector + adapter_scale * jnp.dot(inner_product_rows, up_term, precision=exact_precision)

def attend(queries, keys_all, values_all, pos_rows, doc_rows):
    block_count = TOKENS // KEY_BLOCK

    def one_block(block_item):
        query_blk, query_pos, query_doc = block_item
        scores = jnp.einsum('qhd,khd->qhk', query_blk, keys_all, precision=exact_precision) * HEAD_DIM ** (-0.5)
        allowed = (query_doc[:, None] == doc_rows[None, :]) & (pos_rows[None, :] <= query_pos[:, None])
        scores = low_back(jnp.where(allowed[:, None, :], scores, masked_value))
        top_score = lax.optimization_barrier(jnp.max(scores, axis=-1, keepdims=True))
        weights_exp = jnp.exp(scores - top_score)
        weights_exp = weights_exp / lax.optimization_barrier(jnp.sum(weights_exp, axis=-1, keepdims=True))
        return jnp.einsum('qhk,khd->qhd', low(weights_exp), values_all, precision=exact_precision)
    stacked = lax.map(jax.checkpoint(one_block), (queries.reshape(block_count, KEY_BLOCK, HEADS, HEAD_DIM), pos_rows.reshape(block_count, KEY_BLOCK), doc_rows.reshape(block_count, KEY_BLOCK)))
    return stacked.reshape(TOKENS, HEADS, HEAD_DIM)

def reference(tokens, out_cotangent, norm_gains, norm_biases, qkv_weight, out_weight, up_weight, down_weight, proj_biases, adapters, first_moment, second_moment, doc_starts, doc_adapter, block_order):
    w_qkv = qkv_weight.astype(jnp.float32)
    w_out = out_weight.astype(jnp.float32)
    w_up = up_weight.astype(jnp.float32)
    w_down = down_weight.astype(jnp.float32)
    layouts = [token_layout(block_order[stream], doc_starts[stream], doc_adapter[stream]) for stream in range(STREAMS)]

    def forward(tokens_f, adapters_f):
        low_adapters = low(adapters_f)
        qkv_pair = adapter_pair(low_adapters, 0, D, 3 * D + FF, 3 * D)
        out_pair = adapter_pair(low_adapters, D, D, 6 * D + FF, D)
        up_pair = adapter_pair(low_adapters, 2 * D, D, 7 * D + FF, FF)
        down_pair = adapter_pair(low_adapters, 3 * D, FF, 7 * D + 2 * FF, D)
        outputs = []
        for stream in range(STREAMS):
            stream_pos, doc_index, doc_place, chosen = layouts[stream]
            column_mask = jnp.repeat(chosen.astype(jnp.float32), RANK, axis=1)
            inputs = tokens_f[stream]
            h_attn = low(layer_norm(inputs, norm_gains[0], norm_biases[0]))
            qkv_full = low_back(adapted(h_attn, w_qkv, proj_biases[0:3 * D], qkv_pair, column_mask))
            cosine_table, sine_table = rope_tables(doc_place)
            queries = low(low_back(rotary(qkv_full[:, 0:D].reshape(TOKENS, HEADS, HEAD_DIM), cosine_table, sine_table)))
            keys_all = low(low_back(rotary(qkv_full[:, D:2 * D].reshape(TOKENS, HEADS, HEAD_DIM), cosine_table, sine_table)))
            values_all = low(qkv_full[:, 2 * D:3 * D].reshape(TOKENS, HEADS, HEAD_DIM))
            attended = attend(queries, keys_all, values_all, stream_pos, doc_index)
            attended_low = low(low_back(attended.reshape(TOKENS, D)))
            attn_out = adapted(attended_low, w_out, proj_biases[3 * D:4 * D], out_pair, column_mask)
            h_mlp = low(layer_norm(inputs, norm_gains[1], norm_biases[1]))
            up_full = low_back(adapted(h_mlp, w_up, proj_biases[4 * D:4 * D + FF], up_pair, column_mask))
            hidden_low = low(jax.nn.gelu(up_full, approximate=False))
            mlp_out = adapted(hidden_low, w_down, proj_biases[4 * D + FF:5 * D + FF], down_pair, column_mask)
            outputs.append(inputs + attn_out + mlp_out)
        return jnp.stack(outputs)
    primal, pullback = jax.vjp(forward, tokens.astype(jnp.float32), adapters)
    tokens_grad, adapter_grad = pullback(out_cotangent.astype(jnp.float32))
    new_first = beta_first * first_moment + (1.0 - beta_first) * adapter_grad
    new_second = beta_second * second_moment + (1.0 - beta_second) * adapter_grad * adapter_grad
    first_hat = new_first / (1.0 - beta_first ** STEP)
    second_hat = new_second / (1.0 - beta_second ** STEP)
    new_adapters = adapters - learn_rate * (first_hat / (jnp.sqrt(second_hat) + adam_epsilon) + weight_decay * adapters)
    return (primal.astype(jnp.bfloat16), tokens_grad, adapter_grad, new_adapters, new_first, new_second, new_adapters.astype(jnp.bfloat16))
```

```python
from types import SimpleNamespace

import jax
import jax.numpy as jnp
from jax import lax
from jax.experimental import pallas as pl
from jax.experimental.pallas import tpu as pltpu
from jax.sharding import PartitionSpec as P

D = 1024
HEADS = 16
FF = 4096
HEAD_DIM = 64
ROT = 16
ADAPTERS = 8
RANK = 16
STEP = 8
COLS = 8 * D + 2 * FF
CB = 512
NB = COLS // CB
WIDE = 512
UP_CUT = 1024
DOWN_CUT = 384
TILE = 256

A_QKV, A_OUT, A_UP, A_DOWN = 0, 1, 2, 3
B_QKV, B_OUT, B_UP, B_DOWN = 7, 10, 11, 15

epsilon = 1e-05
adapter_scale = 8.0
rope_base = 10000.0
learn_rate = 0.02
beta_first = 0.5
beta_second = 0.5
weight_decay = 0.01
adam_epsilon = 1e-08
masked_value = -1e30

bf16 = jnp.bfloat16
f32 = jnp.float32

HBM = pl.BlockSpec(memory_space=pltpu.HBM)


def dot_nn(a, b):
    return jnp.dot(a, b, preferred_element_type=f32)


def dot_nt(a, b):
    return lax.dot_general(a, b, (((1,), (1,)), ((), ())), preferred_element_type=f32)


def dot_tn(a, b):
    return lax.dot_general(a, b, (((0,), (0,)), ((), ())), preferred_element_type=f32)


def shape(dims, dtype=bf16):
    return jax.ShapeDtypeStruct(tuple(dims), dtype)


def cut(index, width=D):
    return slice(index * width, (index + 1) * width)


class Stage:
    def __init__(self, loads, scalar, raw, out, targets):
        self.loads = loads
        self.scalar = scalar
        self.raw = raw
        self.out = out
        self.targets = targets
        self.waited = set()
        self.pending = []

    def __getattr__(self, name):
        buffer, copy = self.loads[name]
        if name not in self.waited:
            self.waited.add(name)
            copy.wait()
        return buffer

    def start(self, *ends):
        copy = pltpu.make_async_copy(*ends)
        copy.start()
        self.pending.append(copy)

    def store(self, buffer, at=None, into=None):
        target, sems = self.targets[id(buffer)]
        if into is not None:
            self.start(buffer, target.at[into], sems.at[0])
        elif at is None:
            self.start(buffer, target, sems.at[0])
        else:
            self.start(buffer.at[at], target.at[at], sems.at[at])


def staged(body, loads, results, raws=None, scalars=None, scratch=(), parts=None, micros=2, inside=None, alias=None):
    raws, scalars, parts, inside, alias = raws or {}, scalars or {}, parts or {}, inside or {}, alias or {}
    raw_list, raw_tree = jax.tree.flatten(raws)

    def kernel(*refs):
        refs = list(refs)

        def take(count):
            head = refs[:count]
            del refs[:count]
            return head

        scalar_from, load_from = take(len(scalars)), take(len(loads))
        raw = jax.tree.unflatten(raw_tree, take(len(raw_list)))
        targets = take(len(results))
        scalar_to, load_to, out = take(len(scalars)), take(len(loads)), take(len(results))
        (sems,) = take(1)
        out_sems = take(len(results))
        moves = [
            pltpu.make_async_copy(source, buffer, sems.at[i])
            for i, (source, buffer) in enumerate(zip(scalar_from + load_from, scalar_to + load_to))
        ]
        for move in moves:
            move.start()
        for move in moves[: len(scalars)]:
            move.wait()
        stage = Stage(
            dict(zip(loads, zip(load_to, moves[len(scalars) :]))),
            SimpleNamespace(**dict(zip(scalars, scalar_to))),
            SimpleNamespace(**raw),
            SimpleNamespace(**dict(zip(results, out))),
            {id(buffer): ends for buffer, ends in zip(out, zip(targets, out_sems))},
        )
        body(stage, *refs)
        for name in loads:
            getattr(stage, name)
        for copy in stage.pending:
            copy.wait()

    raw_names = list(raws)
    made = pl.pallas_call(
        kernel,
        out_shape=tuple(results.values()),
        in_specs=[HBM] * (len(scalars) + len(loads) + len(raw_list)),
        out_specs=(HBM,) * len(results),
        scratch_shapes=[pltpu.SMEM(a.shape, a.dtype) for a in scalars.values()]
        + [pltpu.VMEM(a.shape, a.dtype) for a in loads.values()]
        + [pltpu.VMEM(inside.get(n, s.shape), s.dtype) for n, s in results.items()]
        + [pltpu.SemaphoreType.DMA((len(loads) + len(scalars) + 1,))]
        + [pltpu.SemaphoreType.DMA((parts.get(n, 1),)) for n in results]
        + list(scratch),
        compiler_params=pltpu.CompilerParams(vmem_limit_bytes=56 * 1024 * 1024),
        input_output_aliases={
            len(scalars) + len(loads) + raw_names.index(a): list(results).index(b) for a, b in alias.items()
        },
        cost_estimate=pl.CostEstimate(flops=int(micros * 1.15e9), bytes_accessed=1024, transcendentals=0),
        name=body.__name__,
    )(*scalars.values(), *loads.values(), *raw_list)
    return SimpleNamespace(**dict(zip(results, made)))


def normalize(values):
    center = values - jnp.mean(values, axis=-1, keepdims=True)
    spread = jnp.mean(center * center, axis=-1, keepdims=True)
    scale = lax.rsqrt(spread + epsilon)
    return center * scale, scale


def give_adapters(stage):
    give = stage.out.give
    for a in range(ADAPTERS):
        give[cut(a, RANK), :] = stage.adapters[a].astype(bf16)
    row = lax.broadcasted_iota(jnp.int32, (RANK, give.shape[1]), 0)
    lane = lax.broadcasted_iota(jnp.int32, (RANK, give.shape[1]), 1)
    choice = jnp.zeros((RANK, give.shape[1]), f32)
    for j in range(stage.scalar.chosen.shape[1]):
        for a in range(ADAPTERS):
            choice = jnp.where((row == j) & (lane == a), stage.scalar.chosen[0, j, a].astype(f32), choice)
    give[ADAPTERS * RANK :, :] = choice.astype(bf16)
    stage.store(give)


def layer_norms(stage, sems):
    raw, out = stage.raw, stage.out
    copies = [
        pltpu.make_async_copy(raw.out.at[own_part(raw.out, 4), :], out.o, sems.at[0]),
        pltpu.make_async_copy(raw.up.at[own_part(raw.up, 4), :UP_CUT], out.t, sems.at[1]),
    ]
    for copy in copies:
        copy.start()
    normed, _ = normalize(stage.tok[...].astype(f32))
    gain, shift = stage.gain, stage.shift
    attn = stage.out.attn
    attn[...] = (normed * gain[0:1, :] + shift[0:1, :]).astype(bf16)
    half = pl.multiple_of((1 - lax.axis_index("wsh")) * (D // 2), D // 2)
    stage.out.give[...] = attn[:, pl.ds(half, D // 2)]
    stage.store(stage.out.give)
    stage.store(attn)
    for copy, buffer in zip(copies, (out.o, out.t)):
        copy.wait()
        stage.store(buffer)
    stage.out.mlp[...] = (normed * gain[1:2, :] + shift[1:2, :]).astype(bf16)
    stage.store(stage.out.mlp)


def choose_adapters(stage):
    adapters, given = stage.adapters, stage.given
    rows = stage.out.rows
    target, sems = stage.targets[id(rows)]
    columns = adapters.shape[2]
    wsh = lax.axis_index("wsh")
    for j in range(rows.shape[0] // RANK):
        index = 0
        for a in range(1, ADAPTERS):
            index = index + a * stage.scalar.chosen[0, j, a]
        start = pl.multiple_of(index * RANK, RANK)
        own_at = pl.multiple_of(wsh * columns, 128)
        other_at = pl.multiple_of((1 - wsh) * columns, 128)
        rows[cut(j, RANK), pl.ds(own_at, columns)] = adapters[index].astype(bf16)
        rows[cut(j, RANK), pl.ds(other_at, columns)] = given[pl.ds(start, RANK), :]
    for i in range(target.shape[0]):
        stage.start(rows, target.at[i], sems.at[i])


def part_orders(share):
    ctx = lax.axis_index("ctx")
    if share == 2:
        return ctx % 2, 1 - ctx % 2
    mine = ctx % 2 * 2 + ctx // 2 % 2
    return mine, mine ^ 1, mine ^ 2, mine ^ 3


def rows_at(first, count):
    return pl.ds(pl.multiple_of(first, count), count)


def own_part(weight, share):
    rows = weight.shape[0] // share
    return rows_at(part_orders(share)[0] * rows, rows)


def cut_parts(stage, sems):
    raw, out = stage.raw, stage.out
    plan = [
        (out.u, raw.up, own_part(raw.up, 4), UP_CUT, FF, 0),
        (out.d, raw.down, own_part(raw.down, 4), 0, DOWN_CUT, 0),
        (out.e, raw.down, own_part(raw.down, 2), DOWN_CUT, D, 0),
        (out.w, raw.qkv, own_part(raw.qkv, 2), 0, 3 * D, 0),
    ]
    copies = []
    for i, (buffer, source, rows, first, last, at) in enumerate(plan):
        copies.append(
            pltpu.make_async_copy(source.at[rows, first:last], buffer.at[:, at : at + last - first], sems.at[i])
        )
        copies[-1].start()
    for i, (buffer, *_) in enumerate(plan):
        copies[i].wait()
        if i + 1 == len(plan) or plan[i + 1][0] is not buffer:
            stage.store(buffer)


def place_weights(own, chunks, target, sems, first):
    half = own.shape[0]
    own_half = lax.axis_index("wsh")
    copies = [pltpu.make_async_copy(own, target.at[rows_at(own_half * half, half), :], sems.at[first])]
    for column, source_column, width, parts in chunks:
        rows = half // len(parts)
        for order, part in zip(part_orders(len(parts)), parts):
            copies.append(
                pltpu.make_async_copy(
                    part.at[:, source_column : source_column + width],
                    target.at[rows_at((1 - own_half) * half + order * rows, rows), column : column + width],
                    sems.at[first + len(copies)],
                )
            )
    for copy in copies:
        copy.start()
    return copies


def turn(values, tab, sign):
    left = pltpu.roll(values, 120, 1)
    right = pltpu.roll(values, 8, 1)
    return values * tab[0] + sign * (left * tab[1] + right * tab[2])


def swap_halves(first, second):
    low = lax.broadcasted_iota(jnp.int32, first.shape, 1) < HEAD_DIM
    one = jnp.where(low, first, pltpu.roll(second, HEAD_DIM, 1))
    two = jnp.where(low, pltpu.roll(first, HEAD_DIM, 1), second)
    return one, two


def both_streams(stage):
    half = pl.multiple_of(lax.axis_index("wsh") * (D // 2), D // 2)
    return jnp.concatenate([stage.h[:, pl.ds(half, D // 2)], stage.given[...]], axis=0)


def weight_columns(source, first, weights, sems):
    copies = []
    for n in range(weights.shape[0]):
        copies.append(
            pltpu.make_async_copy(source.at[:, first + n * WIDE : first + (n + 1) * WIDE], weights.at[n], sems.at[n])
        )
        copies[-1].start()
    return copies


def partial_qk(stage, weights, sems):
    copies = weight_columns(stage.raw.qkv, 0, weights, sems)
    both = both_streams(stage)
    rows = both.shape[0] // 2
    for n, copy in enumerate(copies):
        copy.wait()
        part = dot_nn(both, weights[n])
        stage.out.give[:, cut(n, WIDE)] = part[rows:].astype(bf16)
        stage.out.kept[n] = part[:rows]
    stage.store(stage.out.give)
    stage.store(stage.out.kept)


def partial_v(stage, weights, sems):
    copies = weight_columns(stage.raw.qkv, 2 * D, weights, sems)
    both = both_streams(stage)
    rows = both.shape[0] // 2
    for n, copy in enumerate(copies):
        copy.wait()
        part = dot_nn(both, weights[n])
        stage.out.give[:, cut(n, WIDE)] = part[rows:].astype(bf16)
        stage.out.kept[n] = part[:rows]
    stage.store(stage.out.give)
    stage.store(stage.out.kept)


def queries_keys(stage, wo, sems):
    copies = place_weights(stage.raw.out, [(0, 0, D, stage.raw.o)], wo, sems, 0)
    low, mask, bias, tab, kept, given = stage.low, stage.mask[...], stage.bias, stage.tab, stage.kept, stage.given
    inner = (dot_nt(stage.h[...], low[A_QKV]) * mask).astype(bf16)
    stage.out.inner[...] = inner
    stage.store(stage.out.inner)
    grad_inner = (adapter_scale * dot_nt(stage.grad[...], low[B_OUT]) * mask).astype(bf16)
    stage.out.grad_inner[...] = grad_inner
    stage.store(stage.out.grad_inner)
    steps = D // WIDE
    for n in range(steps):
        sides = []
        for kind in range(2):
            at = cut(kind * steps + n, WIDE)
            part = kept[kind * steps + n] + given[:, at].astype(f32) + bias[:, at]
            sides.append(part + adapter_scale * dot_nn(inner, low[B_QKV + kind][:, cut(n, WIDE)]))
        for pair in range(WIDE // 128):
            query = turn(sides[0][:, cut(pair, 128)], tab, 1.0) * HEAD_DIM**-0.5
            key = turn(sides[1][:, cut(pair, 128)], tab, 1.0)
            head = n * WIDE // HEAD_DIM + 2 * pair
            for i, both in enumerate(swap_halves(query, key)):
                stage.out.send[head + i] = both.astype(bf16)
    stage.store(stage.out.send, into=(slice(None), 0))
    base, grad, kept = stage.out.base, stage.grad[...], stage.kept_v
    for n in range(steps):
        base[n] = kept[n] + bias[:, 2 * D + n * WIDE : 2 * D + (n + 1) * WIDE]
        base[n] += adapter_scale * dot_nn(inner, low[B_QKV + 2][:, cut(n, WIDE)])
    for copy in copies:
        copy.wait()
    for n in range(steps):
        base[steps + n] = dot_nt(grad, wo[cut(n, WIDE), :]) + dot_nn(grad_inner, low[A_OUT][:, cut(n, WIDE)])
    stage.store(base)


def values_grads(stage):
    base, given = stage.base, stage.given
    steps = D // WIDE
    for n in range(steps):
        value = base[n] + given[:, cut(n, WIDE)].astype(f32)
        grad = base[steps + n]
        for pair in range(WIDE // 128):
            head = n * WIDE // HEAD_DIM + 2 * pair
            for i, both in enumerate(swap_halves(value[:, cut(pair, 128)], grad[:, cut(pair, 128)])):
                stage.out.send[head + i] = both.astype(bf16)
    stage.store(stage.out.send, into=(slice(None), 1))


def attention(stage, xt, dks, dvs, ks, vs, aq, s_scr, e_scr):
    order = stage.scalar.order
    rows = aq.shape[0]
    count = rows // TILE
    blocks = order.shape[1]
    half = rows // blocks
    hd = HEAD_DIM
    x = stage.arrived
    per = x.shape[2] // half
    for i in range(blocks):
        start = pl.multiple_of(order[0, i] * half, half)
        for side in range(2):
            aq[pl.ds(start, half), cut(side, 2 * hd)] = x[i // per, side, cut(i % per, half), :]
    for t in range(count):
        part = aq[cut(t, TILE), :]
        ks[cut(t, TILE), :] = part[:, hd : 2 * hd]
        vs[cut(t, TILE), :] = part[:, 2 * hd : 3 * hd]
        xt[:, cut(t, TILE)] = part.T
    dks[...] = jnp.zeros_like(dks)
    dvs[...] = jnp.zeros_like(dvs)
    key_row = lax.broadcasted_iota(jnp.int32, (TILE, TILE), 0)
    query_col = lax.broadcasted_iota(jnp.int32, (TILE, TILE), 1)
    seen = key_row <= query_col
    for b in range(count):
        at = cut(b, TILE)
        q_t = xt[0:hd, at]
        g_t = xt[3 * hd : 4 * hd, at]
        top = jnp.full((8, TILE), masked_value, f32)
        for t in range(b + 1):
            s = dot_nn(ks[cut(t, TILE), :], q_t)
            if t == b:
                s = jnp.where(seen, s, masked_value)
            s_scr[cut(t, TILE), :] = s
            top = jnp.maximum(top, jnp.max(s.reshape(TILE // 8, 8, TILE), axis=0))
        top = jnp.max(top, axis=0, keepdims=True)
        total = jnp.zeros((8, TILE), f32)
        att = jnp.zeros((hd, TILE), f32)
        for t in range(b + 1):
            e = jnp.exp(s_scr[cut(t, TILE), :] - top)
            total = total + jnp.sum(e.reshape(TILE // 8, 8, TILE), axis=0)
            e = e.astype(bf16)
            e_scr[cut(t, TILE), :] = e
            att = att + dot_nn(xt[2 * hd : 3 * hd, cut(t, TILE)], e)
        inverse = 1.0 / jnp.sum(total, axis=0, keepdims=True)
        att = att * inverse
        g_f = g_t.astype(f32)
        delta = jnp.sum(g_f * att, axis=0, keepdims=True) * inverse
        g_n = (g_f * inverse).astype(bf16)
        dq = jnp.zeros((hd, TILE), f32)
        for t in range(b + 1):
            e = e_scr[cut(t, TILE), :]
            dp = dot_nn(vs[cut(t, TILE), :], g_n)
            ds = (e.astype(f32) * (dp - delta)).astype(bf16)
            dq = dq + dot_nn(xt[hd : 2 * hd, cut(t, TILE)], ds)
            dks[cut(t, TILE), :] += dot_nt(ds, q_t)
            dvs[cut(t, TILE), :] += dot_nt(e, g_n)
        both = jnp.concatenate([att, dq * hd**-0.5], axis=0)
        aq[at, 0 : 2 * hd] = both.T.astype(bf16)
    for t in range(count):
        aq[cut(t, TILE), 2 * hd : 3 * hd] = dks[cut(t, TILE), :].astype(bf16)
        aq[cut(t, TILE), 3 * hd :] = dvs[cut(t, TILE), :].astype(bf16)
    for i in range(blocks):
        start = pl.multiple_of(order[0, i] * half, half)
        stage.out.back[cut(i, half), :] = aq[pl.ds(start, half), :]
    stage.store(stage.out.back)


def attention_one_document(order, arrived):
    rows = arrived.shape[0] * arrived.shape[2]
    hd = HEAD_DIM
    return staged(
        attention,
        dict(arrived=arrived),
        dict(back=shape((rows, 4 * hd))),
        scalars=dict(order=order),
        scratch=[
            pltpu.VMEM((4 * hd, rows), bf16),
            pltpu.VMEM((rows, hd), f32),
            pltpu.VMEM((rows, hd), f32),
            pltpu.VMEM((rows, hd), bf16),
            pltpu.VMEM((rows, hd), bf16),
            pltpu.VMEM((rows, 4 * hd), bf16),
            pltpu.VMEM((rows, TILE), f32),
            pltpu.VMEM((rows, TILE), bf16),
        ],
        micros=17,
    ).back


def attention_documents(arrived, pos, doc, groups, first_row):
    rows = arrived.shape[0] * arrived.shape[2]
    hd = HEAD_DIM
    qk, vg = (arrived[:, side].reshape(rows, 2 * hd) for side in range(2))
    q, k, v, g = qk[:, :hd], qk[:, hd:], vg[:, :hd], vg[:, hd:]
    if groups is not None:
        both = lax.all_gather(jnp.concatenate([k, v], 1), "ctx", axis=0, tiled=True, axis_index_groups=groups)
        k, v = both[:, :hd], both[:, hd:]
    step = 512
    my_pos = lax.dynamic_slice_in_dim(pos, first_row, rows)
    my_doc = lax.dynamic_slice_in_dim(doc, first_row, rows)

    def one(sums, item):
        q_b, g_b, pos_b, doc_b = item
        scores = dot_nt(q_b, k)
        allowed = (doc_b[:, None] == doc[None, :]) & (pos[None, :] <= pos_b[:, None])
        scores = jnp.where(allowed, scores, masked_value)
        top = jnp.max(scores, axis=1, keepdims=True)
        weights = jnp.exp(scores - top)
        weights = weights / jnp.sum(weights, axis=1, keepdims=True)
        weights_low = weights.astype(bf16)
        att = dot_nn(weights_low, v)
        delta = jnp.sum(g_b.astype(f32) * att, axis=1, keepdims=True)
        ds = (weights * (dot_nt(g_b, v) - delta)).astype(bf16)
        dq = dot_nn(ds, k) * hd**-0.5
        sums = (sums[0] + dot_tn(ds, q_b), sums[1] + dot_tn(weights_low, g_b))
        return sums, jnp.concatenate([att, dq], 1).astype(bf16)

    zero = jnp.zeros((k.shape[0], hd), f32)
    split = lambda a: a.reshape((rows // step, step) + a.shape[1:])
    sums, att_dq = lax.scan(one, (zero, zero), tuple(map(split, (q, g, my_pos, my_doc))))
    sums = jnp.concatenate(sums, 1)
    if groups is not None:
        sums = lax.psum_scatter(sums, "ctx", scatter_dimension=0, tiled=True, axis_index_groups=groups)
    return jnp.concatenate([att_dq.reshape(rows, 2 * hd), sums.astype(bf16)], axis=1)


def mlp_both_ways(stage, wu, wd, sems):
    raw = stage.raw
    copies = place_weights(raw.up, [(0, 0, UP_CUT, raw.t), (UP_CUT, 0, FF - UP_CUT, raw.u)], wu, sems, 0)
    copies += place_weights(raw.down, [(0, 0, DOWN_CUT, raw.d), (DOWN_CUT, 0, D - DOWN_CUT, raw.e)], wd, sems, 9)
    h, grad, low, mask, bias = stage.h[...], stage.grad[...], stage.low, stage.mask[...], stage.bias
    rows, rank = mask.shape
    out, back, grads = stage.out.out, stage.out.back, stage.out.grads
    inner_up = (dot_nt(h, low[A_UP]) * mask).astype(bf16)
    gi_down = (adapter_scale * dot_nt(grad, low[B_DOWN]) * mask).astype(bf16)
    for copy in copies:
        copy.wait()
    inner_down = jnp.zeros((rows, rank), f32)
    gi_up = jnp.zeros((rows, rank), f32)
    out[...] = jnp.zeros_like(out)
    back[...] = jnp.zeros_like(back)
    for f in range(FF // CB):
        big, small = divmod(f * CB, D)
        a_down = low[A_DOWN + big][:, small : small + CB]
        b_up = low[B_UP + big][:, small : small + CB]
        up = dot_nn(h, wu[:, cut(f, CB)]) + bias[:, 4 * D + f * CB : 4 * D + (f + 1) * CB]
        up = up + adapter_scale * dot_nn(inner_up, b_up)
        spread = 0.5 * (1.0 + lax.erf(up * (0.5**0.5)))
        hidden = (up * spread).astype(bf16)
        slope = spread + up * (jnp.exp(-0.5 * up * up) * (0.5 / jnp.pi) ** 0.5)
        down_rows = wd[cut(f, CB), :]
        out[...] += dot_nn(hidden, down_rows)
        inner_down = inner_down + dot_nt(hidden, a_down)
        grad_hidden = dot_nt(grad, down_rows) + dot_nn(gi_down, a_down)
        grad_up = (grad_hidden * slope).astype(bf16)
        back[...] += dot_nt(grad_up, wu[:, cut(f, CB)])
        gi_up = gi_up + dot_nt(grad_up, b_up)
        grads[2 + f] = dot_tn(gi_down, hidden).astype(bf16)
        grads[10 + f] = (adapter_scale * dot_tn(inner_up, grad_up)).astype(bf16)
    inner_down = (inner_down * mask).astype(bf16)
    gi_up = (adapter_scale * gi_up * mask).astype(bf16)
    for i in range(2):
        at = cut(i, CB)
        grads[i] = dot_tn(gi_up, h[:, at]).astype(bf16)
        grads[18 + i] = (adapter_scale * dot_tn(inner_down, grad[:, at])).astype(bf16)
    stage.store(grads)
    out[...] += bias[:, 4 * D + FF : 5 * D + FF] + adapter_scale * dot_nn(inner_down, low[B_DOWN])
    stage.store(out)
    back[...] += dot_nn(gi_up, low[A_UP])
    stage.store(back)


def adapter_gradients(stage):
    arrived, tab = stage.arrived, stage.tab
    att, gq, flat = stage.out.att, stage.out.gq, stage.out.flat
    for pair in range(HEADS // 2):
        at = cut(pair, 128)
        one, two = arrived[2 * pair].astype(f32), arrived[2 * pair + 1].astype(f32)
        attended, query = swap_halves(one[:, :128], two[:, :128])
        key, value = swap_halves(one[:, 128:], two[:, 128:])
        att[:, at] = attended.astype(bf16)
        for kind, part in enumerate((turn(query, tab, -1.0), turn(key, tab, -1.0), value)):
            gq[:, kind * D + pair * 128 : kind * D + (pair + 1) * 128] = part.astype(bf16)
    stage.store(att)
    stage.store(gq)
    low, mask, h, grad = stage.low, stage.mask[...], stage.h, stage.grad
    inner_out = (dot_nt(att[...], low[A_OUT]) * mask).astype(bf16)
    stage.out.inner_out[...] = inner_out
    stage.store(stage.out.inner_out)
    gi = sum(dot_nt(gq[:, cut(i)], low[B_QKV + i]) for i in range(3))
    gi = (adapter_scale * gi * mask).astype(bf16)
    stage.out.gi[...] = gi
    stage.store(stage.out.gi)
    per = D // CB

    def put(block, value):
        for i in range(per):
            flat[block * per + i] = value[:, cut(i, CB)].astype(bf16)

    put(A_QKV, dot_tn(gi, h[...]))
    put(A_OUT, dot_tn(stage.grad_inner[...], att[...]))
    put(B_OUT, adapter_scale * dot_tn(inner_out, grad[...]))
    for i in range(3):
        put(B_QKV + i, adapter_scale * dot_tn(stage.inner[...], gq[:, cut(i)]))
    flat[A_UP * per : A_UP * per + 10] = stage.mlp[0:10]
    flat[B_UP * per : B_UP * per + 10] = stage.mlp[10:20]
    stage.store(flat)


def outputs(stage, wq, wo, sems):
    raw = stage.raw
    o_copies = place_weights(raw.out, [(0, 0, D, raw.o)], wo, sems, 0)
    q_copies = place_weights(raw.qkv, [(0, 0, 3 * D, raw.w)], wq, sems, 5)
    tok, grad, low, gain, bias = stage.tok, stage.grad, stage.low, stage.gain, stage.bias
    att, inner_out, mlp_out, back = stage.att[...], stage.inner_out[...], stage.mlp_out, stage.back
    block = stage.out.block
    for copy in o_copies:
        copy.wait()
    for n in range(D // WIDE):
        at = cut(n, WIDE)
        part = dot_nn(att, wo[:, at]) + bias[:, 3 * D + n * WIDE : 3 * D + (n + 1) * WIDE]
        part = part + adapter_scale * dot_nn(inner_out, low[B_OUT][:, at])
        block[:, at] = (part + tok[:, at].astype(f32) + mlp_out[:, at]).astype(bf16)
    stage.store(block)
    normed, scale = normalize(tok[...].astype(f32))
    for copy in q_copies:
        copy.wait()
    grad_h = dot_nt(stage.gq[...], wq[...]) + dot_nn(stage.gi[...], low[A_QKV])
    grad_n = grad_h * gain[0:1, :] + back[...] * gain[1:2, :]
    grad_v = grad_n - jnp.mean(grad_n, axis=-1, keepdims=True) - normed * jnp.mean(grad_n * normed, axis=-1, keepdims=True)
    stage.out.tokens[...] = grad[...].astype(f32) + scale * grad_v
    stage.store(stage.out.tokens)


def adamw(stage):
    chosen, parts, out = stage.scalar.chosen, stage.parts, stage.out
    sums = []
    for stream in range(2):
        total = parts[stream].astype(f32)
        for source in range(stream + 2, parts.shape[0], 2):
            total = total + parts[source].astype(f32)
        sums.append(total)
    ndoc = sums[0].shape[0] // RANK
    for a in range(ADAPTERS):
        grad = None
        for stream in range(2):
            for j in range(ndoc):
                pick = chosen[stream, j, a].astype(f32)
                term = pick * sums[stream][cut(j, RANK), :]
                grad = term if grad is None else grad + term
        new_first = beta_first * stage.first[a] + (1.0 - beta_first) * grad
        new_second = beta_second * stage.second[a] + (1.0 - beta_second) * grad * grad
        first_hat = new_first / (1.0 - beta_first**STEP)
        second_hat = new_second / (1.0 - beta_second**STEP)
        old = stage.adapters[a]
        new = old - learn_rate * (first_hat / (jnp.sqrt(second_hat) + adam_epsilon) + weight_decay * old)
        for buffer, value in (
            (out.grad, grad),
            (out.new, new),
            (out.first, new_first),
            (out.second, new_second),
            (out.low, new.astype(bf16)),
        ):
            buffer[a] = value
            stage.store(buffer, a)


def stream_layout(order_row, starts_row, rows, total_rows, half_dev):
    slot = rows // half_dev
    picked = (slot[:, None] == jnp.arange(order_row.shape[0], dtype=jnp.int32)[None, :]).astype(jnp.int32)
    pos = jnp.sum(picked * order_row[None, :], axis=1) * half_dev + rows % half_dev
    finish = jnp.concatenate([starts_row[1:], jnp.full((1,), total_rows, jnp.int32)])
    inside = ((pos[:, None] >= starts_row[None, :]) & (pos[:, None] < finish[None, :])).astype(jnp.int32)
    doc = jnp.sum(inside * jnp.arange(starts_row.shape[0], dtype=jnp.int32)[None, :], axis=1)
    place = pos - jnp.sum(inside * starts_row[None, :], axis=1)
    return pos, doc, place, inside


def turn_tables(place):
    frequency = rope_base ** (-jnp.arange(0, ROT, 2, dtype=f32) / ROT)
    lane = jnp.arange(128, dtype=jnp.int32) % HEAD_DIM
    angles = place.astype(f32)[:, None] * jnp.tile(frequency, 128 // (ROT // 2))[None, :]
    cosine = jnp.where(lane < ROT, jnp.cos(angles), 1.0)
    sine = jnp.sin(angles)
    left = jnp.where(lane < ROT // 2, -sine, 0.0)
    right = jnp.where((lane >= ROT // 2) & (lane < ROT), sine, 0.0)
    return jnp.stack([cosine, left, right])


def tie(first, *others):
    return lax.optimization_barrier((first,) + others)[0]


def on_device(
    tokens,
    out_cotangent,
    norm_gains,
    norm_biases,
    qkv_weight,
    out_weight,
    up_weight,
    down_weight,
    proj_biases,
    adapters,
    first_moment,
    second_moment,
    doc_starts,
    doc_adapter,
    block_order,
):
    n_ctx = lax.axis_size("ctx")
    n_dev = n_ctx * lax.axis_size("wsh")
    ctx = lax.axis_index("ctx")
    wsh = lax.axis_index("wsh")
    tok_dev = tokens.shape[1]
    half_dev = tok_dev // 2
    total_rows = tok_dev * n_ctx
    ndoc = doc_starts.shape[1]
    rank = ndoc * RANK
    columns = adapters.shape[2]
    tok, grad = tokens[0], out_cotangent[0]
    bias = proj_biases[None, :]

    def to_y(a, name):
        with jax.named_scope("y_" + name):
            return lax.ppermute(a, "wsh", [(0, 1), (1, 0)])

    def to_x(a, name):
        with jax.named_scope("x_" + name):
            return lax.ppermute(a, "ctx", [(i, i ^ 2) for i in range(n_ctx)])

    def to_core(a, name):
        with jax.named_scope("c_" + name):
            return lax.ppermute(a, "ctx", [(i, i ^ 1) for i in range(n_ctx)])

    give = staged(
        give_adapters,
        dict(adapters=adapters),
        dict(give=shape(((ADAPTERS + 1) * RANK, columns))),
        scalars=dict(chosen=doc_adapter),
    ).give
    adapters_given = to_y(give, "adapters")
    normed = staged(
        layer_norms,
        dict(tok=tie(tok, give), gain=norm_gains, shift=norm_biases),
        dict(
            attn=shape(tok.shape),
            mlp=shape(tok.shape),
            give=shape((tok_dev, D // 2)),
            o=shape((D // 8, D)),
            t=shape((D // 8, UP_CUT)),
        ),
        raws=dict(out=out_weight, up=up_weight),
        scratch=[pltpu.SemaphoreType.DMA((2,))],
    )
    h_attn, h_mlp = normed.attn, normed.mlp
    o_y = to_y(normed.o, "o")
    given = to_y(normed.give, "h")
    chosen_rows = staged(
        choose_adapters,
        dict(adapters=adapters, given=tie(adapters_given, h_attn)),
        dict(rows=shape((n_ctx, rank, 2 * columns))),
        scalars=dict(chosen=doc_adapter),
        parts=dict(rows=n_ctx),
        inside=dict(rows=(rank, 2 * columns)),
    ).rows
    low = lax.all_to_all(chosen_rows, "ctx", 0, 0, tiled=True)
    if n_ctx != HEADS:
        low = low.reshape(COLS // D, n_ctx // HEADS, rank, 2 * columns).transpose(0, 2, 1, 3).reshape(COLS // D, rank, D)

    t_y = to_y(tie(normed.t, o_y), "t")
    o_x = to_x(o_y, "o")
    both = staged(
        partial_qk,
        dict(h=h_attn, given=tie(given, chosen_rows)),
        dict(give=shape((tok_dev, 2 * D)), kept=shape((2 * D // WIDE, tok_dev, WIDE), f32)),
        raws=dict(qkv=qkv_weight),
        scratch=[pltpu.VMEM((2 * D // WIDE, D // 2, WIDE), bf16), pltpu.SemaphoreType.DMA((2 * D // WIDE,))],
        micros=3,
    )
    kept_qk, give_qk = both.kept, both.give
    given_qk = to_y(give_qk, "qk")
    both = staged(
        partial_v,
        dict(h=tie(h_attn, give_qk, t_y), given=given),
        dict(give=shape((tok_dev, D)), kept=shape((D // WIDE, tok_dev, WIDE), f32)),
        raws=dict(qkv=qkv_weight),
        scratch=[pltpu.VMEM((D // WIDE, D // 2, WIDE), bf16), pltpu.SemaphoreType.DMA((D // WIDE,))],
        micros=3,
    )
    given_v = to_y(both.give, "v")
    my_rows = ctx * tok_dev + jnp.arange(tok_dev, dtype=jnp.int32)
    _, _, place, inside = stream_layout(tie(block_order, both.give)[0], doc_starts[0], my_rows, total_rows, half_dev)
    mask = jnp.repeat(inside.astype(f32), RANK, axis=1)
    tab = turn_tables(place)
    t_x = to_x(t_y, "t")

    def quarters(y, x, name, *after):
        return [y, x, to_core(tie(y, *after), name + "y"), to_core(tie(x, *after), name + "x")]

    def halves(y, name, *after):
        return [y, to_core(tie(y, *after), name)]

    o_parts, t_parts = quarters(o_y, o_x, "o"), quarters(t_y, t_x, "t")
    cuts = staged(
        cut_parts,
        {},
        dict(
            u=shape((D // 8, FF - UP_CUT)),
            d=shape((FF // 8, DOWN_CUT)),
            e=shape((FF // 4, D - DOWN_CUT)),
            w=shape((D // 4, 3 * D)),
        ),
        raws=dict(up=tie(up_weight, both.give), down=down_weight, qkv=qkv_weight),
        scratch=[pltpu.SemaphoreType.DMA((4,))],
    )
    heads = shape((HEADS, 2, tok_dev, 2 * HEAD_DIM))
    one = (HEADS, tok_dev, 2 * HEAD_DIM)
    made = staged(
        queries_keys,
        dict(
            h=tie(h_attn, cuts.u),
            grad=grad,
            low=low,
            mask=mask,
            bias=bias,
            tab=tab,
            kept=kept_qk,
            given=given_qk,
            kept_v=both.kept,
        ),
        dict(
            inner=shape((tok_dev, rank)),
            grad_inner=shape((tok_dev, rank)),
            send=heads,
            base=shape((2 * D // WIDE, tok_dev, WIDE), f32),
        ),
        raws=dict(out=out_weight, o=o_parts),
        inside=dict(send=one),
        scratch=[pltpu.VMEM((D, D), bf16), pltpu.SemaphoreType.DMA((5,))],
        micros=4,
    )
    inner_qkv, grad_inner_out = made.inner, made.grad_inner
    made = staged(
        values_grads,
        dict(base=made.base, given=given_v),
        dict(send=heads),
        raws=dict(send=made.send),
        inside=dict(send=one),
        alias=dict(send="send"),
        micros=3,
    )
    parts = n_ctx // HEADS
    near = None if parts == 1 else [[g * HEADS + i for i in range(HEADS)] for g in range(parts)]

    def exchange(a):
        return lax.all_to_all(a, "ctx", 0, 0, tiled=True, axis_index_groups=near)

    u_y = to_y(cuts.u, "u")
    d_y = to_y(tie(cuts.d, u_y), "d")
    e_y = to_y(tie(cuts.e, u_y), "e")
    u_x = to_x(u_y, "u")

    other = adapters_given[ADAPTERS * RANK : ADAPTERS * RANK + ndoc, :ADAPTERS].astype(jnp.int32)[None]
    chosen = jnp.where(wsh == 0, jnp.concatenate([doc_adapter, other]), jnp.concatenate([other, doc_adapter]))

    arrived = tie(exchange(made.send), u_y, *t_parts, chosen)
    if parts == 1 and ndoc == 1:
        done = attention_one_document(block_order, arrived)
    else:
        all_pos, all_doc, _, _ = stream_layout(
            block_order[0], doc_starts[0], jnp.arange(total_rows, dtype=jnp.int32), total_rows, half_dev
        )
        far = None if parts == 1 else [[g * HEADS + i for g in range(parts)] for i in range(HEADS)]
        done = attention_documents(arrived, all_pos, all_doc, far, ctx // HEADS * HEADS * tok_dev)
    d_x = to_x(tie(d_y, done), "d")
    u_parts, d_parts = quarters(u_y, u_x, "u", done), quarters(d_y, d_x, "d", done)
    back = exchange(tie(done.reshape(HEADS, tok_dev, 4 * HEAD_DIM), *u_parts, *d_parts, e_y))

    w_y = to_y(tie(cuts.w, done), "w")
    mlp = staged(
        mlp_both_ways,
        dict(h=h_mlp, grad=grad, low=low, mask=mask, bias=bias),
        dict(out=shape((tok_dev, D), f32), back=shape((tok_dev, D), f32), grads=shape((20, rank, CB))),
        raws=dict(
            up=up_weight,
            down=down_weight,
            t=t_parts,
            u=u_parts,
            d=d_parts,
            e=halves(e_y, "e", done),
        ),
        scratch=[
            pltpu.VMEM((D, FF), bf16),
            pltpu.VMEM((FF, D), bf16),
            pltpu.SemaphoreType.DMA((18,)),
        ],
        micros=0.1,
    )
    tail = staged(
        adapter_gradients,
        dict(
            arrived=back,
            tab=tab,
            low=low,
            mask=mask,
            h=h_attn,
            grad=grad,
            inner=inner_qkv,
            grad_inner=grad_inner_out,
            mlp=mlp.grads,
        ),
        dict(
            att=shape((tok_dev, D)),
            gq=shape((tok_dev, 3 * D)),
            inner_out=shape((tok_dev, rank)),
            gi=shape((tok_dev, rank)),
            flat=shape((NB, rank, CB)),
        ),
        micros=5,
    )
    flat = tail.flat
    if columns != CB:
        flat = flat.reshape(NB, rank, CB // columns, columns).transpose(0, 2, 1, 3).reshape(n_dev, rank, columns)
    shares = lax.all_to_all(flat, ("ctx", "wsh"), 0, 0, tiled=True)
    ends = staged(
        outputs,
        dict(
            tok=tok,
            grad=grad,
            gain=norm_gains,
            att=tail.att,
            gq=tail.gq,
            inner_out=tail.inner_out,
            gi=tail.gi,
            low=low,
            bias=bias,
            mlp_out=mlp.out,
            back=mlp.back,
        ),
        dict(block=shape((tok_dev, D)), tokens=shape((tok_dev, D), f32)),
        raws=dict(qkv=qkv_weight, out=out_weight, o=o_parts, w=halves(w_y, "w", tail.flat)),
        scratch=[pltpu.VMEM((D, 3 * D), bf16), pltpu.VMEM((D, D), bf16), pltpu.SemaphoreType.DMA((10,))],
        micros=0.1,
    )
    full = shape(adapters.shape, f32)
    new = staged(
        adamw,
        dict(adapters=adapters, first=first_moment, second=second_moment, parts=tie(shares, ends.block)),
        dict(grad=full, new=full, first=full, second=full, low=shape(adapters.shape)),
        scalars=dict(chosen=chosen),
        parts=dict(grad=ADAPTERS, new=ADAPTERS, first=ADAPTERS, second=ADAPTERS, low=ADAPTERS),
    )
    return (ends.block[None], ends.tokens[None], new.grad, new.new, new.first, new.second, new.low)


def solution(mesh):
    spread = P(None, None, ("ctx", "wsh"))
    rows = P("wsh", "ctx", None)
    half = P("wsh", None)
    in_specs = (rows, rows, P(), P(), half, half, half, half, P(), spread, spread, spread, half, P("wsh", None, None), half)
    out_specs = (rows, rows, spread, spread, spread, spread, spread)
    return jax.shard_map(on_device, mesh=mesh, in_specs=in_specs, out_specs=out_specs, check_vma=False)
```

```python
from types import SimpleNamespace

import jax
import jax.numpy as jnp
from jax import lax
from jax.experimental import pallas as pl
from jax.experimental.pallas import tpu as pltpu
from jax.sharding import PartitionSpec as P

D = 1024
HEADS = 16
FF = 4096
HEAD_DIM = 64
ROT = 16
ADAPTERS = 8
RANK = 16
STEP = 8
COLS = 8 * D + 2 * FF
CB = 512
NB = COLS // CB
WIDE = 512
W_CUT = 2560
HALF = FF // 2 // CB
TILE = 256

A_QKV, A_OUT, A_UP, A_DOWN = 0, 1, 2, 3
B_QKV, B_OUT, B_UP, B_DOWN = 7, 10, 11, 15

epsilon = 1e-05
adapter_scale = 8.0
rope_base = 10000.0
learn_rate = 0.02
beta_first = 0.5
beta_second = 0.5
weight_decay = 0.01
adam_epsilon = 1e-08
masked_value = -1e30

bf16 = jnp.bfloat16
f32 = jnp.float32

HBM = pl.BlockSpec(memory_space=pltpu.HBM)


def dot_nn(a, b):
    return jnp.dot(a, b, preferred_element_type=f32)


def dot_nt(a, b):
    return lax.dot_general(a, b, (((1,), (1,)), ((), ())), preferred_element_type=f32)


def dot_tn(a, b):
    return lax.dot_general(a, b, (((0,), (0,)), ((), ())), preferred_element_type=f32)


def shape(dims, dtype=bf16):
    return jax.ShapeDtypeStruct(tuple(dims), dtype)


def cut(index, width=D):
    return slice(index * width, (index + 1) * width)


class Stage:
    def __init__(self, loads, scalar, raw, out, targets):
        self.loads = loads
        self.scalar = scalar
        self.raw = raw
        self.out = out
        self.targets = targets
        self.waited = set()
        self.pending = []

    def __getattr__(self, name):
        buffer, copy = self.loads[name]
        if name not in self.waited:
            self.waited.add(name)
            copy.wait()
        return buffer

    def start(self, *ends):
        copy = pltpu.make_async_copy(*ends)
        copy.start()
        self.pending.append(copy)

    def store(self, buffer, at=None, into=None):
        target, sems = self.targets[id(buffer)]
        if into is not None:
            self.start(buffer, target.at[into], sems.at[0])
        elif at is None:
            self.start(buffer, target, sems.at[0])
        else:
            self.start(buffer.at[at], target.at[at], sems.at[at])


def staged(body, loads, results, raws=None, scalars=None, scratch=(), parts=None, micros=2, inside=None, alias=None):
    raws, scalars, parts, inside, alias = raws or {}, scalars or {}, parts or {}, inside or {}, alias or {}
    raw_list, raw_tree = jax.tree.flatten(raws)

    def kernel(*refs):
        refs = list(refs)

        def take(count):
            head = refs[:count]
            del refs[:count]
            return head

        scalar_from, load_from = take(len(scalars)), take(len(loads))
        raw = jax.tree.unflatten(raw_tree, take(len(raw_list)))
        targets = take(len(results))
        scalar_to, load_to, out = take(len(scalars)), take(len(loads)), take(len(results))
        (sems,) = take(1)
        out_sems = take(len(results))
        moves = [
            pltpu.make_async_copy(source, buffer, sems.at[i])
            for i, (source, buffer) in enumerate(zip(scalar_from + load_from, scalar_to + load_to))
        ]
        for move in moves:
            move.start()
        for move in moves[: len(scalars)]:
            move.wait()
        stage = Stage(
            dict(zip(loads, zip(load_to, moves[len(scalars) :]))),
            SimpleNamespace(**dict(zip(scalars, scalar_to))),
            SimpleNamespace(**raw),
            SimpleNamespace(**dict(zip(results, out))),
            {id(buffer): ends for buffer, ends in zip(out, zip(targets, out_sems))},
        )
        body(stage, *refs)
        for name in loads:
            getattr(stage, name)
        for copy in stage.pending:
            copy.wait()

    raw_names = list(raws)
    made = pl.pallas_call(
        kernel,
        out_shape=tuple(results.values()),
        in_specs=[HBM] * (len(scalars) + len(loads) + len(raw_list)),
        out_specs=(HBM,) * len(results),
        scratch_shapes=[pltpu.SMEM(a.shape, a.dtype) for a in scalars.values()]
        + [pltpu.VMEM(a.shape, a.dtype) for a in loads.values()]
        + [pltpu.VMEM(inside.get(n, s.shape), s.dtype) for n, s in results.items()]
        + [pltpu.SemaphoreType.DMA((len(loads) + len(scalars) + 1,))]
        + [pltpu.SemaphoreType.DMA((parts.get(n, 1),)) for n in results]
        + list(scratch),
        compiler_params=pltpu.CompilerParams(vmem_limit_bytes=64 * 1024 * 1024),
        input_output_aliases={
            len(scalars) + len(loads) + raw_names.index(a): list(results).index(b) for a, b in alias.items()
        },
        cost_estimate=pl.CostEstimate(flops=int(micros * 1.15e9), bytes_accessed=1024, transcendentals=0),
        name=body.__name__,
    )(*scalars.values(), *loads.values(), *raw_list)
    return SimpleNamespace(**dict(zip(results, made)))


def normalize(values):
    center = values - jnp.mean(values, axis=-1, keepdims=True)
    spread = jnp.mean(center * center, axis=-1, keepdims=True)
    scale = lax.rsqrt(spread + epsilon)
    return center * scale, scale


def give_adapters(stage):
    give = stage.out.give
    for a in range(ADAPTERS):
        give[cut(a, RANK), :] = stage.adapters[a].astype(bf16)
    row = lax.broadcasted_iota(jnp.int32, (RANK, give.shape[1]), 0)
    lane = lax.broadcasted_iota(jnp.int32, (RANK, give.shape[1]), 1)
    choice = jnp.zeros((RANK, give.shape[1]), f32)
    for j in range(stage.scalar.chosen.shape[1]):
        for a in range(ADAPTERS):
            choice = jnp.where((row == j) & (lane == a), stage.scalar.chosen[0, j, a].astype(f32), choice)
    give[ADAPTERS * RANK :, :] = choice.astype(bf16)
    stage.store(give)


def layer_norms(stage):
    out = stage.out
    normed, _ = normalize(stage.tok[...].astype(f32))
    gain, shift = stage.gain, stage.shift
    half = pl.multiple_of((1 - lax.axis_index("wsh")) * (D // 2), D // 2)
    for i, buffer in enumerate((out.attn, out.mlp)):
        buffer[...] = (normed * gain[i : i + 1, :] + shift[i : i + 1, :]).astype(bf16)
        out.give[:, cut(i, D // 2)] = buffer[:, pl.ds(half, D // 2)]
    stage.store(out.give)
    stage.store(out.attn)
    stage.store(out.mlp)


def tables(stage):
    order, starts, out = stage.scalar.order, stage.scalar.starts, stage.out
    rows, lanes = out.tab.shape[1:]
    ndoc = starts.shape[1]
    ctx = lax.axis_index("ctx")
    half = rows // 2

    def positions(dims, axis):
        index = lax.broadcasted_iota(jnp.int32, dims, axis)
        block = jnp.where(index < half, order[0, 2 * ctx], order[0, 2 * ctx + 1])
        return block * half + index % half

    pos = positions((rows, lanes), 0)
    start = jnp.zeros((rows, lanes), jnp.int32)
    for j in range(1, ndoc):
        start = jnp.where(pos >= starts[0, j], starts[0, j], start)
    lane = lax.broadcasted_iota(jnp.int32, (rows, lanes), 1) % HEAD_DIM
    frequency = jnp.ones((rows, lanes), f32)
    for i in range(1, ROT // 2):
        frequency = jnp.where(lane % (ROT // 2) == i, rope_base ** (-2.0 * i / ROT), frequency)
    angle = (pos - start).astype(f32) * frequency
    sine = jnp.sin(angle)
    out.tab[0] = jnp.where(lane < ROT, jnp.cos(angle), 1.0)
    out.tab[1] = jnp.where(lane < ROT // 2, -sine, 0.0)
    out.tab[2] = jnp.where((lane >= ROT // 2) & (lane < ROT), sine, 0.0)
    stage.store(out.tab)

    def used(dims, row_axis):
        pos = positions(dims, row_axis)
        doc = lax.broadcasted_iota(jnp.int32, dims, 1 - row_axis) // RANK
        held = jnp.zeros(dims, jnp.int32)
        for j in range(1, ndoc):
            held = jnp.where(pos >= starts[0, j], j, held)
        return (held == doc).astype(f32)

    out.mask[...] = used(out.mask.shape, 0)
    out.mask_t[...] = used(out.mask_t.shape, 1)
    stage.store(out.mask)
    stage.store(out.mask_t)


def choose_adapters(stage):
    adapters, given = stage.adapters, stage.given
    rows = stage.out.rows
    target, sems = stage.targets[id(rows)]
    columns = adapters.shape[2]
    wsh = lax.axis_index("wsh")
    for j in range(rows.shape[0] // RANK):
        index = 0
        for a in range(1, ADAPTERS):
            index = index + a * stage.scalar.chosen[0, j, a]
        start = pl.multiple_of(index * RANK, RANK)
        own_at = pl.multiple_of(wsh * columns, 128)
        other_at = pl.multiple_of((1 - wsh) * columns, 128)
        rows[cut(j, RANK), pl.ds(own_at, columns)] = adapters[index].astype(bf16)
        rows[cut(j, RANK), pl.ds(other_at, columns)] = given[pl.ds(start, RANK), :]
    for i in range(target.shape[0]):
        stage.start(rows, target.at[i], sems.at[i])


def part_orders(share):
    ctx = lax.axis_index("ctx")
    if share == 2:
        return ctx % 2, 1 - ctx % 2
    mine = ctx % 2 * 2 + ctx // 2 % 2
    return mine, mine ^ 1, mine ^ 2, mine ^ 3


def rows_at(first, count):
    return pl.ds(pl.multiple_of(first, count), count)


def own_part(weight, share):
    rows = weight.shape[0] // share
    return rows_at(part_orders(share)[0] * rows, rows)


def place_weights(own, chunks, target, sems, first):
    half = own.shape[0]
    own_half = lax.axis_index("wsh")
    copies = [pltpu.make_async_copy(own, target.at[rows_at(own_half * half, half), :], sems.at[first])]
    for column, source_column, width, parts in chunks:
        rows = half // len(parts)
        for order, part in zip(part_orders(len(parts)), parts):
            copies.append(
                pltpu.make_async_copy(
                    part.at[:, source_column : source_column + width],
                    target.at[rows_at((1 - own_half) * half + order * rows, rows), column : column + width],
                    sems.at[first + len(copies)],
                )
            )
    for copy in copies:
        copy.start()
    return copies


def turn(values, tab, sign):
    left = pltpu.roll(values, 120, 1)
    right = pltpu.roll(values, 8, 1)
    return values * tab[0] + sign * (left * tab[1] + right * tab[2])


def swap_halves(first, second):
    low = lax.broadcasted_iota(jnp.int32, first.shape, 1) < HEAD_DIM
    one = jnp.where(low, first, pltpu.roll(second, HEAD_DIM, 1))
    two = jnp.where(low, pltpu.roll(first, HEAD_DIM, 1), second)
    return one, two


def both_streams(stage, side=0):
    half = pl.multiple_of(lax.axis_index("wsh") * (D // 2), D // 2)
    return jnp.concatenate([stage.h[:, pl.ds(half, D // 2)], stage.given[:, cut(side, D // 2)]], axis=0)


def weight_columns(source, first, weights, sems):
    copies = []
    for n in range(weights.shape[0]):
        copies.append(
            pltpu.make_async_copy(source.at[:, first + n * WIDE : first + (n + 1) * WIDE], weights.at[n], sems.at[n])
        )
        copies[-1].start()
    return copies


def partial_qk(stage, weights, sems):
    copies = weight_columns(stage.raw.qkv, 0, weights, sems)
    both = both_streams(stage)
    rows = both.shape[0] // 2
    for n, copy in enumerate(copies):
        copy.wait()
        part = dot_nn(both, weights[n])
        stage.out.give[:, cut(n, WIDE)] = part[rows:].astype(bf16)
        stage.out.kept[n] = part[:rows]
    stage.store(stage.out.give)
    stage.store(stage.out.kept)


def partial_vg(stage, weights, out_rows, sems):
    copies = weight_columns(stage.raw.qkv, 2 * D, weights, sems)
    out_copy = pltpu.make_async_copy(stage.raw.out, out_rows, sems.at[len(copies)])
    out_copy.start()
    both = both_streams(stage)
    rows = both.shape[0] // 2
    for n, copy in enumerate(copies):
        copy.wait()
        part = dot_nn(both, weights[n])
        stage.out.give[:, cut(n, WIDE)] = part[rows:].astype(bf16)
        stage.out.kept[n] = part[:rows]
    grads = jnp.concatenate([stage.grad[...], stage.grad_given[...]], axis=0)
    out_copy.wait()
    part = dot_nt(grads, out_rows[...])
    stage.out.give[:, D:] = part[rows:].astype(bf16)
    stage.store(stage.out.give)
    stage.out.kept[D // WIDE] = part[:rows]
    stage.store(stage.out.kept)


def queries_keys(stage):
    low, mask, bias, tab, kept, given = stage.low, stage.mask[...], stage.bias, stage.tab, stage.kept, stage.given
    inner = (dot_nt(stage.h[...], low[A_QKV]) * mask).astype(bf16)
    stage.out.inner[...] = inner
    stage.store(stage.out.inner)
    grad_inner = (adapter_scale * dot_nt(stage.grad[...], low[B_OUT]) * mask).astype(bf16)
    stage.out.grad_inner[...] = grad_inner
    stage.store(stage.out.grad_inner)
    steps = D // WIDE
    for n in range(steps):
        sides = []
        for kind in range(2):
            at = cut(kind * steps + n, WIDE)
            part = kept[kind * steps + n] + given[:, at].astype(f32) + bias[:, at]
            sides.append(part + adapter_scale * dot_nn(inner, low[B_QKV + kind][:, cut(n, WIDE)]))
        for pair in range(WIDE // 128):
            query = turn(sides[0][:, cut(pair, 128)], tab, 1.0) * HEAD_DIM**-0.5
            key = turn(sides[1][:, cut(pair, 128)], tab, 1.0)
            head = n * WIDE // HEAD_DIM + 2 * pair
            for i, both in enumerate(swap_halves(query, key)):
                stage.out.send[head + i] = both.astype(bf16)
    stage.store(stage.out.send, into=(slice(None), 0))
    base, kept, wsh = stage.out.base, stage.kept_vg, lax.axis_index("wsh")
    for n in range(steps):
        base[n] = kept[n] + bias[:, 2 * D + n * WIDE : 2 * D + (n + 1) * WIDE]
        base[n] += adapter_scale * dot_nn(inner, low[B_QKV + 2][:, cut(n, WIDE)])
        base[steps + n] = jnp.where(wsh == n, kept[steps], 0.0) + dot_nn(grad_inner, low[A_OUT][:, cut(n, WIDE)])
    stage.store(base)


def values_grads(stage):
    base, given = stage.base, stage.given
    steps = D // WIDE
    wsh = lax.axis_index("wsh")
    for n in range(steps):
        value = base[n] + given[:, cut(n, WIDE)].astype(f32)
        grad = base[steps + n] + jnp.where(wsh == n, 0.0, given[:, D:].astype(f32))
        for pair in range(WIDE // 128):
            head = n * WIDE // HEAD_DIM + 2 * pair
            for i, both in enumerate(swap_halves(value[:, cut(pair, 128)], grad[:, cut(pair, 128)])):
                stage.out.send[head + i] = both.astype(bf16)
    stage.store(stage.out.send, into=(slice(None), 1))


def attention(stage, xt, dks, dvs, ks, vs, aq, s_scr, e_scr):
    order = stage.scalar.order
    rows = aq.shape[0]
    count = rows // TILE
    blocks = order.shape[1]
    half = rows // blocks
    hd = HEAD_DIM
    x = stage.arrived
    per = x.shape[2] // half
    for i in range(blocks):
        start = pl.multiple_of(order[0, i] * half, half)
        for side in range(2):
            aq[pl.ds(start, half), cut(side, 2 * hd)] = x[i // per, side, cut(i % per, half), :]
    for t in range(count):
        part = aq[cut(t, TILE), :]
        ks[cut(t, TILE), :] = part[:, hd : 2 * hd]
        vs[cut(t, TILE), :] = part[:, 2 * hd : 3 * hd]
        xt[:, cut(t, TILE)] = part.T
    dks[...] = jnp.zeros_like(dks)
    dvs[...] = jnp.zeros_like(dvs)
    key_row = lax.broadcasted_iota(jnp.int32, (TILE, TILE), 0)
    query_col = lax.broadcasted_iota(jnp.int32, (TILE, TILE), 1)
    seen = key_row <= query_col
    for b in range(count):
        at = cut(b, TILE)
        q_t = xt[0:hd, at]
        g_t = xt[3 * hd : 4 * hd, at]
        top = jnp.full((8, TILE), masked_value, f32)
        for t in range(b + 1):
            s = dot_nn(ks[cut(t, TILE), :], q_t)
            if t == b:
                s = jnp.where(seen, s, masked_value)
            s_scr[cut(t, TILE), :] = s
            top = jnp.maximum(top, jnp.max(s.reshape(TILE // 8, 8, TILE), axis=0))
        top = jnp.max(top, axis=0, keepdims=True)
        total = jnp.zeros((8, TILE), f32)
        att = jnp.zeros((hd, TILE), f32)
        for t in range(b + 1):
            e = jnp.exp(s_scr[cut(t, TILE), :] - top)
            total = total + jnp.sum(e.reshape(TILE // 8, 8, TILE), axis=0)
            e = e.astype(bf16)
            e_scr[cut(t, TILE), :] = e
            att = att + dot_nn(xt[2 * hd : 3 * hd, cut(t, TILE)], e)
        inverse = 1.0 / jnp.sum(total, axis=0, keepdims=True)
        att = att * inverse
        g_f = g_t.astype(f32)
        delta = jnp.sum(g_f * att, axis=0, keepdims=True) * inverse
        g_n = (g_f * inverse).astype(bf16)
        dq = jnp.zeros((hd, TILE), f32)
        for t in range(b + 1):
            e = e_scr[cut(t, TILE), :]
            dp = dot_nn(vs[cut(t, TILE), :], g_n)
            ds = (e.astype(f32) * (dp - delta)).astype(bf16)
            dq = dq + dot_nn(xt[hd : 2 * hd, cut(t, TILE)], ds)
            dks[cut(t, TILE), :] += dot_nt(ds, q_t)
            dvs[cut(t, TILE), :] += dot_nt(e, g_n)
        both = jnp.concatenate([att, dq * hd**-0.5], axis=0)
        aq[at, 0 : 2 * hd] = both.T.astype(bf16)
    for t in range(count):
        aq[cut(t, TILE), 2 * hd : 3 * hd] = dks[cut(t, TILE), :].astype(bf16)
        aq[cut(t, TILE), 3 * hd :] = dvs[cut(t, TILE), :].astype(bf16)
    for i in range(blocks):
        start = pl.multiple_of(order[0, i] * half, half)
        stage.out.back[cut(i, half), :] = aq[pl.ds(start, half), :]
    stage.store(stage.out.back)


def attention_one_document(order, arrived):
    rows = arrived.shape[0] * arrived.shape[2]
    hd = HEAD_DIM
    return staged(
        attention,
        dict(arrived=arrived),
        dict(back=shape((rows, 4 * hd))),
        scalars=dict(order=order),
        scratch=[
            pltpu.VMEM((4 * hd, rows), bf16),
            pltpu.VMEM((rows, hd), f32),
            pltpu.VMEM((rows, hd), f32),
            pltpu.VMEM((rows, hd), bf16),
            pltpu.VMEM((rows, hd), bf16),
            pltpu.VMEM((rows, 4 * hd), bf16),
            pltpu.VMEM((rows, TILE), f32),
            pltpu.VMEM((rows, TILE), bf16),
        ],
        micros=17,
    ).back


def attention_documents(arrived, pos, doc, groups, first_row):
    rows = arrived.shape[0] * arrived.shape[2]
    hd = HEAD_DIM
    qk, vg = (arrived[:, side].reshape(rows, 2 * hd) for side in range(2))
    q, k, v, g = qk[:, :hd], qk[:, hd:], vg[:, :hd], vg[:, hd:]
    if groups is not None:
        both = lax.all_gather(jnp.concatenate([k, v], 1), "ctx", axis=0, tiled=True, axis_index_groups=groups)
        k, v = both[:, :hd], both[:, hd:]
    step = 512
    my_pos = lax.dynamic_slice_in_dim(pos, first_row, rows)
    my_doc = lax.dynamic_slice_in_dim(doc, first_row, rows)

    def one(sums, item):
        q_b, g_b, pos_b, doc_b = item
        scores = dot_nt(q_b, k)
        allowed = (doc_b[:, None] == doc[None, :]) & (pos[None, :] <= pos_b[:, None])
        scores = jnp.where(allowed, scores, masked_value)
        top = jnp.max(scores, axis=1, keepdims=True)
        weights = jnp.exp(scores - top)
        weights = weights / jnp.sum(weights, axis=1, keepdims=True)
        weights_low = weights.astype(bf16)
        att = dot_nn(weights_low, v)
        delta = jnp.sum(g_b.astype(f32) * att, axis=1, keepdims=True)
        ds = (weights * (dot_nt(g_b, v) - delta)).astype(bf16)
        dq = dot_nn(ds, k) * hd**-0.5
        sums = (sums[0] + dot_tn(ds, q_b), sums[1] + dot_tn(weights_low, g_b))
        return sums, jnp.concatenate([att, dq], 1).astype(bf16)

    zero = jnp.zeros((k.shape[0], hd), f32)
    split = lambda a: a.reshape((rows // step, step) + a.shape[1:])
    sums, att_dq = lax.scan(one, (zero, zero), tuple(map(split, (q, g, my_pos, my_doc))))
    sums = jnp.concatenate(sums, 1)
    if groups is not None:
        sums = lax.psum_scatter(sums, "ctx", scatter_dimension=0, tiled=True, axis_index_groups=groups)
    return jnp.concatenate([att_dq.reshape(rows, 2 * hd), sums.astype(bf16)], axis=1)


def swapped(rows):
    half = rows.shape[0] // 2
    return jnp.concatenate([rows[half:], rows[:half]], axis=0)


def hidden_block(j):
    wsh = lax.axis_index("wsh")
    return (wsh if j < HALF else 1 - wsh) * HALF + j % HALF


def hidden_columns(j):
    return pl.ds(pl.multiple_of(hidden_block(j // HALF * HALF) * CB, HALF * CB), HALF * CB)


def up_blocks(source, weights, sems, order):
    copies = {}
    for j in order:
        first = pl.multiple_of(hidden_block(j) * CB, CB)
        copies[j] = pltpu.make_async_copy(source.at[:, pl.ds(first, CB)], weights.at[j], sems.at[j])
        copies[j].start()
    return copies


def adapter_block(low, first, j):
    return low[first + hidden_block(j) // 2, :, cut(j % 2, CB)]


def mlp_up(stage, weights, sems):
    out = stage.out
    order = [*range(HALF, 2 * HALF), *range(HALF)]
    copies = up_blocks(stage.raw.up, weights, sems, order)
    both = both_streams(stage, 1)
    for j in order:
        copies[j].wait()
        part = dot_nn(both, weights[j])
        if j < HALF:
            out.kept[j] = part
        elif j == HALF:
            out.early[...] = part.astype(bf16)
            stage.store(out.early)
        else:
            out.late[:, cut(j - HALF - 1, CB)] = part.astype(bf16)
            if j == 2 * HALF - 1:
                stage.store(out.late, into=pl.ds(0, part.shape[0]))
    stage.store(out.kept)


def share_at(kind, j, rank, rows):
    down, right = divmod(kind * HALF + j, HALF - 1)
    return pl.ds(rows + down * rank, rank), cut(right, CB)


def mlp_share(stage, sems):
    out = stage.out
    qkv, weight = stage.raw.qkv, stage.raw.out
    mine = own_part(qkv, 4)
    copies = [
        pltpu.make_async_copy(weight.at[mine, :], out.first.at[:, :D], sems.at[0]),
        pltpu.make_async_copy(qkv.at[mine, :W_CUT], out.first.at[:, D:], sems.at[1]),
        pltpu.make_async_copy(qkv.at[own_part(qkv, 2), W_CUT:], out.second, sems.at[2]),
        pltpu.make_async_copy(stage.raw.up.at[mine, hidden_columns(HALF)], out.up, sems.at[3]),
    ]
    for copy in copies:
        copy.start()
    share, low, mask = out.late, stage.low, stage.mask_t[...]
    rank, rows = mask.shape
    for j in range(HALF):
        share[share_at(0, j, rank, 0)] = adapter_block(low, A_DOWN, HALF + j)
        share[share_at(1, j, rank, 0)] = adapter_block(low, B_UP, HALF + j)
    inner = (dot_nt(low[A_UP], stage.h[...]) * mask).astype(bf16)
    back = (adapter_scale * dot_nt(low[B_DOWN], stage.grad[...]) * mask).astype(bf16)
    zero = jnp.zeros((rank, CB - 2 * rows), bf16)
    share[share_at(2, 0, rank, 0)] = jnp.concatenate([inner, back, zero], axis=1)
    stage.store(share, into=pl.ds(2 * rows, 3 * rank))
    out.products[...] = jnp.concatenate([inner, back], axis=1)
    stage.store(out.products)
    for copy in copies:
        copy.wait()
    for buffer in (out.up, out.first, out.second):
        stage.store(buffer)


def diagonal(one, two):
    zero = jnp.zeros_like(one)
    return jnp.concatenate([jnp.concatenate([one, zero], axis=1), jnp.concatenate([zero, two], axis=1)], axis=0)


def mlp_middle(stage, weights, sems):
    out, low = stage.out, stage.low
    copies = []
    for j in range(HALF):
        copies.append(pltpu.make_async_copy(stage.raw.down.at[cut(j, CB), :], weights.at[j], sems.at[j]))
        copies[-1].start()
    grads = jnp.concatenate([stage.grad[...], stage.grad_given[...]], axis=0)
    rows = grads.shape[0] // 2
    products, late = stage.products[...], stage.late
    rank = products.shape[0]
    other = late[share_at(2, 0, rank, 2 * rows)]
    inner, back = (diagonal(products[:, cut(i, rows)], other[:, cut(i, rows)]) for i in range(2))
    sums = None
    for j in range(HALF):
        at = cut(j, CB)
        a_both = jnp.concatenate([adapter_block(low, A_DOWN, j), late[share_at(0, j, rank, 2 * rows)]], axis=0)
        b_both = jnp.concatenate([adapter_block(low, B_UP, j), late[share_at(1, j, rank, 2 * rows)]], axis=0)
        part = stage.early[...] if j == 0 else late[: 2 * rows, cut(j - 1, CB)]
        shift = pl.multiple_of(4 * D + hidden_block(j) * CB, CB)
        up = stage.kept[j] + swapped(part.astype(f32)) + stage.bias[:, pl.ds(shift, CB)]
        up = up + adapter_scale * dot_tn(inner, b_both)
        spread = 0.5 * (1.0 + lax.erf(up * (0.5**0.5)))
        hidden = (up * spread).astype(bf16)
        slope = spread + up * (jnp.exp(-0.5 * up * up) * (0.5 / jnp.pi) ** 0.5)
        copies[j].wait()
        down = weights[j]
        grad_hidden = dot_nt(grads, down) + dot_tn(back, a_both)
        grad_up = (grad_hidden * slope).astype(bf16)
        out.grad_up[j] = grad_up
        stage.store(out.grad_up, j)
        parts = dot_nn(hidden, down), dot_nt(a_both, hidden), dot_nt(b_both, grad_up)
        sums = parts if sums is None else tuple(one + two for one, two in zip(sums, parts))
        a_grad = dot_nn(back, hidden).astype(bf16)
        b_grad = (adapter_scale * dot_nn(inner, grad_up)).astype(bf16)
        out.grads[j], out.grads[HALF + j] = a_grad[:rank], b_grad[:rank]
        out.pack[0:rank, at], out.pack[rank : 2 * rank, at] = a_grad[rank:], b_grad[rank:]
    down, inner_down, gi_up = sums
    out.down[...] = down[:rows]
    out.small[0], out.small[1] = inner_down[:rank, :rows], gi_up[:rank, :rows]
    out.pack[2 * rank : 3 * rank, :] = jnp.zeros((rank, 2 * D), bf16)
    out.pack[2 * rank : 3 * rank, 0:rows] = inner_down[rank:, rows:].astype(bf16)
    out.pack[2 * rank : 3 * rank, rows : 2 * rows] = gi_up[rank:, rows:].astype(bf16)
    out.rest[...] = down[rows:].astype(bf16)
    for buffer in (out.pack, out.small, out.grads, out.rest, out.down):
        stage.store(buffer)


def mlp_back(stage, weights, sems):
    copies = place_weights(stage.raw.up.at[:, hidden_columns(0)], [(0, 0, HALF * CB, stage.raw.u)], weights, sems, 0)
    for copy in copies:
        copy.wait()
    total = None
    for j in range(HALF):
        part = dot_nt(stage.grad_up[j], weights[:, cut(j, CB)])
        total = part if total is None else total + part
    rows = total.shape[0] // 2
    stage.out.give[...] = total[rows:].astype(bf16)
    stage.store(stage.out.give)
    stage.out.kept[...] = total[:rows]
    stage.store(stage.out.kept)


def mlp_finish(stage):
    out, low, mask = stage.out, stage.low, stage.mask_t[...]
    rank, rows = mask.shape
    pack, small, wsh = stage.pack, stage.small, lax.axis_index("wsh")
    extra = pack[2 * rank : 3 * rank, :].astype(f32)
    inner_down = ((small[0] + extra[:, 0:rows]) * mask).astype(bf16)
    gi_up = (adapter_scale * (small[1] + extra[:, rows : 2 * rows]) * mask).astype(bf16)
    for j in range(HALF):
        for kind in range(2):
            out.grads[2 + kind * 2 * HALF + wsh * HALF + j] = stage.grads[kind * HALF + j]
            other = pack[kind * rank : (kind + 1) * rank, cut(j, CB)]
            out.grads[2 + kind * 2 * HALF + (1 - wsh) * HALF + j] = other
    up_grad = dot_nn(gi_up, stage.h[...])
    down_grad = adapter_scale * dot_nn(inner_down, stage.grad[...])
    for i in range(2):
        out.grads[i] = up_grad[:, cut(i, CB)].astype(bf16)
        out.grads[18 + i] = down_grad[:, cut(i, CB)].astype(bf16)
    stage.store(out.grads)
    out.inner_down[...] = inner_down
    stage.store(out.inner_down)
    out.back[...] = stage.kept[...] + stage.given[...].astype(f32) + dot_tn(gi_up, low[A_UP])
    stage.store(out.back)


def adapter_gradients(stage):
    arrived, tab = stage.arrived, stage.tab
    att, gq, flat = stage.out.att, stage.out.gq, stage.out.flat
    for pair in range(HEADS // 2):
        at = cut(pair, 128)
        one, two = arrived[2 * pair].astype(f32), arrived[2 * pair + 1].astype(f32)
        attended, query = swap_halves(one[:, :128], two[:, :128])
        key, value = swap_halves(one[:, 128:], two[:, 128:])
        att[:, at] = attended.astype(bf16)
        for kind, part in enumerate((turn(query, tab, -1.0), turn(key, tab, -1.0), value)):
            gq[:, kind * D + pair * 128 : kind * D + (pair + 1) * 128] = part.astype(bf16)
    stage.store(att)
    stage.store(gq)
    low, mask, h, grad = stage.low, stage.mask[...], stage.h, stage.grad
    inner_out = (dot_nt(att[...], low[A_OUT]) * mask).astype(bf16)
    stage.out.inner_out[...] = inner_out
    stage.store(stage.out.inner_out)
    gi = sum(dot_nt(gq[:, cut(i)], low[B_QKV + i]) for i in range(3))
    gi = (adapter_scale * gi * mask).astype(bf16)
    stage.out.gi[...] = gi
    stage.store(stage.out.gi)
    per = D // CB

    def put(block, value):
        for i in range(per):
            flat[block * per + i] = value[:, cut(i, CB)].astype(bf16)

    put(A_QKV, dot_tn(gi, h[...]))
    put(A_OUT, dot_tn(stage.grad_inner[...], att[...]))
    put(B_OUT, adapter_scale * dot_tn(inner_out, grad[...]))
    for i in range(3):
        put(B_QKV + i, adapter_scale * dot_tn(stage.inner[...], gq[:, cut(i)]))
    flat[A_UP * per : A_UP * per + 10] = stage.mlp[0:10]
    flat[B_UP * per : B_UP * per + 10] = stage.mlp[10:20]
    stage.store(flat)


def outputs(stage, wq, wo, sems):
    raw = stage.raw
    o_copies = place_weights(raw.out, [(0, 0, D, raw.v)], wo, sems, 0)
    q_copies = place_weights(raw.qkv, [(0, D, W_CUT, raw.v), (W_CUT, 0, 3 * D - W_CUT, raw.w)], wq, sems, 5)
    tok, grad, low, gain, bias = stage.tok, stage.grad, stage.low, stage.gain, stage.bias
    att, inner_out, inner_down, back = stage.att[...], stage.inner_out[...], stage.inner_down[...], stage.back
    block = stage.out.block
    for copy in o_copies:
        copy.wait()
    for n in range(D // WIDE):
        at = cut(n, WIDE)
        shift = n * WIDE
        part = dot_nn(att, wo[:, at]) + bias[:, 3 * D + shift : 3 * D + shift + WIDE]
        part = part + adapter_scale * dot_nn(inner_out, low[B_OUT][:, at])
        mlp = stage.down[:, at] + stage.rest[:, at].astype(f32) + bias[:, 4 * D + FF + shift : 4 * D + FF + shift + WIDE]
        mlp = mlp + adapter_scale * dot_tn(inner_down, low[B_DOWN][:, at])
        block[:, at] = (part + tok[:, at].astype(f32) + mlp).astype(bf16)
    stage.store(block)
    normed, scale = normalize(tok[...].astype(f32))
    for copy in q_copies:
        copy.wait()
    grad_h = dot_nt(stage.gq[...], wq[...]) + dot_nn(stage.gi[...], low[A_QKV])
    grad_n = grad_h * gain[0:1, :] + back[...] * gain[1:2, :]
    grad_v = grad_n - jnp.mean(grad_n, axis=-1, keepdims=True) - normed * jnp.mean(grad_n * normed, axis=-1, keepdims=True)
    stage.out.tokens[...] = grad[...].astype(f32) + scale * grad_v
    stage.store(stage.out.tokens)


def adamw(stage):
    chosen, parts, out = stage.scalar.chosen, stage.parts, stage.out
    given, wsh = stage.given, lax.axis_index("wsh")
    sums = []
    for stream in range(2):
        total = parts[stream].astype(f32)
        for source in range(stream + 2, parts.shape[0], 2):
            total = total + parts[source].astype(f32)
        sums.append(total)
    ndoc = sums[0].shape[0] // RANK
    for a in range(ADAPTERS):
        grad = None
        for stream in range(2):
            for j in range(ndoc):
                own = chosen[0, j, a].astype(f32)
                other = given[ADAPTERS * RANK + j : ADAPTERS * RANK + j + 1, a : a + 1].astype(f32)
                term = jnp.where(wsh == stream, own, other) * sums[stream][cut(j, RANK), :]
                grad = term if grad is None else grad + term
        new_first = beta_first * stage.first[a] + (1.0 - beta_first) * grad
        new_second = beta_second * stage.second[a] + (1.0 - beta_second) * grad * grad
        first_hat = new_first / (1.0 - beta_first**STEP)
        second_hat = new_second / (1.0 - beta_second**STEP)
        old = stage.adapters[a]
        new = old - learn_rate * (first_hat / (jnp.sqrt(second_hat) + adam_epsilon) + weight_decay * old)
        for buffer, value in (
            (out.grad, grad),
            (out.new, new),
            (out.first, new_first),
            (out.second, new_second),
            (out.low, new.astype(bf16)),
        ):
            buffer[a] = value
            stage.store(buffer, a)


def stream_layout(order_row, starts_row, rows, total_rows, half_dev):
    slot = rows // half_dev
    picked = (slot[:, None] == jnp.arange(order_row.shape[0], dtype=jnp.int32)[None, :]).astype(jnp.int32)
    pos = jnp.sum(picked * order_row[None, :], axis=1) * half_dev + rows % half_dev
    finish = jnp.concatenate([starts_row[1:], jnp.full((1,), total_rows, jnp.int32)])
    inside = ((pos[:, None] >= starts_row[None, :]) & (pos[:, None] < finish[None, :])).astype(jnp.int32)
    doc = jnp.sum(inside * jnp.arange(starts_row.shape[0], dtype=jnp.int32)[None, :], axis=1)
    place = pos - jnp.sum(inside * starts_row[None, :], axis=1)
    return pos, doc, place, inside


def tie(first, *others):
    return lax.optimization_barrier((first,) + others)[0]


def on_device(
    tokens,
    out_cotangent,
    norm_gains,
    norm_biases,
    qkv_weight,
    out_weight,
    up_weight,
    down_weight,
    proj_biases,
    adapters,
    first_moment,
    second_moment,
    doc_starts,
    doc_adapter,
    block_order,
):
    n_ctx = lax.axis_size("ctx")
    n_dev = n_ctx * lax.axis_size("wsh")
    ctx = lax.axis_index("ctx")
    wsh = lax.axis_index("wsh")
    tok_dev = tokens.shape[1]
    half_dev = tok_dev // 2
    total_rows = tok_dev * n_ctx
    ndoc = doc_starts.shape[1]
    rank = ndoc * RANK
    columns = adapters.shape[2]
    tok, grad = tokens[0], out_cotangent[0]
    bias = proj_biases[None, :]

    def to_y(a, name):
        with jax.named_scope("y_" + name):
            return lax.ppermute(a, "wsh", [(0, 1), (1, 0)])

    def to_x(a, name):
        with jax.named_scope("x_" + name):
            return lax.ppermute(a, "ctx", [(i, i ^ 2) for i in range(n_ctx)])

    def to_core(a, name):
        with jax.named_scope("c_" + name):
            return lax.ppermute(a, "ctx", [(i, i ^ 1) for i in range(n_ctx)])

    give = staged(
        give_adapters,
        dict(adapters=adapters),
        dict(give=shape(((ADAPTERS + 1) * RANK, columns))),
        scalars=dict(chosen=doc_adapter),
    ).give
    adapters_given = to_y(give, "adapters")
    normed = staged(
        layer_norms,
        dict(tok=tie(tok, give), gain=norm_gains, shift=norm_biases),
        dict(attn=shape(tok.shape), mlp=shape(tok.shape), give=shape((tok_dev, D))),
    )
    h_attn, h_mlp = normed.attn, normed.mlp
    given = to_y(normed.give, "h")
    grad_given = to_y(tie(grad, normed.give), "grad")
    chosen_rows = staged(
        choose_adapters,
        dict(adapters=adapters, given=tie(adapters_given, h_attn)),
        dict(rows=shape((n_ctx, rank, 2 * columns))),
        scalars=dict(chosen=doc_adapter),
        parts=dict(rows=n_ctx),
        inside=dict(rows=(rank, 2 * columns)),
    ).rows
    low = lax.all_to_all(chosen_rows, "ctx", 0, 0, tiled=True)
    if n_ctx != HEADS:
        low = low.reshape(COLS // D, n_ctx // HEADS, rank, 2 * columns).transpose(0, 2, 1, 3).reshape(COLS // D, rank, D)

    both = staged(
        partial_qk,
        dict(h=h_attn, given=tie(given, chosen_rows)),
        dict(give=shape((tok_dev, 2 * D)), kept=shape((2 * D // WIDE, tok_dev, WIDE), f32)),
        raws=dict(qkv=qkv_weight),
        scratch=[pltpu.VMEM((2 * D // WIDE, D // 2, WIDE), bf16), pltpu.SemaphoreType.DMA((2 * D // WIDE,))],
        micros=3,
    )
    kept_qk, give_qk = both.kept, both.give
    given_qk = to_y(give_qk, "qk")
    both = staged(
        partial_vg,
        dict(h=tie(h_attn, give_qk), given=given, grad=grad, grad_given=grad_given),
        dict(give=shape((tok_dev, 3 * D // 2)), kept=shape((D // WIDE + 1, tok_dev, WIDE), f32)),
        raws=dict(qkv=qkv_weight, out=out_weight),
        scratch=[
            pltpu.VMEM((D // WIDE, D // 2, WIDE), bf16),
            pltpu.VMEM((D // 2, D), bf16),
            pltpu.SemaphoreType.DMA((D // WIDE + 1,)),
        ],
        micros=3,
    )
    given_vg = to_y(both.give, "vg")
    table = staged(
        tables,
        {},
        dict(tab=shape((3, tok_dev, 128), f32), mask=shape((tok_dev, rank), f32), mask_t=shape((rank, tok_dev), f32)),
        scalars=dict(order=tie(block_order, both.give), starts=doc_starts),
        micros=0.1,
    )
    tab, mask, mask_t = table.tab, table.mask, table.mask_t
    up = staged(
        mlp_up,
        dict(h=tie(h_mlp, both.give), given=given),
        dict(
            early=shape((2 * tok_dev, CB)),
            late=shape((2 * tok_dev + 3 * rank, (HALF - 1) * CB)),
            kept=shape((HALF, 2 * tok_dev, CB), f32),
        ),
        raws=dict(up=up_weight),
        inside=dict(late=(2 * tok_dev, (HALF - 1) * CB)),
        scratch=[pltpu.VMEM((2 * HALF, D // 2, CB), bf16), pltpu.SemaphoreType.DMA((2 * HALF,))],
        micros=0.1,
    )
    early_given = to_y(up.early, "early")
    heads = shape((HEADS, 2, tok_dev, 2 * HEAD_DIM))
    one = (HEADS, tok_dev, 2 * HEAD_DIM)
    made = staged(
        queries_keys,
        dict(
            h=tie(h_attn, up.early),
            grad=grad,
            low=low,
            mask=mask,
            bias=bias,
            tab=tab,
            kept=kept_qk,
            given=given_qk,
            kept_vg=both.kept,
        ),
        dict(
            inner=shape((tok_dev, rank)),
            grad_inner=shape((tok_dev, rank)),
            send=heads,
            base=shape((2 * D // WIDE, tok_dev, WIDE), f32),
        ),
        inside=dict(send=one),
        micros=0.1,
    )
    inner_qkv, grad_inner_out = made.inner, made.grad_inner
    made = staged(
        values_grads,
        dict(base=made.base, given=given_vg),
        dict(send=heads),
        raws=dict(send=made.send),
        inside=dict(send=one),
        alias=dict(send="send"),
        micros=3,
    )
    parts = n_ctx // HEADS
    near = None if parts == 1 else [[g * HEADS + i for i in range(HEADS)] for g in range(parts)]

    def exchange(a):
        return lax.all_to_all(a, "ctx", 0, 0, tiled=True, axis_index_groups=near)

    shared = staged(
        mlp_share,
        dict(h=h_mlp, grad=grad, low=low, mask_t=mask_t),
        dict(
            late=shape(up.late.shape),
            products=shape((rank, 2 * tok_dev)),
            first=shape((D // 8, D + W_CUT)),
            second=shape((D // 4, 3 * D - W_CUT)),
            up=shape((D // 8, HALF * CB)),
        ),
        raws=dict(late=up.late, qkv=qkv_weight, out=out_weight, up=up_weight),
        inside=dict(late=(3 * rank, (HALF - 1) * CB)),
        alias=dict(late="late"),
        scratch=[pltpu.SemaphoreType.DMA((4,))],
    )
    late_given = to_y(shared.late, "late")
    middle = staged(
        mlp_middle,
        dict(
            kept=up.kept,
            early=early_given,
            late=late_given,
            grad=grad,
            grad_given=grad_given,
            low=low,
            bias=bias,
            products=shared.products,
        ),
        dict(
            grad_up=shape((HALF, 2 * tok_dev, CB)),
            down=shape((tok_dev, D), f32),
            small=shape((2, rank, tok_dev), f32),
            grads=shape((2 * HALF, rank, CB)),
            pack=shape((3 * rank, 2 * D)),
            rest=shape((tok_dev, D)),
        ),
        raws=dict(down=down_weight),
        scratch=[pltpu.VMEM((HALF, CB, D), bf16), pltpu.SemaphoreType.DMA((HALF,))],
        parts=dict(grad_up=HALF),
        micros=0.1,
    )
    def quarters(y, x, name, *after):
        return [y, x, to_core(tie(y, *after), name + "y"), to_core(tie(x, *after), name + "x")]

    u_y = to_y(tie(shared.up, late_given), "u")
    u_x = to_x(u_y, "u")
    v_y = to_y(tie(shared.first, middle.pack), "v")
    arrived = tie(exchange(tie(made.send, early_given, shared.products)), middle.pack, u_y)
    if parts == 1 and ndoc == 1:
        done = attention_one_document(block_order, arrived)
    else:
        all_pos, all_doc, _, _ = stream_layout(
            block_order[0], doc_starts[0], jnp.arange(total_rows, dtype=jnp.int32), total_rows, half_dev
        )
        far = None if parts == 1 else [[g * HEADS + i for g in range(parts)] for i in range(HEADS)]
        done = attention_documents(arrived, all_pos, all_doc, far, ctx // HEADS * HEADS * tok_dev)
    back = exchange(tie(done.reshape(HEADS, tok_dev, 4 * HEAD_DIM), v_y, u_x))
    v_x = to_x(tie(v_y, done), "v")
    pack_given = to_y(tie(middle.pack, done), "pack")
    last = staged(
        mlp_back,
        dict(grad_up=tie(middle.grad_up, pack_given)),
        dict(give=shape((tok_dev, D)), kept=shape((tok_dev, D), f32)),
        raws=dict(up=up_weight, u=quarters(u_y, u_x, "u", done)),
        scratch=[pltpu.VMEM((D, HALF * CB), bf16), pltpu.SemaphoreType.DMA((5,))],
        micros=0.1,
    )
    back_given = to_y(last.give, "back")
    w_y = to_y(tie(shared.second, last.give), "w")
    rest_given = to_y(tie(middle.rest, last.give), "rest")
    mlp = staged(
        mlp_finish,
        dict(
            small=middle.small,
            grads=middle.grads,
            pack=pack_given,
            kept=last.kept,
            given=back_given,
            h=h_mlp,
            grad=grad,
            low=low,
            mask_t=mask_t,
        ),
        dict(inner_down=shape((rank, tok_dev)), back=shape((tok_dev, D), f32), grads=shape((20, rank, CB))),
        micros=0.1,
    )
    tail = staged(
        adapter_gradients,
        dict(
            arrived=back,
            tab=tab,
            low=low,
            mask=mask,
            h=h_attn,
            grad=grad,
            inner=inner_qkv,
            grad_inner=grad_inner_out,
            mlp=mlp.grads,
        ),
        dict(
            att=shape((tok_dev, D)),
            gq=shape((tok_dev, 3 * D)),
            inner_out=shape((tok_dev, rank)),
            gi=shape((tok_dev, rank)),
            flat=shape((NB, rank, CB)),
        ),
        micros=0.1,
    )
    flat = tail.flat
    if columns != CB:
        flat = flat.reshape(NB, rank, CB // columns, columns).transpose(0, 2, 1, 3).reshape(n_dev, rank, columns)
    shares = lax.all_to_all(tie(flat, w_y, rest_given), ("ctx", "wsh"), 0, 0, tiled=True)
    ends = staged(
        outputs,
        dict(
            tok=tok,
            grad=grad,
            gain=norm_gains,
            att=tail.att,
            gq=tail.gq,
            inner_out=tail.inner_out,
            gi=tail.gi,
            low=low,
            bias=bias,
            down=middle.down,
            rest=rest_given,
            inner_down=mlp.inner_down,
            back=mlp.back,
        ),
        dict(block=shape((tok_dev, D)), tokens=shape((tok_dev, D), f32)),
        raws=dict(
            qkv=qkv_weight,
            out=out_weight,
            v=quarters(v_y, v_x, "v", done),
            w=[w_y, to_core(w_y, "w")],
        ),
        scratch=[pltpu.VMEM((D, 3 * D), bf16), pltpu.VMEM((D, D), bf16), pltpu.SemaphoreType.DMA((14,))],
        micros=0.1,
    )
    full = shape(adapters.shape, f32)
    new = staged(
        adamw,
        dict(adapters=adapters, first=first_moment, second=second_moment, parts=tie(shares, ends.block), given=adapters_given),
        dict(grad=full, new=full, first=full, second=full, low=shape(adapters.shape)),
        scalars=dict(chosen=doc_adapter),
        parts=dict(grad=ADAPTERS, new=ADAPTERS, first=ADAPTERS, second=ADAPTERS, low=ADAPTERS),
    )
    return (ends.block[None], ends.tokens[None], new.grad, new.new, new.first, new.second, new.low)


def solution(mesh):
    spread = P(None, None, ("ctx", "wsh"))
    rows = P("wsh", "ctx", None)
    half = P("wsh", None)
    in_specs = (rows, rows, P(), P(), half, half, half, half, P(), spread, spread, spread, half, P("wsh", None, None), half)
    out_specs = (rows, rows, spread, spread, spread, spread, spread)
    return jax.shard_map(on_device, mesh=mesh, in_specs=in_specs, out_specs=out_specs, check_vma=False)
```

```python
from types import SimpleNamespace

import jax
import jax.numpy as jnp
from jax import lax
from jax.experimental import pallas as pl
from jax.experimental.pallas import tpu as pltpu
from jax.sharding import PartitionSpec as P

D = 1024
HEADS = 16
FF = 4096
HEAD_DIM = 64
ROT = 16
ADAPTERS = 8
RANK = 16
STEP = 8
COLS = 8 * D + 2 * FF
CB = 512
NB = COLS // CB
WIDE = 512
W_CUT = 1536
HALF = FF // 2 // CB
TILE = 256

A_QKV, A_OUT, A_UP, A_DOWN = 0, 1, 2, 3
B_QKV, B_OUT, B_UP, B_DOWN = 7, 10, 11, 15

epsilon = 1e-05
adapter_scale = 8.0
rope_base = 10000.0
learn_rate = 0.02
beta_first = 0.5
beta_second = 0.5
weight_decay = 0.01
adam_epsilon = 1e-08
masked_value = -1e30

bf16 = jnp.bfloat16
f32 = jnp.float32

HBM = pl.BlockSpec(memory_space=pltpu.HBM)


def dot_nn(a, b):
    return jnp.dot(a, b, preferred_element_type=f32)


def dot_nt(a, b):
    return lax.dot_general(a, b, (((1,), (1,)), ((), ())), preferred_element_type=f32)


def dot_tn(a, b):
    return lax.dot_general(a, b, (((0,), (0,)), ((), ())), preferred_element_type=f32)


def shape(dims, dtype=bf16):
    return jax.ShapeDtypeStruct(tuple(dims), dtype)


def cut(index, width=D):
    return slice(index * width, (index + 1) * width)


class Stage:
    def __init__(self, loads, scalar, raw, out, targets):
        self.loads = loads
        self.scalar = scalar
        self.raw = raw
        self.out = out
        self.targets = targets
        self.waited = set()
        self.pending = []

    def __getattr__(self, name):
        buffer, copy = self.loads[name]
        if name not in self.waited:
            self.waited.add(name)
            copy.wait()
        return buffer

    def start(self, *ends):
        copy = pltpu.make_async_copy(*ends)
        copy.start()
        self.pending.append(copy)

    def store(self, buffer, at=None, into=None, sem=0):
        target, sems = self.targets[id(buffer)]
        if at is not None and into is None:
            into, sem = at, at
        source = buffer if at is None else buffer.at[at]
        self.start(source, target if into is None else target.at[into], sems.at[sem])


def staged(body, loads, results, raws=None, scalars=None, scratch=(), parts=None, micros=2, inside=None, alias=None):
    raws, scalars, parts, inside, alias = raws or {}, scalars or {}, parts or {}, inside or {}, alias or {}
    raw_list, raw_tree = jax.tree.flatten(raws)

    def kernel(*refs):
        refs = list(refs)

        def take(count):
            head = refs[:count]
            del refs[:count]
            return head

        scalar_from, load_from = take(len(scalars)), take(len(loads))
        raw = jax.tree.unflatten(raw_tree, take(len(raw_list)))
        targets = take(len(results))
        scalar_to, load_to, out = take(len(scalars)), take(len(loads)), take(len(results))
        (sems,) = take(1)
        out_sems = take(len(results))
        moves = [
            pltpu.make_async_copy(source, buffer, sems.at[i])
            for i, (source, buffer) in enumerate(zip(scalar_from + load_from, scalar_to + load_to))
        ]
        for move in moves:
            move.start()
        for move in moves[: len(scalars)]:
            move.wait()
        stage = Stage(
            dict(zip(loads, zip(load_to, moves[len(scalars) :]))),
            SimpleNamespace(**dict(zip(scalars, scalar_to))),
            SimpleNamespace(**raw),
            SimpleNamespace(**dict(zip(results, out))),
            {id(buffer): ends for buffer, ends in zip(out, zip(targets, out_sems))},
        )
        body(stage, *refs)
        for name in loads:
            getattr(stage, name)
        for copy in stage.pending:
            copy.wait()

    raw_names = list(raws)
    made = pl.pallas_call(
        kernel,
        out_shape=tuple(results.values()),
        in_specs=[HBM] * (len(scalars) + len(loads) + len(raw_list)),
        out_specs=(HBM,) * len(results),
        scratch_shapes=[pltpu.SMEM(a.shape, a.dtype) for a in scalars.values()]
        + [pltpu.VMEM(a.shape, a.dtype) for a in loads.values()]
        + [pltpu.VMEM(inside.get(n, s.shape), s.dtype) for n, s in results.items()]
        + [pltpu.SemaphoreType.DMA((len(loads) + len(scalars) + 1,))]
        + [pltpu.SemaphoreType.DMA((parts.get(n, 1),)) for n in results]
        + list(scratch),
        compiler_params=pltpu.CompilerParams(vmem_limit_bytes=64 * 1024 * 1024),
        input_output_aliases={
            len(scalars) + len(loads) + raw_names.index(a): list(results).index(b) for a, b in alias.items()
        },
        cost_estimate=pl.CostEstimate(flops=int(micros * 1.15e9), bytes_accessed=1024, transcendentals=0),
        name=body.__name__,
    )(*scalars.values(), *loads.values(), *raw_list)
    return SimpleNamespace(**dict(zip(results, made)))


def normalize(values):
    center = values - jnp.mean(values, axis=-1, keepdims=True)
    spread = jnp.mean(center * center, axis=-1, keepdims=True)
    scale = lax.rsqrt(spread + epsilon)
    return center * scale, scale


def give_adapters(stage):
    give = stage.out.give
    for a in range(ADAPTERS):
        give[cut(a, RANK), :] = stage.adapters[a].astype(bf16)
    row = lax.broadcasted_iota(jnp.int32, (RANK, give.shape[1]), 0)
    lane = lax.broadcasted_iota(jnp.int32, (RANK, give.shape[1]), 1)
    choice = jnp.zeros((RANK, give.shape[1]), f32)
    for j in range(stage.scalar.chosen.shape[1]):
        for a in range(ADAPTERS):
            choice = jnp.where((row == j) & (lane == a), stage.scalar.chosen[0, j, a].astype(f32), choice)
    give[ADAPTERS * RANK :, :] = choice.astype(bf16)
    stage.store(give)


def layer_norms(stage):
    out = stage.out
    normed, _ = normalize(stage.tok[...].astype(f32))
    gain, shift = stage.gain, stage.shift
    half = pl.multiple_of((1 - lax.axis_index("wsh")) * (D // 2), D // 2)
    for i, buffer in enumerate((out.attn, out.mlp)):
        buffer[...] = (normed * gain[i : i + 1, :] + shift[i : i + 1, :]).astype(bf16)
        out.give[:, cut(i, D // 2)] = buffer[:, pl.ds(half, D // 2)]
    stage.store(out.give)
    stage.store(out.attn)
    stage.store(out.mlp)


def tables(stage, sem):
    order, starts, out = stage.scalar.order, stage.scalar.starts, stage.out
    source = stage.raw.up
    copy = pltpu.make_async_copy(source.at[own_part(source, 4), hidden_columns(HALF)], out.up, sem)
    copy.start()
    rows, lanes = out.tab.shape[1:]
    ndoc = starts.shape[1]
    ctx = lax.axis_index("ctx")
    half = rows // 2

    def positions(dims, axis):
        index = lax.broadcasted_iota(jnp.int32, dims, axis)
        block = jnp.where(index < half, order[0, 2 * ctx], order[0, 2 * ctx + 1])
        return block * half + index % half

    pos = positions((rows, lanes), 0)
    start = jnp.zeros((rows, lanes), jnp.int32)
    for j in range(1, ndoc):
        start = jnp.where(pos >= starts[0, j], starts[0, j], start)
    lane = lax.broadcasted_iota(jnp.int32, (rows, lanes), 1) % HEAD_DIM
    frequency = jnp.ones((rows, lanes), f32)
    for i in range(1, ROT // 2):
        frequency = jnp.where(lane % (ROT // 2) == i, rope_base ** (-2.0 * i / ROT), frequency)
    angle = (pos - start).astype(f32) * frequency
    sine = jnp.sin(angle)
    out.tab[0] = jnp.where(lane < ROT, jnp.cos(angle), 1.0)
    out.tab[1] = jnp.where(lane < ROT // 2, -sine, 0.0)
    out.tab[2] = jnp.where((lane >= ROT // 2) & (lane < ROT), sine, 0.0)
    stage.store(out.tab)

    def used(dims, row_axis):
        pos = positions(dims, row_axis)
        doc = lax.broadcasted_iota(jnp.int32, dims, 1 - row_axis) // RANK
        held = jnp.zeros(dims, jnp.int32)
        for j in range(1, ndoc):
            held = jnp.where(pos >= starts[0, j], j, held)
        return (held == doc).astype(f32)

    out.mask[...] = used(out.mask.shape, 0)
    out.mask_t[...] = used(out.mask_t.shape, 1)
    stage.store(out.mask)
    stage.store(out.mask_t)
    copy.wait()
    stage.store(out.up)


def choose_adapters(stage):
    adapters, given = stage.adapters, stage.given
    rows = stage.out.rows
    target, sems = stage.targets[id(rows)]
    columns = adapters.shape[2]
    wsh = lax.axis_index("wsh")
    for j in range(rows.shape[0] // RANK):
        index = 0
        for a in range(1, ADAPTERS):
            index = index + a * stage.scalar.chosen[0, j, a]
        start = pl.multiple_of(index * RANK, RANK)
        own_at = pl.multiple_of(wsh * columns, 128)
        other_at = pl.multiple_of((1 - wsh) * columns, 128)
        rows[cut(j, RANK), pl.ds(own_at, columns)] = adapters[index].astype(bf16)
        rows[cut(j, RANK), pl.ds(other_at, columns)] = given[pl.ds(start, RANK), :]
    for i in range(target.shape[0]):
        stage.start(rows, target.at[i], sems.at[i])


def part_orders(share):
    ctx = lax.axis_index("ctx")
    if share == 2:
        return ctx % 2, 1 - ctx % 2
    mine = ctx % 2 * 2 + ctx // 2 % 2
    return mine, mine ^ 1, mine ^ 2, mine ^ 3


def rows_at(first, count):
    return pl.ds(pl.multiple_of(first, count), count)


def own_part(weight, share):
    rows = weight.shape[0] // share
    return rows_at(part_orders(share)[0] * rows, rows)


def place_weights(own, chunks, target, sems, first=0):
    half = own.shape[0]
    own_half = lax.axis_index("wsh")
    copies = [pltpu.make_async_copy(own, target.at[rows_at(own_half * half, half), :], sems.at[first])]
    for column, source_column, width, parts in chunks:
        rows = half // len(parts)
        for order, part in zip(part_orders(len(parts)), parts):
            copies.append(
                pltpu.make_async_copy(
                    part.at[:, source_column : source_column + width],
                    target.at[rows_at((1 - own_half) * half + order * rows, rows), column : column + width],
                    sems.at[first + len(copies)],
                )
            )
    for copy in copies:
        copy.start()
    return copies


def turn(values, tab, sign):
    left = pltpu.roll(values, 120, 1)
    right = pltpu.roll(values, 8, 1)
    return values * tab[0] + sign * (left * tab[1] + right * tab[2])


def swap_halves(first, second):
    low = lax.broadcasted_iota(jnp.int32, first.shape, 1) < HEAD_DIM
    one = jnp.where(low, first, pltpu.roll(second, HEAD_DIM, 1))
    two = jnp.where(low, pltpu.roll(first, HEAD_DIM, 1), second)
    return one, two


def both_streams(stage, side=0):
    half = pl.multiple_of(lax.axis_index("wsh") * (D // 2), D // 2)
    return jnp.concatenate([stage.h[:, pl.ds(half, D // 2)], stage.given[:, cut(side, D // 2)]], axis=0)


def weight_columns(source, first, weights, sems):
    copies = []
    for n in range(weights.shape[0]):
        copies.append(
            pltpu.make_async_copy(source.at[:, first + n * WIDE : first + (n + 1) * WIDE], weights.at[n], sems.at[n])
        )
        copies[-1].start()
    return copies


def partial_qk(stage, weights, sems):
    copies = weight_columns(stage.raw.qkv, 0, weights, sems)
    both = both_streams(stage)
    rows = both.shape[0] // 2
    for n, copy in enumerate(copies):
        copy.wait()
        part = dot_nn(both, weights[n])
        stage.out.give[:, cut(n, WIDE)] = part[rows:].astype(bf16)
        stage.out.kept[n] = part[:rows]
    stage.store(stage.out.give)
    stage.store(stage.out.kept)


def partial_vg(stage, weights, out_rows, sems):
    copies = weight_columns(stage.raw.qkv, 2 * D, weights, sems)
    out_copy = pltpu.make_async_copy(stage.raw.out, out_rows, sems.at[len(copies)])
    out_copy.start()
    both = both_streams(stage)
    rows = both.shape[0] // 2
    for n, copy in enumerate(copies):
        copy.wait()
        part = dot_nn(both, weights[n])
        stage.out.give[:, cut(n, WIDE)] = part[rows:].astype(bf16)
        stage.out.kept[n] = part[:rows]
    grads = jnp.concatenate([stage.grad[...], stage.grad_given[...]], axis=0)
    out_copy.wait()
    part = dot_nt(grads, out_rows[...])
    stage.out.give[:, D:] = part[rows:].astype(bf16)
    stage.store(stage.out.give)
    stage.out.kept[D // WIDE] = part[:rows]
    stage.store(stage.out.kept)


def queries_keys(stage):
    low, mask, bias, tab, kept, given = stage.low, stage.mask[...], stage.bias, stage.tab, stage.kept, stage.given
    inner = (dot_nt(stage.h[...], low[A_QKV]) * mask).astype(bf16)
    stage.out.inner[...] = inner
    stage.store(stage.out.inner)
    grad_inner = (adapter_scale * dot_nt(stage.grad[...], low[B_OUT]) * mask).astype(bf16)
    stage.out.grad_inner[...] = grad_inner
    stage.store(stage.out.grad_inner)
    steps = D // WIDE
    for n in range(steps):
        sides = []
        for kind in range(2):
            at = cut(kind * steps + n, WIDE)
            part = kept[kind * steps + n] + given[:, at].astype(f32) + bias[:, at]
            sides.append(part + adapter_scale * dot_nn(inner, low[B_QKV + kind][:, cut(n, WIDE)]))
        for pair in range(WIDE // 128):
            query = turn(sides[0][:, cut(pair, 128)], tab, 1.0) * HEAD_DIM**-0.5
            key = turn(sides[1][:, cut(pair, 128)], tab, 1.0)
            head = n * WIDE // HEAD_DIM + 2 * pair
            for i, both in enumerate(swap_halves(query, key)):
                stage.out.send[head + i] = both.astype(bf16)
    stage.store(stage.out.send, into=(slice(None), 0))
    base, kept, wsh = stage.out.base, stage.kept_vg, lax.axis_index("wsh")
    for n in range(steps):
        base[n] = kept[n] + bias[:, 2 * D + n * WIDE : 2 * D + (n + 1) * WIDE]
        base[n] += adapter_scale * dot_nn(inner, low[B_QKV + 2][:, cut(n, WIDE)])
        base[steps + n] = jnp.where(wsh == n, kept[steps], 0.0) + dot_nn(grad_inner, low[A_OUT][:, cut(n, WIDE)])
    stage.store(base)


def values_grads(stage):
    base, given = stage.base, stage.given
    steps = D // WIDE
    wsh = lax.axis_index("wsh")
    for n in range(steps):
        value = base[n] + given[:, cut(n, WIDE)].astype(f32)
        grad = base[steps + n] + jnp.where(wsh == n, 0.0, given[:, D:].astype(f32))
        for pair in range(WIDE // 128):
            head = n * WIDE // HEAD_DIM + 2 * pair
            for i, both in enumerate(swap_halves(value[:, cut(pair, 128)], grad[:, cut(pair, 128)])):
                stage.out.send[head + i] = both.astype(bf16)
    stage.store(stage.out.send, into=(slice(None), 1))


def attention(stage, xt, dks, dvs, ks, vs, aq, s_scr, e_scr):
    order = stage.scalar.order
    rows = aq.shape[0]
    count = rows // TILE
    blocks = order.shape[1]
    half = rows // blocks
    hd = HEAD_DIM
    x = stage.arrived
    per = x.shape[2] // half
    for i in range(blocks):
        start = pl.multiple_of(order[0, i] * half, half)
        for side in range(2):
            aq[pl.ds(start, half), cut(side, 2 * hd)] = x[i // per, side, cut(i % per, half), :]
    for t in range(count):
        part = aq[cut(t, TILE), :]
        ks[cut(t, TILE), :] = part[:, hd : 2 * hd]
        vs[cut(t, TILE), :] = part[:, 2 * hd : 3 * hd]
        xt[:, cut(t, TILE)] = part.T
    dks[...] = jnp.zeros_like(dks)
    dvs[...] = jnp.zeros_like(dvs)
    key_row = lax.broadcasted_iota(jnp.int32, (TILE, TILE), 0)
    query_col = lax.broadcasted_iota(jnp.int32, (TILE, TILE), 1)
    seen = key_row <= query_col
    for b in range(count):
        at = cut(b, TILE)
        q_t = xt[0:hd, at]
        g_t = xt[3 * hd : 4 * hd, at]
        top = jnp.full((8, TILE), masked_value, f32)
        for t in range(b + 1):
            s = dot_nn(ks[cut(t, TILE), :], q_t)
            if t == b:
                s = jnp.where(seen, s, masked_value)
            s_scr[cut(t, TILE), :] = s
            top = jnp.maximum(top, jnp.max(s.reshape(TILE // 8, 8, TILE), axis=0))
        top = jnp.max(top, axis=0, keepdims=True)
        total = jnp.zeros((8, TILE), f32)
        att = jnp.zeros((hd, TILE), f32)
        for t in range(b + 1):
            e = jnp.exp(s_scr[cut(t, TILE), :] - top)
            total = total + jnp.sum(e.reshape(TILE // 8, 8, TILE), axis=0)
            e = e.astype(bf16)
            e_scr[cut(t, TILE), :] = e
            att = att + dot_nn(xt[2 * hd : 3 * hd, cut(t, TILE)], e)
        inverse = 1.0 / jnp.sum(total, axis=0, keepdims=True)
        att = att * inverse
        g_f = g_t.astype(f32)
        delta = jnp.sum(g_f * att, axis=0, keepdims=True) * inverse
        g_n = (g_f * inverse).astype(bf16)
        dq = jnp.zeros((hd, TILE), f32)
        for t in range(b + 1):
            e = e_scr[cut(t, TILE), :]
            dp = dot_nn(vs[cut(t, TILE), :], g_n)
            ds = (e.astype(f32) * (dp - delta)).astype(bf16)
            dq = dq + dot_nn(xt[hd : 2 * hd, cut(t, TILE)], ds)
            dks[cut(t, TILE), :] += dot_nt(ds, q_t)
            dvs[cut(t, TILE), :] += dot_nt(e, g_n)
        both = jnp.concatenate([att, dq * hd**-0.5], axis=0)
        aq[at, 0 : 2 * hd] = both.T.astype(bf16)
    for t in range(count):
        aq[cut(t, TILE), 2 * hd : 3 * hd] = dks[cut(t, TILE), :].astype(bf16)
        aq[cut(t, TILE), 3 * hd :] = dvs[cut(t, TILE), :].astype(bf16)
    for i in range(blocks):
        start = pl.multiple_of(order[0, i] * half, half)
        stage.out.back[cut(i, half), :] = aq[pl.ds(start, half), :]
    stage.store(stage.out.back)


def attention_one_document(order, arrived):
    rows = arrived.shape[0] * arrived.shape[2]
    hd = HEAD_DIM
    return staged(
        attention,
        dict(arrived=arrived),
        dict(back=shape((rows, 4 * hd))),
        scalars=dict(order=order),
        scratch=[
            pltpu.VMEM((4 * hd, rows), bf16),
            pltpu.VMEM((rows, hd), f32),
            pltpu.VMEM((rows, hd), f32),
            pltpu.VMEM((rows, hd), bf16),
            pltpu.VMEM((rows, hd), bf16),
            pltpu.VMEM((rows, 4 * hd), bf16),
            pltpu.VMEM((rows, TILE), f32),
            pltpu.VMEM((rows, TILE), bf16),
        ],
        micros=17,
    ).back


def attention_documents(arrived, pos, doc, groups, first_row):
    rows = arrived.shape[0] * arrived.shape[2]
    hd = HEAD_DIM
    qk, vg = (arrived[:, side].reshape(rows, 2 * hd) for side in range(2))
    q, k, v, g = qk[:, :hd], qk[:, hd:], vg[:, :hd], vg[:, hd:]
    if groups is not None:
        both = lax.all_gather(jnp.concatenate([k, v], 1), "ctx", axis=0, tiled=True, axis_index_groups=groups)
        k, v = both[:, :hd], both[:, hd:]
    step = 512
    my_pos = lax.dynamic_slice_in_dim(pos, first_row, rows)
    my_doc = lax.dynamic_slice_in_dim(doc, first_row, rows)

    def one(sums, item):
        q_b, g_b, pos_b, doc_b = item
        scores = dot_nt(q_b, k)
        allowed = (doc_b[:, None] == doc[None, :]) & (pos[None, :] <= pos_b[:, None])
        scores = jnp.where(allowed, scores, masked_value)
        top = jnp.max(scores, axis=1, keepdims=True)
        weights = jnp.exp(scores - top)
        weights = weights / jnp.sum(weights, axis=1, keepdims=True)
        weights_low = weights.astype(bf16)
        att = dot_nn(weights_low, v)
        delta = jnp.sum(g_b.astype(f32) * att, axis=1, keepdims=True)
        ds = (weights * (dot_nt(g_b, v) - delta)).astype(bf16)
        dq = dot_nn(ds, k) * hd**-0.5
        sums = (sums[0] + dot_tn(ds, q_b), sums[1] + dot_tn(weights_low, g_b))
        return sums, jnp.concatenate([att, dq], 1).astype(bf16)

    zero = jnp.zeros((k.shape[0], hd), f32)
    split = lambda a: a.reshape((rows // step, step) + a.shape[1:])
    sums, att_dq = lax.scan(one, (zero, zero), tuple(map(split, (q, g, my_pos, my_doc))))
    sums = jnp.concatenate(sums, 1)
    if groups is not None:
        sums = lax.psum_scatter(sums, "ctx", scatter_dimension=0, tiled=True, axis_index_groups=groups)
    return jnp.concatenate([att_dq.reshape(rows, 2 * hd), sums.astype(bf16)], axis=1)


def swapped(rows):
    half = rows.shape[0] // 2
    return jnp.concatenate([rows[half:], rows[:half]], axis=0)


def hidden_block(j):
    wsh = lax.axis_index("wsh")
    return (wsh if j < HALF else 1 - wsh) * HALF + j % HALF


def hidden_columns(j):
    return pl.ds(pl.multiple_of(hidden_block(j // HALF * HALF) * CB, HALF * CB), HALF * CB)


def up_blocks(source, weights, sems, order):
    copies = {}
    for j in order:
        first = pl.multiple_of(hidden_block(j) * CB, CB)
        copies[j] = pltpu.make_async_copy(source.at[:, pl.ds(first, CB)], weights.at[j], sems.at[j])
        copies[j].start()
    return copies


def adapter_block(low, first, j):
    return low[first + hidden_block(j) // 2, :, cut(j % 2, CB)]


def mlp_up(stage, weights, sems):
    out = stage.out
    order = [*range(HALF, 2 * HALF), *range(HALF)]
    copies = up_blocks(stage.raw.up, weights, sems, order)
    both = both_streams(stage, 1)
    for j in order:
        copies[j].wait()
        part = dot_nn(both, weights[j])
        if j < HALF:
            out.kept[j] = part
        elif j == HALF:
            out.early[...] = part.astype(bf16)
            stage.store(out.early)
        else:
            out.late[:, cut(j - HALF - 1, CB)] = part.astype(bf16)
            if j == 2 * HALF - 1:
                stage.store(out.late, into=pl.ds(0, part.shape[0]))
    stage.store(out.kept)


def share_at(kind, j, rank, rows):
    down, right = divmod(kind * HALF + j, HALF - 1)
    return pl.ds(rows + down * rank, rank), cut(right, CB)


def mlp_share(stage, sems):
    out = stage.out
    qkv, weight = stage.raw.qkv, stage.raw.out
    mine = own_part(qkv, 4)
    copies = [
        pltpu.make_async_copy(weight.at[mine, :], out.first.at[:, :D], sems.at[0]),
        pltpu.make_async_copy(qkv.at[mine, :W_CUT], out.first.at[:, D:], sems.at[1]),
        pltpu.make_async_copy(qkv.at[mine, W_CUT:], out.second, sems.at[2]),
    ]
    for copy in copies:
        copy.start()
    share, low, mask = out.late, stage.low, stage.mask_t[...]
    rank, rows = mask.shape
    for j in range(HALF):
        share[share_at(0, j, rank, 0)] = adapter_block(low, A_DOWN, HALF + j)
        share[share_at(1, j, rank, 0)] = adapter_block(low, B_UP, HALF + j)
    inner = (dot_nt(low[A_UP], stage.h[...]) * mask).astype(bf16)
    back = (adapter_scale * dot_nt(low[B_DOWN], stage.grad[...]) * mask).astype(bf16)
    zero = jnp.zeros((rank, CB - 2 * rows), bf16)
    share[share_at(2, 0, rank, 0)] = jnp.concatenate([inner, back, zero], axis=1)
    stage.store(share, into=pl.ds(2 * rows, 3 * rank))
    out.products[...] = jnp.concatenate([inner, back], axis=1)
    stage.store(out.products)
    for copy in copies:
        copy.wait()
    for buffer in (out.first, out.second):
        stage.store(buffer)


def diagonal(one, two):
    zero = jnp.zeros_like(one)
    return jnp.concatenate([jnp.concatenate([one, zero], axis=1), jnp.concatenate([zero, two], axis=1)], axis=0)


def mlp_middle(stage, down_rows, up_rows, down_sems, up_sems):
    out, low = stage.out, stage.low
    copies = []
    for j in range(HALF):
        copies.append(pltpu.make_async_copy(stage.raw.down.at[cut(j, CB), :], down_rows.at[j], down_sems.at[j]))
        copies[-1].start()
    up_copies = place_weights(
        stage.raw.up.at[:, hidden_columns(0)], [(0, 0, HALF * CB, stage.raw.u)], up_rows, up_sems, 0
    )
    grads = jnp.concatenate([stage.grad[...], stage.grad_given[...]], axis=0)
    rows = grads.shape[0] // 2
    products, late = stage.products[...], stage.late
    rank = products.shape[0]
    other = late[share_at(2, 0, rank, 2 * rows)]
    inner, back = (diagonal(products[:, cut(i, rows)], other[:, cut(i, rows)]) for i in range(2))
    sums = None
    grad_ups = []
    for j in range(HALF):
        at = cut(j, CB)
        a_both = jnp.concatenate([adapter_block(low, A_DOWN, j), late[share_at(0, j, rank, 2 * rows)]], axis=0)
        b_both = jnp.concatenate([adapter_block(low, B_UP, j), late[share_at(1, j, rank, 2 * rows)]], axis=0)
        part = stage.early[...] if j == 0 else late[: 2 * rows, cut(j - 1, CB)]
        shift = pl.multiple_of(4 * D + hidden_block(j) * CB, CB)
        up = stage.kept[j] + swapped(part.astype(f32)) + stage.bias[:, pl.ds(shift, CB)]
        up = up + adapter_scale * dot_tn(inner, b_both)
        spread = 0.5 * (1.0 + lax.erf(up * (0.5**0.5)))
        hidden = (up * spread).astype(bf16)
        slope = spread + up * (jnp.exp(-0.5 * up * up) * (0.5 / jnp.pi) ** 0.5)
        copies[j].wait()
        down = down_rows[j]
        grad_hidden = dot_nt(grads, down) + dot_tn(back, a_both)
        grad_up = (grad_hidden * slope).astype(bf16)
        grad_ups.append(grad_up)
        parts = dot_nn(hidden, down), dot_nt(a_both, hidden), dot_nt(b_both, grad_up)
        sums = parts if sums is None else tuple(one + two for one, two in zip(sums, parts))
        a_grad = dot_nn(back, hidden).astype(bf16)
        b_grad = (adapter_scale * dot_nn(inner, grad_up)).astype(bf16)
        out.grads[j], out.grads[HALF + j] = a_grad[:rank], b_grad[:rank]
        out.pack[pack_at(0, j, rank)], out.pack[pack_at(1, j, rank)] = a_grad[rank:], b_grad[rank:]
    down, inner_down, gi_up = sums
    out.small[0], out.small[1] = inner_down[:rank, :rows], gi_up[:rank, :rows]
    out.pack[4 * rank : 5 * rank, :] = jnp.zeros((rank, D), bf16)
    out.pack[4 * rank : 5 * rank, 0:rows] = inner_down[rank:, rows:].astype(bf16)
    out.pack[4 * rank : 5 * rank, rows : 2 * rows] = gi_up[rank:, rows:].astype(bf16)
    for copy in up_copies:
        copy.wait()
    total = None
    for j in range(HALF):
        part = dot_nt(grad_ups[j], up_rows[:, cut(j, CB)])
        total = part if total is None else total + part
    out.pack[5 * rank :, :] = total[rows:].astype(bf16)
    stage.store(out.pack)
    out.kept[...] = total[:rows]
    out.rest[...] = down[rows:].astype(bf16)
    out.down[...] = down[:rows]
    for buffer in (out.small, out.grads, out.kept, out.rest, out.down):
        stage.store(buffer)


def pack_at(kind, j, rank):
    return pl.ds((2 * kind + j // 2) * rank, rank), cut(j % 2, CB)


def mlp_finish(stage):
    out, low, mask = stage.out, stage.low, stage.mask_t[...]
    rank, rows = mask.shape
    pack, small, wsh = stage.pack, stage.small, lax.axis_index("wsh")
    extra = pack[4 * rank : 5 * rank, :].astype(f32)
    inner_down = ((small[0] + extra[:, 0:rows]) * mask).astype(bf16)
    gi_up = (adapter_scale * (small[1] + extra[:, rows : 2 * rows]) * mask).astype(bf16)
    for j in range(HALF):
        for kind in range(2):
            out.flat[2 + kind * 2 * HALF + wsh * HALF + j] = stage.grads[kind * HALF + j]
            out.flat[2 + kind * 2 * HALF + (1 - wsh) * HALF + j] = pack[pack_at(kind, j, rank)]
    up_grad = dot_nn(gi_up, stage.h[...])
    down_grad = adapter_scale * dot_nn(inner_down, stage.grad[...])
    for i in range(2):
        out.flat[i] = up_grad[:, cut(i, CB)].astype(bf16)
        out.flat[18 + i] = down_grad[:, cut(i, CB)].astype(bf16)
    per = D // CB
    stage.store(out.flat, at=pl.ds(0, 10), into=pl.ds(A_UP * per, 10), sem=0)
    stage.store(out.flat, at=pl.ds(10, 10), into=pl.ds(B_UP * per, 10), sem=1)
    out.inner_down[...] = inner_down
    stage.store(out.inner_down)
    out.back[...] = stage.kept[...] + pack[5 * rank :, :].astype(f32) + dot_tn(gi_up, low[A_UP])
    stage.store(out.back)


def adapter_gradients(stage):
    arrived, tab = stage.arrived, stage.tab
    att, gq, flat = stage.out.att, stage.out.gq, stage.out.flat
    for pair in range(HEADS // 2):
        at = cut(pair, 128)
        one, two = arrived[2 * pair].astype(f32), arrived[2 * pair + 1].astype(f32)
        attended, query = swap_halves(one[:, :128], two[:, :128])
        key, value = swap_halves(one[:, 128:], two[:, 128:])
        att[:, at] = attended.astype(bf16)
        for kind, part in enumerate((turn(query, tab, -1.0), turn(key, tab, -1.0), value)):
            gq[:, kind * D + pair * 128 : kind * D + (pair + 1) * 128] = part.astype(bf16)
    stage.store(att)
    stage.store(gq)
    low, mask, h, grad = stage.low, stage.mask[...], stage.h, stage.grad
    inner_out = (dot_nt(att[...], low[A_OUT]) * mask).astype(bf16)
    stage.out.inner_out[...] = inner_out
    stage.store(stage.out.inner_out)
    gi = sum(dot_nt(gq[:, cut(i)], low[B_QKV + i]) for i in range(3))
    gi = (adapter_scale * gi * mask).astype(bf16)
    stage.out.gi[...] = gi
    stage.store(stage.out.gi)
    per = D // CB

    def put(block, value):
        place = block if block < A_UP else block - B_QKV + A_UP
        for i in range(per):
            flat[place * per + i] = value[:, cut(i, CB)].astype(bf16)

    put(A_QKV, dot_tn(gi, h[...]))
    put(A_OUT, dot_tn(stage.grad_inner[...], att[...]))
    put(B_OUT, adapter_scale * dot_tn(inner_out, grad[...]))
    for i in range(3):
        put(B_QKV + i, adapter_scale * dot_tn(stage.inner[...], gq[:, cut(i)]))
    first, rest = A_UP * per, (B_UP - B_QKV) * per
    stage.store(flat, at=pl.ds(0, first), into=pl.ds(0, first), sem=0)
    stage.store(flat, at=pl.ds(first, rest), into=pl.ds(B_QKV * per, rest), sem=1)


def first_outputs(stage, wq, wo, sems):
    raw, low, bias = stage.raw, stage.low, stage.bias
    o_copies = place_weights(raw.out, [(0, 0, D, raw.v)], wo, sems)
    q_copies = place_weights(raw.qkv.at[:, :W_CUT], [(0, D, W_CUT, raw.v)], wq, sems, 5)
    att, inner_out, inner_down = stage.att[...], stage.inner_out[...], stage.inner_down[...]
    for copy in o_copies:
        copy.wait()
    for n in range(D // WIDE):
        at = cut(n, WIDE)
        shift = n * WIDE
        part = dot_nn(att, wo[:, at]) + bias[:, 3 * D + shift : 3 * D + shift + WIDE]
        part = part + adapter_scale * dot_nn(inner_out, low[B_OUT][:, at])
        mlp = stage.down[:, at] + bias[:, 4 * D + FF + shift : 4 * D + FF + shift + WIDE]
        mlp = mlp + adapter_scale * dot_tn(inner_down, low[B_DOWN][:, at])
        stage.out.block[:, at] = part + stage.tok[:, at].astype(f32) + mlp
    stage.store(stage.out.block)
    for copy in q_copies:
        copy.wait()
    stage.out.grad_h[...] = dot_nt(stage.gq[:, :W_CUT], wq[...]) + dot_nn(stage.gi[...], low[A_QKV])
    stage.store(stage.out.grad_h)


def last_outputs(stage, wq, sems):
    raw, gain, out = stage.raw, stage.gain, stage.out
    copies = place_weights(raw.qkv.at[:, W_CUT:], [(0, 0, 3 * D - W_CUT, raw.w)], wq, sems)
    normed, scale = normalize(stage.tok[...].astype(f32))
    out.block[...] = (stage.block[...] + stage.rest[...].astype(f32)).astype(bf16)
    stage.store(out.block)
    for copy in copies:
        copy.wait()
    grad_h = stage.grad_h[...] + dot_nt(stage.gq[:, W_CUT:], wq[...])
    grad_n = grad_h * gain[0:1, :] + stage.back[...] * gain[1:2, :]
    grad_v = grad_n - jnp.mean(grad_n, axis=-1, keepdims=True) - normed * jnp.mean(grad_n * normed, axis=-1, keepdims=True)
    out.tokens[...] = stage.grad[...].astype(f32) + scale * grad_v
    stage.store(out.tokens)


def adamw(stage):
    chosen, parts, out = stage.scalar.chosen, stage.parts, stage.out
    given, wsh = stage.given, lax.axis_index("wsh")
    sums = []
    for stream in range(2):
        total = parts[stream].astype(f32)
        for source in range(stream + 2, parts.shape[0], 2):
            total = total + parts[source].astype(f32)
        sums.append(total)
    ndoc = sums[0].shape[0] // RANK
    for a in range(ADAPTERS):
        grad = None
        for stream in range(2):
            for j in range(ndoc):
                own = chosen[0, j, a].astype(f32)
                other = given[ADAPTERS * RANK + j : ADAPTERS * RANK + j + 1, a : a + 1].astype(f32)
                term = jnp.where(wsh == stream, own, other) * sums[stream][cut(j, RANK), :]
                grad = term if grad is None else grad + term
        new_first = beta_first * stage.first[a] + (1.0 - beta_first) * grad
        new_second = beta_second * stage.second[a] + (1.0 - beta_second) * grad * grad
        first_hat = new_first / (1.0 - beta_first**STEP)
        second_hat = new_second / (1.0 - beta_second**STEP)
        old = stage.adapters[a]
        new = old - learn_rate * (first_hat / (jnp.sqrt(second_hat) + adam_epsilon) + weight_decay * old)
        for buffer, value in (
            (out.grad, grad),
            (out.new, new),
            (out.first, new_first),
            (out.second, new_second),
            (out.low, new.astype(bf16)),
        ):
            buffer[a] = value
            stage.store(buffer, a)


def stream_layout(order_row, starts_row, rows, total_rows, half_dev):
    slot = rows // half_dev
    picked = (slot[:, None] == jnp.arange(order_row.shape[0], dtype=jnp.int32)[None, :]).astype(jnp.int32)
    pos = jnp.sum(picked * order_row[None, :], axis=1) * half_dev + rows % half_dev
    finish = jnp.concatenate([starts_row[1:], jnp.full((1,), total_rows, jnp.int32)])
    inside = ((pos[:, None] >= starts_row[None, :]) & (pos[:, None] < finish[None, :])).astype(jnp.int32)
    doc = jnp.sum(inside * jnp.arange(starts_row.shape[0], dtype=jnp.int32)[None, :], axis=1)
    place = pos - jnp.sum(inside * starts_row[None, :], axis=1)
    return pos, doc, place, inside


def tie(first, *others):
    return lax.optimization_barrier((first,) + others)[0]


def on_device(
    tokens,
    out_cotangent,
    norm_gains,
    norm_biases,
    qkv_weight,
    out_weight,
    up_weight,
    down_weight,
    proj_biases,
    adapters,
    first_moment,
    second_moment,
    doc_starts,
    doc_adapter,
    block_order,
):
    n_ctx = lax.axis_size("ctx")
    n_dev = n_ctx * lax.axis_size("wsh")
    ctx = lax.axis_index("ctx")
    wsh = lax.axis_index("wsh")
    tok_dev = tokens.shape[1]
    half_dev = tok_dev // 2
    total_rows = tok_dev * n_ctx
    ndoc = doc_starts.shape[1]
    rank = ndoc * RANK
    columns = adapters.shape[2]
    tok, grad = tokens[0], out_cotangent[0]
    bias = proj_biases[None, :]

    def to_y(a, name):
        with jax.named_scope("y_" + name):
            return lax.ppermute(a, "wsh", [(0, 1), (1, 0)])

    def to_x(a, name):
        with jax.named_scope("x_" + name):
            return lax.ppermute(a, "ctx", [(i, i ^ 2) for i in range(n_ctx)])

    def to_core(a, name):
        with jax.named_scope("c_" + name):
            return lax.ppermute(a, "ctx", [(i, i ^ 1) for i in range(n_ctx)])

    give = staged(
        give_adapters,
        dict(adapters=adapters),
        dict(give=shape(((ADAPTERS + 1) * RANK, columns))),
        scalars=dict(chosen=doc_adapter),
    ).give
    adapters_given = to_y(give, "adapters")
    normed = staged(
        layer_norms,
        dict(tok=tie(tok, give), gain=norm_gains, shift=norm_biases),
        dict(attn=shape(tok.shape), mlp=shape(tok.shape), give=shape((tok_dev, D))),
    )
    h_attn, h_mlp = normed.attn, normed.mlp
    given = to_y(normed.give, "h")
    grad_given = to_y(tie(grad, normed.give), "grad")
    chosen_rows = staged(
        choose_adapters,
        dict(adapters=adapters, given=tie(adapters_given, h_attn)),
        dict(rows=shape((n_ctx, rank, 2 * columns))),
        scalars=dict(chosen=doc_adapter),
        parts=dict(rows=n_ctx),
        inside=dict(rows=(rank, 2 * columns)),
    ).rows
    low = lax.all_to_all(chosen_rows, "ctx", 0, 0, tiled=True)
    if n_ctx != HEADS:
        low = low.reshape(COLS // D, n_ctx // HEADS, rank, 2 * columns).transpose(0, 2, 1, 3).reshape(COLS // D, rank, D)

    both = staged(
        partial_qk,
        dict(h=h_attn, given=tie(given, chosen_rows)),
        dict(give=shape((tok_dev, 2 * D)), kept=shape((2 * D // WIDE, tok_dev, WIDE), f32)),
        raws=dict(qkv=qkv_weight),
        scratch=[pltpu.VMEM((2 * D // WIDE, D // 2, WIDE), bf16), pltpu.SemaphoreType.DMA((2 * D // WIDE,))],
        micros=3,
    )
    kept_qk, give_qk = both.kept, both.give
    given_qk = to_y(give_qk, "qk")
    both = staged(
        partial_vg,
        dict(h=tie(h_attn, give_qk), given=given, grad=grad, grad_given=grad_given),
        dict(give=shape((tok_dev, 3 * D // 2)), kept=shape((D // WIDE + 1, tok_dev, WIDE), f32)),
        raws=dict(qkv=qkv_weight, out=out_weight),
        scratch=[
            pltpu.VMEM((D // WIDE, D // 2, WIDE), bf16),
            pltpu.VMEM((D // 2, D), bf16),
            pltpu.SemaphoreType.DMA((D // WIDE + 1,)),
        ],
        micros=3,
    )
    given_vg = to_y(both.give, "vg")
    table = staged(
        tables,
        {},
        dict(tab=shape((3, tok_dev, 128), f32), mask=shape((tok_dev, rank), f32), mask_t=shape((rank, tok_dev), f32), up=shape((D // 8, HALF * CB))),
        raws=dict(up=up_weight),
        scalars=dict(order=tie(block_order, both.give), starts=doc_starts),
        scratch=[pltpu.SemaphoreType.DMA],
        micros=0.1,
    )
    tab, mask, mask_t = table.tab, table.mask, table.mask_t
    up = staged(
        mlp_up,
        dict(h=tie(h_mlp, both.give), given=given),
        dict(
            early=shape((2 * tok_dev, CB)),
            late=shape((2 * tok_dev + 3 * rank, (HALF - 1) * CB)),
            kept=shape((HALF, 2 * tok_dev, CB), f32),
        ),
        raws=dict(up=up_weight),
        inside=dict(late=(2 * tok_dev, (HALF - 1) * CB)),
        scratch=[pltpu.VMEM((2 * HALF, D // 2, CB), bf16), pltpu.SemaphoreType.DMA((2 * HALF,))],
        micros=0.1,
    )
    heads = shape((HEADS, 2, tok_dev, 2 * HEAD_DIM))
    one = (HEADS, tok_dev, 2 * HEAD_DIM)
    made = staged(
        queries_keys,
        dict(
            h=tie(h_attn, up.kept),
            grad=grad,
            low=low,
            mask=mask,
            bias=bias,
            tab=tab,
            kept=kept_qk,
            given=given_qk,
            kept_vg=both.kept,
        ),
        dict(
            inner=shape((tok_dev, rank)),
            grad_inner=shape((tok_dev, rank)),
            send=heads,
            base=shape((2 * D // WIDE, tok_dev, WIDE), f32),
        ),
        inside=dict(send=one),
        micros=0.1,
    )
    inner_qkv, grad_inner_out = made.inner, made.grad_inner
    made = staged(
        values_grads,
        dict(base=made.base, given=given_vg),
        dict(send=heads),
        raws=dict(send=made.send),
        inside=dict(send=one),
        alias=dict(send="send"),
        micros=3,
    )
    parts = n_ctx // HEADS
    near = None if parts == 1 else [[g * HEADS + i for i in range(HEADS)] for g in range(parts)]

    def exchange(a):
        return lax.all_to_all(a, "ctx", 0, 0, tiled=True, axis_index_groups=near)

    shared = staged(
        mlp_share,
        dict(h=h_mlp, grad=grad, low=low, mask_t=mask_t),
        dict(
            late=shape(up.late.shape),
            products=shape((rank, 2 * tok_dev)),
            first=shape((D // 8, D + W_CUT)),
            second=shape((D // 8, 3 * D - W_CUT)),
        ),
        raws=dict(late=up.late, qkv=qkv_weight, out=out_weight),
        inside=dict(late=(3 * rank, (HALF - 1) * CB)),
        alias=dict(late="late"),
        scratch=[pltpu.SemaphoreType.DMA((3,))],
    )

    def quarters(y, x, name, *after):
        return [y, x, to_core(tie(y, *after), name + "y"), to_core(tie(x, *after), name + "x")]

    u_y = to_y(table.up, "u")
    early_given = to_y(up.early, "early")
    u_x = to_x(tie(u_y, early_given, shared.products), "u")
    late_given = to_y(shared.late, "late")
    arrived = tie(exchange(made.send), u_y)
    if parts == 1 and ndoc == 1:
        done = attention_one_document(block_order, arrived)
    else:
        all_pos, all_doc, _, _ = stream_layout(
            block_order[0], doc_starts[0], jnp.arange(total_rows, dtype=jnp.int32), total_rows, half_dev
        )
        far = None if parts == 1 else [[g * HEADS + i for g in range(parts)] for i in range(HEADS)]
        done = attention_documents(arrived, all_pos, all_doc, far, ctx // HEADS * HEADS * tok_dev)
    back = exchange(tie(done.reshape(HEADS, tok_dev, 4 * HEAD_DIM), u_x, late_given))
    v_y = to_y(tie(shared.first, done), "v")
    middle = staged(
        mlp_middle,
        dict(
            kept=up.kept,
            early=tie(early_given, done),
            late=late_given,
            grad=grad,
            grad_given=grad_given,
            low=low,
            bias=bias,
            products=shared.products,
        ),
        dict(
            pack=shape((5 * rank + tok_dev, D)),
            small=shape((2, rank, tok_dev), f32),
            grads=shape((2 * HALF, rank, CB)),
            kept=shape((tok_dev, D), f32),
            rest=shape((tok_dev, D)),
            down=shape((tok_dev, D), f32),
        ),
        raws=dict(down=down_weight, up=up_weight, u=quarters(u_y, u_x, "u", done)),
        scratch=[
            pltpu.VMEM((HALF, CB, D), bf16),
            pltpu.VMEM((D, HALF * CB), bf16),
            pltpu.SemaphoreType.DMA((HALF,)),
            pltpu.SemaphoreType.DMA((5,)),
        ],
        micros=0.1,
    )
    pack_given = to_y(middle.pack, "pack")
    v_x = to_x(tie(v_y, middle.pack), "v")
    w_y = to_y(tie(shared.second, pack_given), "w")
    rest_given = to_y(tie(middle.rest, pack_given), "rest")
    tail = staged(
        adapter_gradients,
        dict(
            arrived=back,
            tab=tab,
            low=low,
            mask=mask,
            h=h_attn,
            grad=grad,
            inner=inner_qkv,
            grad_inner=grad_inner_out,
        ),
        dict(
            att=shape((tok_dev, D)),
            gq=shape((tok_dev, 3 * D)),
            inner_out=shape((tok_dev, rank)),
            gi=shape((tok_dev, rank)),
            flat=shape((NB, rank, CB)),
        ),
        inside=dict(flat=(12, rank, CB)),
        parts=dict(flat=2),
        micros=0.1,
    )
    mlp = staged(
        mlp_finish,
        dict(
            small=middle.small,
            grads=middle.grads,
            pack=pack_given,
            kept=middle.kept,
            h=h_mlp,
            grad=grad,
            low=low,
            mask_t=mask_t,
        ),
        dict(inner_down=shape((rank, tok_dev)), back=shape((tok_dev, D), f32), flat=shape((NB, rank, CB))),
        raws=dict(flat=tail.flat),
        inside=dict(flat=(20, rank, CB)),
        alias=dict(flat="flat"),
        parts=dict(flat=2),
        micros=0.1,
    )
    flat = mlp.flat
    if columns != CB:
        flat = flat.reshape(NB, rank, CB // columns, columns).transpose(0, 2, 1, 3).reshape(n_dev, rank, columns)
    shares = lax.all_to_all(tie(flat, w_y), ("ctx", "wsh"), 0, 0, tiled=True)
    v_parts = quarters(v_y, v_x, "v", tail.att)
    w_x = to_x(tie(w_y, flat), "w")
    firsts = staged(
        first_outputs,
        dict(
            tok=tok,
            att=tail.att,
            gq=tail.gq,
            inner_out=tail.inner_out,
            gi=tail.gi,
            low=low,
            bias=bias,
            down=middle.down,
            inner_down=mlp.inner_down,
        ),
        dict(block=shape((tok_dev, D), f32), grad_h=shape((tok_dev, D), f32)),
        raws=dict(qkv=qkv_weight, out=out_weight, v=v_parts),
        scratch=[pltpu.VMEM((D, W_CUT), bf16), pltpu.VMEM((D, D), bf16), pltpu.SemaphoreType.DMA((10,))],
        micros=0.1,
    )
    ends = staged(
        last_outputs,
        dict(
            tok=tok,
            grad=grad,
            gain=norm_gains,
            gq=tail.gq,
            back=mlp.back,
            rest=rest_given,
            block=firsts.block,
            grad_h=firsts.grad_h,
        ),
        dict(block=shape((tok_dev, D)), tokens=shape((tok_dev, D), f32)),
        raws=dict(qkv=qkv_weight, w=quarters(w_y, w_x, "w", firsts.block, rest_given)),
        scratch=[pltpu.VMEM((D, 3 * D - W_CUT), bf16), pltpu.SemaphoreType.DMA((5,))],
        micros=0.1,
    )
    full = shape(adapters.shape, f32)
    new = staged(
        adamw,
        dict(adapters=adapters, first=first_moment, second=second_moment, parts=shares, given=adapters_given),
        dict(grad=full, new=full, first=full, second=full, low=shape(adapters.shape)),
        scalars=dict(chosen=doc_adapter),
        parts=dict(grad=ADAPTERS, new=ADAPTERS, first=ADAPTERS, second=ADAPTERS, low=ADAPTERS),
    )
    return (ends.block[None], ends.tokens[None], new.grad, new.new, new.first, new.second, new.low)


def solution(mesh):
    spread = P(None, None, ("ctx", "wsh"))
    rows = P("wsh", "ctx", None)
    half = P("wsh", None)
    in_specs = (rows, rows, P(), P(), half, half, half, half, P(), spread, spread, spread, half, P("wsh", None, None), half)
    out_specs = (rows, rows, spread, spread, spread, spread, spread)
    return jax.shard_map(on_device, mesh=mesh, in_specs=in_specs, out_specs=out_specs, check_vma=False)
```

```python
from types import SimpleNamespace

import jax
import jax.numpy as jnp
from jax import lax
from jax.experimental import pallas as pl
from jax.experimental.pallas import tpu as pltpu
from jax.sharding import PartitionSpec as P

D = 1024
HEADS = 16
FF = 4096
HEAD_DIM = 64
ROT = 16
ADAPTERS = 8
RANK = 16
STEP = 8
COLS = 8 * D + 2 * FF
CB = 512
NB = COLS // CB
WIDE = 512
W_CUT = 2048
HALF = FF // 2 // CB
QUERIES, KEYS = 512, 512

A_QKV, A_OUT, A_UP, A_DOWN = 0, 1, 2, 3
B_QKV, B_OUT, B_UP, B_DOWN = 7, 10, 11, 15

epsilon = 1e-05
adapter_scale = 8.0
rope_base = 10000.0
learn_rate = 0.02
beta_first = 0.5
beta_second = 0.5
weight_decay = 0.01
adam_epsilon = 1e-08
masked_value = -1e30

bf16 = jnp.bfloat16
f32 = jnp.float32

HBM = pl.BlockSpec(memory_space=pltpu.HBM)


def dot_nn(a, b):
    return jnp.dot(a, b, preferred_element_type=f32)


def dot_nt(a, b):
    return lax.dot_general(a, b, (((1,), (1,)), ((), ())), preferred_element_type=f32)


def dot_tn(a, b):
    return lax.dot_general(a, b, (((0,), (0,)), ((), ())), preferred_element_type=f32)


def shape(dims, dtype=bf16):
    return jax.ShapeDtypeStruct(tuple(dims), dtype)


def cut(index, width=D):
    return slice(index * width, (index + 1) * width)


class Stage:
    def __init__(self, loads, scalar, raw, out, targets):
        self.loads = loads
        self.scalar = scalar
        self.raw = raw
        self.out = out
        self.targets = targets
        self.waited = set()
        self.pending = []

    def __getattr__(self, name):
        buffer, copy = self.loads[name]
        if name not in self.waited:
            self.waited.add(name)
            copy.wait()
        return buffer

    def start(self, *ends):
        copy = pltpu.make_async_copy(*ends)
        copy.start()
        self.pending.append(copy)

    def store(self, buffer, at=None, into=None, sem=0):
        target, sems = self.targets[id(buffer)]
        if at is not None and into is None:
            into, sem = at, at
        source = buffer if at is None else buffer.at[at]
        self.start(source, target if into is None else target.at[into], sems.at[sem])


def staged(body, loads, results, raws=None, scalars=None, scratch=(), parts=None, micros=2, inside=None, alias=None):
    raws, scalars, parts, inside, alias = raws or {}, scalars or {}, parts or {}, inside or {}, alias or {}
    raw_list, raw_tree = jax.tree.flatten(raws)

    def kernel(*refs):
        refs = list(refs)

        def take(count):
            head = refs[:count]
            del refs[:count]
            return head

        scalar_from, load_from = take(len(scalars)), take(len(loads))
        raw = jax.tree.unflatten(raw_tree, take(len(raw_list)))
        targets = take(len(results))
        scalar_to, load_to, out = take(len(scalars)), take(len(loads)), take(len(results))
        (sems,) = take(1)
        out_sems = take(len(results))
        moves = [
            pltpu.make_async_copy(source, buffer, sems.at[i])
            for i, (source, buffer) in enumerate(zip(scalar_from + load_from, scalar_to + load_to))
        ]
        for move in moves:
            move.start()
        for move in moves[: len(scalars)]:
            move.wait()
        stage = Stage(
            dict(zip(loads, zip(load_to, moves[len(scalars) :]))),
            SimpleNamespace(**dict(zip(scalars, scalar_to))),
            SimpleNamespace(**raw),
            SimpleNamespace(**dict(zip(results, out))),
            {id(buffer): ends for buffer, ends in zip(out, zip(targets, out_sems))},
        )
        body(stage, *refs)
        for name in loads:
            getattr(stage, name)
        for copy in stage.pending:
            copy.wait()

    raw_names = list(raws)
    made = pl.pallas_call(
        kernel,
        out_shape=tuple(results.values()),
        in_specs=[HBM] * (len(scalars) + len(loads) + len(raw_list)),
        out_specs=(HBM,) * len(results),
        scratch_shapes=[pltpu.SMEM(a.shape, a.dtype) for a in scalars.values()]
        + [pltpu.VMEM(a.shape, a.dtype) for a in loads.values()]
        + [pltpu.VMEM(inside.get(n, s.shape), s.dtype) for n, s in results.items()]
        + [pltpu.SemaphoreType.DMA((len(loads) + len(scalars) + 1,))]
        + [pltpu.SemaphoreType.DMA((parts.get(n, 1),)) for n in results]
        + list(scratch),
        compiler_params=pltpu.CompilerParams(vmem_limit_bytes=64 * 1024 * 1024),
        input_output_aliases={
            len(scalars) + len(loads) + raw_names.index(a): list(results).index(b) for a, b in alias.items()
        },
        cost_estimate=pl.CostEstimate(flops=int(micros * 1.15e9), bytes_accessed=1024, transcendentals=0),
        name=body.__name__,
    )(*scalars.values(), *loads.values(), *raw_list)
    return SimpleNamespace(**dict(zip(results, made)))


def normalize(values):
    center = values - jnp.mean(values, axis=-1, keepdims=True)
    spread = jnp.mean(center * center, axis=-1, keepdims=True)
    scale = lax.rsqrt(spread + epsilon)
    return center * scale, scale


def give_adapters(stage):
    give = stage.out.give
    for a in range(ADAPTERS):
        give[cut(a, RANK), :] = stage.adapters[a].astype(bf16)
    row = lax.broadcasted_iota(jnp.int32, (RANK, give.shape[1]), 0)
    lane = lax.broadcasted_iota(jnp.int32, (RANK, give.shape[1]), 1)
    choice = jnp.zeros((RANK, give.shape[1]), f32)
    for j in range(stage.scalar.chosen.shape[1]):
        for a in range(ADAPTERS):
            choice = jnp.where((row == j) & (lane == a), stage.scalar.chosen[0, j, a].astype(f32), choice)
    give[ADAPTERS * RANK :, :] = choice.astype(bf16)
    stage.store(give)


def layer_norms(stage):
    out = stage.out
    normed, _ = normalize(stage.tok[...].astype(f32))
    gain, shift = stage.gain, stage.shift
    half = pl.multiple_of((1 - lax.axis_index("wsh")) * (D // 2), D // 2)
    for i, buffer in enumerate((out.attn, out.mlp)):
        buffer[...] = (normed * gain[i : i + 1, :] + shift[i : i + 1, :]).astype(bf16)
        out.give[:, cut(i, D // 2)] = buffer[:, pl.ds(half, D // 2)]
    stage.store(out.give)
    stage.store(out.attn)
    stage.store(out.mlp)


def tables(stage, sem):
    order, starts, out = stage.scalar.order, stage.scalar.starts, stage.out
    source = stage.raw.up
    copy = pltpu.make_async_copy(source.at[own_part(source, 4), hidden_columns(HALF)], out.up, sem)
    copy.start()
    rows, lanes = out.tab.shape[1:]
    ndoc = starts.shape[1]
    ctx = lax.axis_index("ctx")
    half = rows // 2

    def positions(dims, axis):
        index = lax.broadcasted_iota(jnp.int32, dims, axis)
        block = jnp.where(index < half, order[0, 2 * ctx], order[0, 2 * ctx + 1])
        return block * half + index % half

    pos = positions((rows, lanes), 0)
    start = jnp.zeros((rows, lanes), jnp.int32)
    for j in range(1, ndoc):
        start = jnp.where(pos >= starts[0, j], starts[0, j], start)
    lane = lax.broadcasted_iota(jnp.int32, (rows, lanes), 1) % HEAD_DIM
    frequency = jnp.ones((rows, lanes), f32)
    for i in range(1, ROT // 2):
        frequency = jnp.where(lane % (ROT // 2) == i, rope_base ** (-2.0 * i / ROT), frequency)
    angle = (pos - start).astype(f32) * frequency
    sine = jnp.sin(angle)
    out.tab[0] = jnp.where(lane < ROT, jnp.cos(angle), 1.0)
    out.tab[1] = jnp.where(lane < ROT // 2, -sine, 0.0)
    out.tab[2] = jnp.where((lane >= ROT // 2) & (lane < ROT), sine, 0.0)
    stage.store(out.tab)

    def used(dims, row_axis):
        pos = positions(dims, row_axis)
        doc = lax.broadcasted_iota(jnp.int32, dims, 1 - row_axis) // RANK
        held = jnp.zeros(dims, jnp.int32)
        for j in range(1, ndoc):
            held = jnp.where(pos >= starts[0, j], j, held)
        return (held == doc).astype(f32)

    out.mask[...] = used(out.mask.shape, 0)
    out.mask_t[...] = used(out.mask_t.shape, 1)
    stage.store(out.mask)
    stage.store(out.mask_t)
    copy.wait()
    stage.store(out.up)


def choose_adapters(stage):
    adapters, given = stage.adapters, stage.given
    rows = stage.out.rows
    target, sems = stage.targets[id(rows)]
    columns = adapters.shape[2]
    wsh = lax.axis_index("wsh")
    for j in range(rows.shape[0] // RANK):
        index = 0
        for a in range(1, ADAPTERS):
            index = index + a * stage.scalar.chosen[0, j, a]
        start = pl.multiple_of(index * RANK, RANK)
        own_at = pl.multiple_of(wsh * columns, 128)
        other_at = pl.multiple_of((1 - wsh) * columns, 128)
        rows[cut(j, RANK), pl.ds(own_at, columns)] = adapters[index].astype(bf16)
        rows[cut(j, RANK), pl.ds(other_at, columns)] = given[pl.ds(start, RANK), :]
    for i in range(target.shape[0]):
        stage.start(rows, target.at[i], sems.at[i])


def part_orders(share):
    ctx = lax.axis_index("ctx")
    if share == 2:
        return ctx % 2, 1 - ctx % 2
    mine = ctx % 2 * 2 + ctx // 2 % 2
    return mine, mine ^ 1, mine ^ 2, mine ^ 3


def rows_at(first, count):
    return pl.ds(pl.multiple_of(first, count), count)


def own_part(weight, share):
    rows = weight.shape[0] // share
    return rows_at(part_orders(share)[0] * rows, rows)


def place_weights(own, chunks, target, sems, first=0):
    half = own.shape[0]
    own_half = lax.axis_index("wsh")
    copies = [pltpu.make_async_copy(own, target.at[rows_at(own_half * half, half), :], sems.at[first])]
    for column, source_column, width, parts in chunks:
        rows = half // len(parts)
        for order, part in zip(part_orders(len(parts)), parts):
            copies.append(
                pltpu.make_async_copy(
                    part.at[:, source_column : source_column + width],
                    target.at[rows_at((1 - own_half) * half + order * rows, rows), column : column + width],
                    sems.at[first + len(copies)],
                )
            )
    for copy in copies:
        copy.start()
    return copies


def turn(values, tab, sign):
    left = pltpu.roll(values, 120, 1)
    right = pltpu.roll(values, 8, 1)
    return values * tab[0] + sign * (left * tab[1] + right * tab[2])


def swap_halves(first, second):
    low = lax.broadcasted_iota(jnp.int32, first.shape, 1) < HEAD_DIM
    one = jnp.where(low, first, pltpu.roll(second, HEAD_DIM, 1))
    two = jnp.where(low, pltpu.roll(first, HEAD_DIM, 1), second)
    return one, two


def both_streams(stage, side=0):
    half = pl.multiple_of(lax.axis_index("wsh") * (D // 2), D // 2)
    return jnp.concatenate([stage.h[:, pl.ds(half, D // 2)], stage.given[:, cut(side, D // 2)]], axis=0)


def weight_columns(source, first, weights, sems):
    copies = []
    for n in range(weights.shape[0]):
        copies.append(
            pltpu.make_async_copy(source.at[:, first + n * WIDE : first + (n + 1) * WIDE], weights.at[n], sems.at[n])
        )
        copies[-1].start()
    return copies


def partial_qk(stage, weights, sems):
    copies = weight_columns(stage.raw.qkv, 0, weights, sems)
    both = both_streams(stage)
    rows = both.shape[0] // 2
    for n, copy in enumerate(copies):
        copy.wait()
        part = dot_nn(both, weights[n])
        stage.out.give[:, cut(n, WIDE)] = part[rows:].astype(bf16)
        stage.out.kept[n] = part[:rows]
    stage.store(stage.out.give)
    stage.store(stage.out.kept)


def partial_vg(stage, weights, out_rows, sems):
    copies = weight_columns(stage.raw.qkv, 2 * D, weights, sems)
    out_copy = pltpu.make_async_copy(stage.raw.out, out_rows, sems.at[len(copies)])
    out_copy.start()
    both = both_streams(stage)
    rows = both.shape[0] // 2
    for n, copy in enumerate(copies):
        copy.wait()
        part = dot_nn(both, weights[n])
        stage.out.give[:, cut(n, WIDE)] = part[rows:].astype(bf16)
        stage.out.kept[n] = part[:rows]
    grads = jnp.concatenate([stage.grad[...], stage.grad_given[...]], axis=0)
    out_copy.wait()
    part = dot_nt(grads, out_rows[...])
    stage.out.give[:, D:] = part[rows:].astype(bf16)
    stage.store(stage.out.give)
    stage.out.kept[D // WIDE] = part[:rows]
    stage.store(stage.out.kept)


def queries_keys(stage):
    low, mask, bias, tab, kept, given = stage.low, stage.mask[...], stage.bias, stage.tab, stage.kept, stage.given
    inner = (dot_nt(stage.h[...], low[A_QKV]) * mask).astype(bf16)
    stage.out.inner[...] = inner
    stage.store(stage.out.inner)
    grad_inner = (adapter_scale * dot_nt(stage.grad[...], low[B_OUT]) * mask).astype(bf16)
    stage.out.grad_inner[...] = grad_inner
    stage.store(stage.out.grad_inner)
    steps = D // WIDE
    for n in range(steps):
        sides = []
        for kind in range(2):
            at = cut(kind * steps + n, WIDE)
            part = kept[kind * steps + n] + given[:, at].astype(f32) + bias[:, at]
            sides.append(part + adapter_scale * dot_nn(inner, low[B_QKV + kind][:, cut(n, WIDE)]))
        for pair in range(WIDE // 128):
            query = turn(sides[0][:, cut(pair, 128)], tab, 1.0) * HEAD_DIM**-0.5
            key = turn(sides[1][:, cut(pair, 128)], tab, 1.0)
            head = n * WIDE // HEAD_DIM + 2 * pair
            for i, both in enumerate(swap_halves(query, key)):
                stage.out.send[head + i] = both.astype(bf16)
    stage.store(stage.out.send, into=(slice(None), 0))
    base, kept, wsh = stage.out.base, stage.kept_vg, lax.axis_index("wsh")
    for n in range(steps):
        base[n] = kept[n] + bias[:, 2 * D + n * WIDE : 2 * D + (n + 1) * WIDE]
        base[n] += adapter_scale * dot_nn(inner, low[B_QKV + 2][:, cut(n, WIDE)])
        base[steps + n] = jnp.where(wsh == n, kept[steps], 0.0) + dot_nn(grad_inner, low[A_OUT][:, cut(n, WIDE)])
    stage.store(base)


def values_grads(stage):
    base, given = stage.base, stage.given
    steps = D // WIDE
    wsh = lax.axis_index("wsh")
    for n in range(steps):
        value = base[n] + given[:, cut(n, WIDE)].astype(f32)
        grad = base[steps + n] + jnp.where(wsh == n, 0.0, given[:, D:].astype(f32))
        for pair in range(WIDE // 128):
            head = n * WIDE // HEAD_DIM + 2 * pair
            for i, both in enumerate(swap_halves(value[:, cut(pair, 128)], grad[:, cut(pair, 128)])):
                stage.out.send[head + i] = both.astype(bf16)
    stage.store(stage.out.send, into=(slice(None), 1))


def attention(stage, xt, dks, dvs, ks, vs, aq, s_scr, e_scr):
    order = stage.scalar.order
    rows = aq.shape[0]
    blocks = order.shape[1]
    half = rows // blocks
    hd = HEAD_DIM
    x = stage.arrived
    per = x.shape[2] // half
    for i in range(blocks):
        start = pl.multiple_of(order[0, i] * half, half)
        for side in range(2):
            aq[pl.ds(start, half), cut(side, 2 * hd)] = x[i // per, side, cut(i % per, half), :]
    for t in range(rows // KEYS):
        part = aq[cut(t, KEYS), :]
        ks[cut(t, KEYS), :] = part[:, hd : 2 * hd]
        vs[cut(t, KEYS), :] = part[:, 2 * hd : 3 * hd]
        xt[:, cut(t, KEYS)] = part.T
    dks[...] = jnp.zeros_like(dks)
    dvs[...] = jnp.zeros_like(dvs)
    later = lax.broadcasted_iota(jnp.int32, (KEYS, QUERIES), 0) - lax.broadcasted_iota(jnp.int32, (KEYS, QUERIES), 1)
    for b in range(rows // QUERIES):
        at = cut(b, QUERIES)
        q_t = xt[0:hd, at]
        g_t = xt[3 * hd : 4 * hd, at]
        tiles = [(cut(t, KEYS), b * QUERIES - t * KEYS) for t in range(-(-(b + 1) * QUERIES // KEYS))]
        top = jnp.full((8, QUERIES), masked_value, f32)
        for part, ahead in tiles:
            s = dot_nn(ks[part, :], q_t)
            if ahead < KEYS - 1:
                s = jnp.where(later <= ahead, s, masked_value)
            s_scr[part, :] = s
            top = jnp.maximum(top, jnp.max(s.reshape(KEYS // 8, 8, QUERIES), axis=0))
        top = jnp.max(top, axis=0, keepdims=True)
        total = jnp.zeros((8, QUERIES), f32)
        att = jnp.zeros((hd, QUERIES), f32)
        for part, _ in tiles:
            e = jnp.exp(s_scr[part, :] - top)
            total = total + jnp.sum(e.reshape(KEYS // 8, 8, QUERIES), axis=0)
            e = e.astype(bf16)
            e_scr[part, :] = e
            att = att + dot_nn(xt[2 * hd : 3 * hd, part], e)
        inverse = 1.0 / jnp.sum(total, axis=0, keepdims=True)
        att = att * inverse
        g_f = g_t.astype(f32)
        delta = jnp.sum(g_f * att, axis=0, keepdims=True) * inverse
        g_n = (g_f * inverse).astype(bf16)
        dq = jnp.zeros((hd, QUERIES), f32)
        for part, _ in tiles:
            e = e_scr[part, :]
            dp = dot_nn(vs[part, :], g_n)
            ds = (e.astype(f32) * (dp - delta)).astype(bf16)
            dq = dq + dot_nn(xt[hd : 2 * hd, part], ds)
            dks[part, :] += dot_nt(ds, q_t)
            dvs[part, :] += dot_nt(e, g_n)
        both = jnp.concatenate([att, dq * hd**-0.5], axis=0)
        aq[at, 0 : 2 * hd] = both.T.astype(bf16)
    for t in range(rows // KEYS):
        aq[cut(t, KEYS), 2 * hd : 3 * hd] = dks[cut(t, KEYS), :].astype(bf16)
        aq[cut(t, KEYS), 3 * hd :] = dvs[cut(t, KEYS), :].astype(bf16)
    for i in range(blocks):
        start = pl.multiple_of(order[0, i] * half, half)
        stage.out.back[cut(i, half), :] = aq[pl.ds(start, half), :]
    stage.store(stage.out.back)


def attention_one_document(order, arrived):
    rows = arrived.shape[0] * arrived.shape[2]
    hd = HEAD_DIM
    return staged(
        attention,
        dict(arrived=arrived),
        dict(back=shape((rows, 4 * hd))),
        scalars=dict(order=order),
        scratch=[
            pltpu.VMEM((4 * hd, rows), bf16),
            pltpu.VMEM((rows, hd), f32),
            pltpu.VMEM((rows, hd), f32),
            pltpu.VMEM((rows, hd), bf16),
            pltpu.VMEM((rows, hd), bf16),
            pltpu.VMEM((rows, 4 * hd), bf16),
            pltpu.VMEM((rows, QUERIES), f32),
            pltpu.VMEM((rows, QUERIES), bf16),
        ],
        micros=17,
    ).back


def attention_documents(arrived, pos, doc, groups, first_row):
    rows = arrived.shape[0] * arrived.shape[2]
    hd = HEAD_DIM
    qk, vg = (arrived[:, side].reshape(rows, 2 * hd) for side in range(2))
    q, k, v, g = qk[:, :hd], qk[:, hd:], vg[:, :hd], vg[:, hd:]
    if groups is not None:
        both = lax.all_gather(jnp.concatenate([k, v], 1), "ctx", axis=0, tiled=True, axis_index_groups=groups)
        k, v = both[:, :hd], both[:, hd:]
    step = 512
    my_pos = lax.dynamic_slice_in_dim(pos, first_row, rows)
    my_doc = lax.dynamic_slice_in_dim(doc, first_row, rows)

    def one(sums, item):
        q_b, g_b, pos_b, doc_b = item
        scores = dot_nt(q_b, k)
        allowed = (doc_b[:, None] == doc[None, :]) & (pos[None, :] <= pos_b[:, None])
        scores = jnp.where(allowed, scores, masked_value)
        top = jnp.max(scores, axis=1, keepdims=True)
        weights = jnp.exp(scores - top)
        weights = weights / jnp.sum(weights, axis=1, keepdims=True)
        weights_low = weights.astype(bf16)
        att = dot_nn(weights_low, v)
        delta = jnp.sum(g_b.astype(f32) * att, axis=1, keepdims=True)
        ds = (weights * (dot_nt(g_b, v) - delta)).astype(bf16)
        dq = dot_nn(ds, k) * hd**-0.5
        sums = (sums[0] + dot_tn(ds, q_b), sums[1] + dot_tn(weights_low, g_b))
        return sums, jnp.concatenate([att, dq], 1).astype(bf16)

    zero = jnp.zeros((k.shape[0], hd), f32)
    split = lambda a: a.reshape((rows // step, step) + a.shape[1:])
    sums, att_dq = lax.scan(one, (zero, zero), tuple(map(split, (q, g, my_pos, my_doc))))
    sums = jnp.concatenate(sums, 1)
    if groups is not None:
        sums = lax.psum_scatter(sums, "ctx", scatter_dimension=0, tiled=True, axis_index_groups=groups)
    return jnp.concatenate([att_dq.reshape(rows, 2 * hd), sums.astype(bf16)], axis=1)


def swapped(rows):
    half = rows.shape[0] // 2
    return jnp.concatenate([rows[half:], rows[:half]], axis=0)


def hidden_block(j):
    wsh = lax.axis_index("wsh")
    return (wsh if j < HALF else 1 - wsh) * HALF + j % HALF


def hidden_columns(j):
    return pl.ds(pl.multiple_of(hidden_block(j // HALF * HALF) * CB, HALF * CB), HALF * CB)


def up_blocks(source, weights, sems, order):
    copies = {}
    for j in order:
        first = pl.multiple_of(hidden_block(j) * CB, CB)
        copies[j] = pltpu.make_async_copy(source.at[:, pl.ds(first, CB)], weights.at[j], sems.at[j])
        copies[j].start()
    return copies


def adapter_block(low, first, j):
    return low[first + hidden_block(j) // 2, :, cut(j % 2, CB)]


def mlp_up(stage, weights, sems):
    out = stage.out
    order = [*range(HALF, 2 * HALF), *range(HALF)]
    copies = up_blocks(stage.raw.up, weights, sems, order)
    both = both_streams(stage, 1)
    for j in order:
        copies[j].wait()
        part = dot_nn(both, weights[j])
        if j < HALF:
            out.kept[j] = part
        elif j == HALF:
            out.early[...] = part.astype(bf16)
            stage.store(out.early)
        else:
            out.late[:, cut(j - HALF - 1, CB)] = part.astype(bf16)
            if j == 2 * HALF - 1:
                stage.store(out.late, into=pl.ds(0, part.shape[0]))
    stage.store(out.kept)


def share_at(kind, j, rank, rows):
    down, right = divmod(kind * HALF + j, HALF - 1)
    return pl.ds(rows + down * rank, rank), cut(right, CB)


def mlp_share(stage, sems):
    out = stage.out
    qkv, weight = stage.raw.qkv, stage.raw.out
    mine = own_part(qkv, 4)
    copies = [
        pltpu.make_async_copy(weight.at[mine, :], out.first.at[:, :D], sems.at[0]),
        pltpu.make_async_copy(qkv.at[mine, :W_CUT], out.first.at[:, D:], sems.at[1]),
        pltpu.make_async_copy(qkv.at[mine, W_CUT:], out.second, sems.at[2]),
    ]
    for copy in copies:
        copy.start()
    share, low, mask = out.late, stage.low, stage.mask_t[...]
    rank, rows = mask.shape
    for j in range(HALF):
        share[share_at(0, j, rank, 0)] = adapter_block(low, A_DOWN, HALF + j)
        share[share_at(1, j, rank, 0)] = adapter_block(low, B_UP, HALF + j)
    inner = (dot_nt(low[A_UP], stage.h[...]) * mask).astype(bf16)
    back = (adapter_scale * dot_nt(low[B_DOWN], stage.grad[...]) * mask).astype(bf16)
    zero = jnp.zeros((rank, CB - 2 * rows), bf16)
    share[share_at(2, 0, rank, 0)] = jnp.concatenate([inner, back, zero], axis=1)
    stage.store(share, into=pl.ds(2 * rows, 3 * rank))
    out.products[...] = jnp.concatenate([inner, back], axis=1)
    stage.store(out.products)
    for copy in copies:
        copy.wait()
    for buffer in (out.first, out.second):
        stage.store(buffer)


def diagonal(one, two):
    zero = jnp.zeros_like(one)
    return jnp.concatenate([jnp.concatenate([one, zero], axis=1), jnp.concatenate([zero, two], axis=1)], axis=0)


def mlp_middle(stage, down_rows, up_rows, down_sems, up_sems):
    out, low = stage.out, stage.low
    copies = []
    for j in range(HALF):
        copies.append(pltpu.make_async_copy(stage.raw.down.at[cut(j, CB), :], down_rows.at[j], down_sems.at[j]))
        copies[-1].start()
    up_copies = place_weights(
        stage.raw.up.at[:, hidden_columns(0)], [(0, 0, HALF * CB, stage.raw.u)], up_rows, up_sems, 0
    )
    grads = jnp.concatenate([stage.grad[...], stage.grad_given[...]], axis=0)
    rows = grads.shape[0] // 2
    products, late = stage.products[...], stage.late
    rank = products.shape[0]
    other = late[share_at(2, 0, rank, 2 * rows)]
    inner, back = (diagonal(products[:, cut(i, rows)], other[:, cut(i, rows)]) for i in range(2))
    sums = None
    grad_ups = []
    for j in range(HALF):
        at = cut(j, CB)
        a_both = jnp.concatenate([adapter_block(low, A_DOWN, j), late[share_at(0, j, rank, 2 * rows)]], axis=0)
        b_both = jnp.concatenate([adapter_block(low, B_UP, j), late[share_at(1, j, rank, 2 * rows)]], axis=0)
        part = stage.early[...] if j == 0 else late[: 2 * rows, cut(j - 1, CB)]
        shift = pl.multiple_of(4 * D + hidden_block(j) * CB, CB)
        up = stage.kept[j] + swapped(part.astype(f32)) + stage.bias[:, pl.ds(shift, CB)]
        up = up + adapter_scale * dot_tn(inner, b_both)
        spread = 0.5 * (1.0 + lax.erf(up * (0.5**0.5)))
        hidden = (up * spread).astype(bf16)
        slope = spread + up * (jnp.exp(-0.5 * up * up) * (0.5 / jnp.pi) ** 0.5)
        copies[j].wait()
        down = down_rows[j]
        grad_hidden = dot_nt(grads, down) + dot_tn(back, a_both)
        grad_up = (grad_hidden * slope).astype(bf16)
        grad_ups.append(grad_up)
        parts = dot_nn(hidden, down), dot_nt(a_both, hidden), dot_nt(b_both, grad_up)
        sums = parts if sums is None else tuple(one + two for one, two in zip(sums, parts))
        a_grad = dot_nn(back, hidden).astype(bf16)
        b_grad = (adapter_scale * dot_nn(inner, grad_up)).astype(bf16)
        out.grads[j], out.grads[HALF + j] = a_grad[:rank], b_grad[:rank]
        out.pack[pack_at(0, j, rank)], out.pack[pack_at(1, j, rank)] = a_grad[rank:], b_grad[rank:]
    down, inner_down, gi_up = sums
    out.small[0], out.small[1] = inner_down[:rank, :rows], gi_up[:rank, :rows]
    out.pack[4 * rank : 5 * rank, :] = jnp.zeros((rank, D), bf16)
    out.pack[4 * rank : 5 * rank, 0:rows] = inner_down[rank:, rows:].astype(bf16)
    out.pack[4 * rank : 5 * rank, rows : 2 * rows] = gi_up[rank:, rows:].astype(bf16)
    for copy in up_copies:
        copy.wait()
    total = None
    for j in range(HALF):
        part = dot_nt(grad_ups[j], up_rows[:, cut(j, CB)])
        total = part if total is None else total + part
    out.pack[5 * rank :, :] = total[rows:].astype(bf16)
    stage.store(out.pack)
    out.kept[...] = total[:rows]
    out.rest[...] = down[rows:].astype(bf16)
    out.down[...] = down[:rows]
    for buffer in (out.small, out.grads, out.kept, out.rest, out.down):
        stage.store(buffer)


def pack_at(kind, j, rank):
    return pl.ds((2 * kind + j // 2) * rank, rank), cut(j % 2, CB)


def mlp_finish(stage):
    out, low, mask = stage.out, stage.low, stage.mask_t[...]
    rank, rows = mask.shape
    pack, small, wsh = stage.pack, stage.small, lax.axis_index("wsh")
    extra = pack[4 * rank : 5 * rank, :].astype(f32)
    inner_down = ((small[0] + extra[:, 0:rows]) * mask).astype(bf16)
    gi_up = (adapter_scale * (small[1] + extra[:, rows : 2 * rows]) * mask).astype(bf16)
    for j in range(HALF):
        for kind in range(2):
            out.flat[2 + kind * 2 * HALF + wsh * HALF + j] = stage.grads[kind * HALF + j]
            out.flat[2 + kind * 2 * HALF + (1 - wsh) * HALF + j] = pack[pack_at(kind, j, rank)]
    up_grad = dot_nn(gi_up, stage.h[...])
    down_grad = adapter_scale * dot_nn(inner_down, stage.grad[...])
    for i in range(2):
        out.flat[i] = up_grad[:, cut(i, CB)].astype(bf16)
        out.flat[18 + i] = down_grad[:, cut(i, CB)].astype(bf16)
    per = D // CB
    stage.store(out.flat, at=pl.ds(0, 10), into=pl.ds(A_UP * per, 10), sem=0)
    stage.store(out.flat, at=pl.ds(10, 10), into=pl.ds(B_UP * per, 10), sem=1)
    out.inner_down[...] = inner_down
    stage.store(out.inner_down)
    out.back[...] = stage.kept[...] + pack[5 * rank :, :].astype(f32) + dot_tn(gi_up, low[A_UP])
    stage.store(out.back)


def adapter_gradients(stage):
    arrived, tab = stage.arrived, stage.tab
    att, gq, flat = stage.out.att, stage.out.gq, stage.out.flat
    for pair in range(HEADS // 2):
        at = cut(pair, 128)
        one, two = arrived[2 * pair].astype(f32), arrived[2 * pair + 1].astype(f32)
        attended, query = swap_halves(one[:, :128], two[:, :128])
        key, value = swap_halves(one[:, 128:], two[:, 128:])
        att[:, at] = attended.astype(bf16)
        for kind, part in enumerate((turn(query, tab, -1.0), turn(key, tab, -1.0), value)):
            gq[:, kind * D + pair * 128 : kind * D + (pair + 1) * 128] = part.astype(bf16)
    stage.store(att)
    stage.store(gq)
    low, mask, h, grad = stage.low, stage.mask[...], stage.h, stage.grad
    inner_out = (dot_nt(att[...], low[A_OUT]) * mask).astype(bf16)
    stage.out.inner_out[...] = inner_out
    stage.store(stage.out.inner_out)
    gi = sum(dot_nt(gq[:, cut(i)], low[B_QKV + i]) for i in range(3))
    gi = (adapter_scale * gi * mask).astype(bf16)
    stage.out.gi[...] = gi
    stage.store(stage.out.gi)
    per = D // CB

    def put(block, value):
        place = block if block < A_UP else block - B_QKV + A_UP
        for i in range(per):
            flat[place * per + i] = value[:, cut(i, CB)].astype(bf16)

    put(A_QKV, dot_tn(gi, h[...]))
    put(A_OUT, dot_tn(stage.grad_inner[...], att[...]))
    put(B_OUT, adapter_scale * dot_tn(inner_out, grad[...]))
    for i in range(3):
        put(B_QKV + i, adapter_scale * dot_tn(stage.inner[...], gq[:, cut(i)]))
    first, rest = A_UP * per, (B_UP - B_QKV) * per
    stage.store(flat, at=pl.ds(0, first), into=pl.ds(0, first), sem=0)
    stage.store(flat, at=pl.ds(first, rest), into=pl.ds(B_QKV * per, rest), sem=1)


def first_outputs(stage, wq, wo, sems):
    raw, low, bias = stage.raw, stage.low, stage.bias
    o_copies = place_weights(raw.out, [(0, 0, D, raw.v)], wo, sems)
    q_copies = place_weights(raw.qkv.at[:, :W_CUT], [(0, D, W_CUT, raw.v)], wq, sems, 5)
    att, inner_out, inner_down = stage.att[...], stage.inner_out[...], stage.inner_down[...]
    for copy in o_copies:
        copy.wait()
    for n in range(D // WIDE):
        at = cut(n, WIDE)
        shift = n * WIDE
        part = dot_nn(att, wo[:, at]) + bias[:, 3 * D + shift : 3 * D + shift + WIDE]
        part = part + adapter_scale * dot_nn(inner_out, low[B_OUT][:, at])
        mlp = stage.down[:, at] + bias[:, 4 * D + FF + shift : 4 * D + FF + shift + WIDE]
        mlp = mlp + adapter_scale * dot_tn(inner_down, low[B_DOWN][:, at])
        stage.out.block[:, at] = part + stage.tok[:, at].astype(f32) + mlp
    stage.store(stage.out.block)
    for copy in q_copies:
        copy.wait()
    stage.out.grad_h[...] = dot_nt(stage.gq[:, :W_CUT], wq[...]) + dot_nn(stage.gi[...], low[A_QKV])
    stage.store(stage.out.grad_h)


def last_outputs(stage, wq, sems):
    raw, gain, out = stage.raw, stage.gain, stage.out
    copies = place_weights(raw.qkv.at[:, W_CUT:], [(0, 0, 3 * D - W_CUT, raw.w)], wq, sems)
    normed, scale = normalize(stage.tok[...].astype(f32))
    out.block[...] = (stage.block[...] + stage.rest[...].astype(f32)).astype(bf16)
    stage.store(out.block)
    for copy in copies:
        copy.wait()
    grad_h = stage.grad_h[...] + dot_nt(stage.gq[:, W_CUT:], wq[...])
    grad_n = grad_h * gain[0:1, :] + stage.back[...] * gain[1:2, :]
    grad_v = grad_n - jnp.mean(grad_n, axis=-1, keepdims=True) - normed * jnp.mean(grad_n * normed, axis=-1, keepdims=True)
    out.tokens[...] = stage.grad[...].astype(f32) + scale * grad_v
    stage.store(out.tokens)


def adamw(stage):
    chosen, parts, out = stage.scalar.chosen, stage.parts, stage.out
    given, wsh = stage.given, lax.axis_index("wsh")
    sums = []
    for stream in range(2):
        total = parts[stream].astype(f32)
        for source in range(stream + 2, parts.shape[0], 2):
            total = total + parts[source].astype(f32)
        sums.append(total)
    ndoc = sums[0].shape[0] // RANK
    for a in range(ADAPTERS):
        grad = None
        for stream in range(2):
            for j in range(ndoc):
                own = chosen[0, j, a].astype(f32)
                other = given[ADAPTERS * RANK + j : ADAPTERS * RANK + j + 1, a : a + 1].astype(f32)
                term = jnp.where(wsh == stream, own, other) * sums[stream][cut(j, RANK), :]
                grad = term if grad is None else grad + term
        new_first = beta_first * stage.first[a] + (1.0 - beta_first) * grad
        new_second = beta_second * stage.second[a] + (1.0 - beta_second) * grad * grad
        first_hat = new_first / (1.0 - beta_first**STEP)
        second_hat = new_second / (1.0 - beta_second**STEP)
        old = stage.adapters[a]
        new = old - learn_rate * (first_hat / (jnp.sqrt(second_hat) + adam_epsilon) + weight_decay * old)
        for buffer, value in (
            (out.grad, grad),
            (out.new, new),
            (out.first, new_first),
            (out.second, new_second),
            (out.low, new.astype(bf16)),
        ):
            buffer[a] = value
            stage.store(buffer, a)


def stream_layout(order_row, starts_row, rows, total_rows, half_dev):
    slot = rows // half_dev
    picked = (slot[:, None] == jnp.arange(order_row.shape[0], dtype=jnp.int32)[None, :]).astype(jnp.int32)
    pos = jnp.sum(picked * order_row[None, :], axis=1) * half_dev + rows % half_dev
    finish = jnp.concatenate([starts_row[1:], jnp.full((1,), total_rows, jnp.int32)])
    inside = ((pos[:, None] >= starts_row[None, :]) & (pos[:, None] < finish[None, :])).astype(jnp.int32)
    doc = jnp.sum(inside * jnp.arange(starts_row.shape[0], dtype=jnp.int32)[None, :], axis=1)
    place = pos - jnp.sum(inside * starts_row[None, :], axis=1)
    return pos, doc, place, inside


def tie(first, *others):
    return lax.optimization_barrier((first,) + others)[0]


def on_device(
    tokens,
    out_cotangent,
    norm_gains,
    norm_biases,
    qkv_weight,
    out_weight,
    up_weight,
    down_weight,
    proj_biases,
    adapters,
    first_moment,
    second_moment,
    doc_starts,
    doc_adapter,
    block_order,
):
    n_ctx = lax.axis_size("ctx")
    n_dev = n_ctx * lax.axis_size("wsh")
    ctx = lax.axis_index("ctx")
    wsh = lax.axis_index("wsh")
    tok_dev = tokens.shape[1]
    half_dev = tok_dev // 2
    total_rows = tok_dev * n_ctx
    ndoc = doc_starts.shape[1]
    rank = ndoc * RANK
    columns = adapters.shape[2]
    tok, grad = tokens[0], out_cotangent[0]
    bias = proj_biases[None, :]

    def to_y(a, name):
        with jax.named_scope("y_" + name):
            return lax.ppermute(a, "wsh", [(0, 1), (1, 0)])

    def to_x(a, name):
        with jax.named_scope("x_" + name):
            return lax.ppermute(a, "ctx", [(i, i ^ 2) for i in range(n_ctx)])

    def to_core(a, name):
        with jax.named_scope("c_" + name):
            return lax.ppermute(a, "ctx", [(i, i ^ 1) for i in range(n_ctx)])

    give = staged(
        give_adapters,
        dict(adapters=adapters),
        dict(give=shape(((ADAPTERS + 1) * RANK, columns))),
        scalars=dict(chosen=doc_adapter),
    ).give
    adapters_given = to_y(give, "adapters")
    normed = staged(
        layer_norms,
        dict(tok=tie(tok, give), gain=norm_gains, shift=norm_biases),
        dict(attn=shape(tok.shape), mlp=shape(tok.shape), give=shape((tok_dev, D))),
    )
    h_attn, h_mlp = normed.attn, normed.mlp
    given = to_y(normed.give, "h")
    grad_given = to_y(tie(grad, normed.give), "grad")
    chosen_rows = staged(
        choose_adapters,
        dict(adapters=adapters, given=tie(adapters_given, h_attn)),
        dict(rows=shape((n_ctx, rank, 2 * columns))),
        scalars=dict(chosen=doc_adapter),
        parts=dict(rows=n_ctx),
        inside=dict(rows=(rank, 2 * columns)),
    ).rows
    low = lax.all_to_all(chosen_rows, "ctx", 0, 0, tiled=True)
    if n_ctx != HEADS:
        low = low.reshape(COLS // D, n_ctx // HEADS, rank, 2 * columns).transpose(0, 2, 1, 3).reshape(COLS // D, rank, D)

    both = staged(
        partial_qk,
        dict(h=h_attn, given=tie(given, chosen_rows)),
        dict(give=shape((tok_dev, 2 * D)), kept=shape((2 * D // WIDE, tok_dev, WIDE), f32)),
        raws=dict(qkv=qkv_weight),
        scratch=[pltpu.VMEM((2 * D // WIDE, D // 2, WIDE), bf16), pltpu.SemaphoreType.DMA((2 * D // WIDE,))],
        micros=3,
    )
    kept_qk, give_qk = both.kept, both.give
    given_qk = to_y(give_qk, "qk")
    both = staged(
        partial_vg,
        dict(h=tie(h_attn, give_qk), given=given, grad=grad, grad_given=grad_given),
        dict(give=shape((tok_dev, 3 * D // 2)), kept=shape((D // WIDE + 1, tok_dev, WIDE), f32)),
        raws=dict(qkv=qkv_weight, out=out_weight),
        scratch=[
            pltpu.VMEM((D // WIDE, D // 2, WIDE), bf16),
            pltpu.VMEM((D // 2, D), bf16),
            pltpu.SemaphoreType.DMA((D // WIDE + 1,)),
        ],
        micros=3,
    )
    given_vg = to_y(both.give, "vg")
    table = staged(
        tables,
        {},
        dict(tab=shape((3, tok_dev, 128), f32), mask=shape((tok_dev, rank), f32), mask_t=shape((rank, tok_dev), f32), up=shape((D // 8, HALF * CB))),
        raws=dict(up=up_weight),
        scalars=dict(order=tie(block_order, both.give), starts=doc_starts),
        scratch=[pltpu.SemaphoreType.DMA],
        micros=0.1,
    )
    tab, mask, mask_t = table.tab, table.mask, table.mask_t
    up = staged(
        mlp_up,
        dict(h=tie(h_mlp, both.give), given=given),
        dict(
            early=shape((2 * tok_dev, CB)),
            late=shape((2 * tok_dev + 3 * rank, (HALF - 1) * CB)),
            kept=shape((HALF, 2 * tok_dev, CB), f32),
        ),
        raws=dict(up=up_weight),
        inside=dict(late=(2 * tok_dev, (HALF - 1) * CB)),
        scratch=[pltpu.VMEM((2 * HALF, D // 2, CB), bf16), pltpu.SemaphoreType.DMA((2 * HALF,))],
        micros=0.1,
    )
    heads = shape((HEADS, 2, tok_dev, 2 * HEAD_DIM))
    one = (HEADS, tok_dev, 2 * HEAD_DIM)
    made = staged(
        queries_keys,
        dict(
            h=tie(h_attn, up.kept),
            grad=grad,
            low=low,
            mask=mask,
            bias=bias,
            tab=tab,
            kept=kept_qk,
            given=given_qk,
            kept_vg=both.kept,
        ),
        dict(
            inner=shape((tok_dev, rank)),
            grad_inner=shape((tok_dev, rank)),
            send=heads,
            base=shape((2 * D // WIDE, tok_dev, WIDE), f32),
        ),
        inside=dict(send=one),
        micros=0.1,
    )
    inner_qkv, grad_inner_out = made.inner, made.grad_inner
    made = staged(
        values_grads,
        dict(base=made.base, given=given_vg),
        dict(send=heads),
        raws=dict(send=made.send),
        inside=dict(send=one),
        alias=dict(send="send"),
        micros=3,
    )
    parts = n_ctx // HEADS
    near = None if parts == 1 else [[g * HEADS + i for i in range(HEADS)] for g in range(parts)]

    def exchange(a):
        return lax.all_to_all(a, "ctx", 0, 0, tiled=True, axis_index_groups=near)

    shared = staged(
        mlp_share,
        dict(h=h_mlp, grad=grad, low=low, mask_t=mask_t),
        dict(
            late=shape(up.late.shape),
            products=shape((rank, 2 * tok_dev)),
            first=shape((D // 8, D + W_CUT)),
            second=shape((D // 8, 3 * D - W_CUT)),
        ),
        raws=dict(late=up.late, qkv=qkv_weight, out=out_weight),
        inside=dict(late=(3 * rank, (HALF - 1) * CB)),
        alias=dict(late="late"),
        scratch=[pltpu.SemaphoreType.DMA((3,))],
    )

    def quarters(y, x, name, *after):
        return [y, x, to_core(tie(y, *after), name + "y"), to_core(tie(x, *after), name + "x")]

    u_y = to_y(table.up, "u")
    early_given = to_y(up.early, "early")
    u_x = to_x(tie(u_y, shared.products), "u")
    late_given = to_y(shared.late, "late")
    arrived = tie(exchange(made.send), u_y, early_given)
    if parts == 1 and ndoc == 1:
        done = attention_one_document(block_order, arrived)
    else:
        all_pos, all_doc, _, _ = stream_layout(
            block_order[0], doc_starts[0], jnp.arange(total_rows, dtype=jnp.int32), total_rows, half_dev
        )
        far = None if parts == 1 else [[g * HEADS + i for g in range(parts)] for i in range(HEADS)]
        done = attention_documents(arrived, all_pos, all_doc, far, ctx // HEADS * HEADS * tok_dev)
    back = exchange(tie(done.reshape(HEADS, tok_dev, 4 * HEAD_DIM), u_x, late_given))
    v_y = to_y(tie(shared.first, done), "v")
    middle = staged(
        mlp_middle,
        dict(
            kept=up.kept,
            early=tie(early_given, done),
            late=late_given,
            grad=grad,
            grad_given=grad_given,
            low=low,
            bias=bias,
            products=shared.products,
        ),
        dict(
            pack=shape((5 * rank + tok_dev, D)),
            small=shape((2, rank, tok_dev), f32),
            grads=shape((2 * HALF, rank, CB)),
            kept=shape((tok_dev, D), f32),
            rest=shape((tok_dev, D)),
            down=shape((tok_dev, D), f32),
        ),
        raws=dict(down=down_weight, up=up_weight, u=quarters(u_y, u_x, "u", done)),
        scratch=[
            pltpu.VMEM((HALF, CB, D), bf16),
            pltpu.VMEM((D, HALF * CB), bf16),
            pltpu.SemaphoreType.DMA((HALF,)),
            pltpu.SemaphoreType.DMA((5,)),
        ],
        micros=0.1,
    )
    pack_given = to_y(middle.pack, "pack")
    v_x = to_x(tie(v_y, middle.pack), "v")
    w_y = to_y(tie(shared.second, v_y, middle.pack), "w")
    rest_given = to_y(tie(middle.rest, pack_given), "rest")
    tail = staged(
        adapter_gradients,
        dict(
            arrived=back,
            tab=tab,
            low=low,
            mask=mask,
            h=h_attn,
            grad=grad,
            inner=inner_qkv,
            grad_inner=grad_inner_out,
        ),
        dict(
            att=shape((tok_dev, D)),
            gq=shape((tok_dev, 3 * D)),
            inner_out=shape((tok_dev, rank)),
            gi=shape((tok_dev, rank)),
            flat=shape((NB, rank, CB)),
        ),
        inside=dict(flat=(12, rank, CB)),
        parts=dict(flat=2),
        micros=0.1,
    )
    mlp = staged(
        mlp_finish,
        dict(
            small=middle.small,
            grads=middle.grads,
            pack=pack_given,
            kept=middle.kept,
            h=h_mlp,
            grad=grad,
            low=low,
            mask_t=mask_t,
        ),
        dict(inner_down=shape((rank, tok_dev)), back=shape((tok_dev, D), f32), flat=shape((NB, rank, CB))),
        raws=dict(flat=tail.flat),
        inside=dict(flat=(20, rank, CB)),
        alias=dict(flat="flat"),
        parts=dict(flat=2),
        micros=0.1,
    )
    flat = mlp.flat
    if columns != CB:
        flat = flat.reshape(NB, rank, CB // columns, columns).transpose(0, 2, 1, 3).reshape(n_dev, rank, columns)
    shares = lax.all_to_all(tie(flat, w_y), ("ctx", "wsh"), 0, 0, tiled=True)
    v_parts = quarters(v_y, v_x, "v", tail.att)
    w_x = to_x(tie(w_y, flat), "w")
    firsts = staged(
        first_outputs,
        dict(
            tok=tok,
            att=tail.att,
            gq=tail.gq,
            inner_out=tail.inner_out,
            gi=tail.gi,
            low=low,
            bias=bias,
            down=middle.down,
            inner_down=mlp.inner_down,
        ),
        dict(block=shape((tok_dev, D), f32), grad_h=shape((tok_dev, D), f32)),
        raws=dict(qkv=qkv_weight, out=out_weight, v=v_parts),
        scratch=[pltpu.VMEM((D, W_CUT), bf16), pltpu.VMEM((D, D), bf16), pltpu.SemaphoreType.DMA((10,))],
        micros=0.1,
    )
    ends = staged(
        last_outputs,
        dict(
            tok=tok,
            grad=grad,
            gain=norm_gains,
            gq=tail.gq,
            back=mlp.back,
            rest=rest_given,
            block=firsts.block,
            grad_h=firsts.grad_h,
        ),
        dict(block=shape((tok_dev, D)), tokens=shape((tok_dev, D), f32)),
        raws=dict(qkv=qkv_weight, w=quarters(w_y, w_x, "w", firsts.block, rest_given)),
        scratch=[pltpu.VMEM((D, 3 * D - W_CUT), bf16), pltpu.SemaphoreType.DMA((5,))],
        micros=0.1,
    )
    full = shape(adapters.shape, f32)
    new = staged(
        adamw,
        dict(adapters=adapters, first=first_moment, second=second_moment, parts=shares, given=adapters_given),
        dict(grad=full, new=full, first=full, second=full, low=shape(adapters.shape)),
        scalars=dict(chosen=doc_adapter),
        parts=dict(grad=ADAPTERS, new=ADAPTERS, first=ADAPTERS, second=ADAPTERS, low=ADAPTERS),
    )
    return (ends.block[None], ends.tokens[None], new.grad, new.new, new.first, new.second, new.low)


def solution(mesh):
    spread = P(None, None, ("ctx", "wsh"))
    rows = P("wsh", "ctx", None)
    half = P("wsh", None)
    in_specs = (rows, rows, P(), P(), half, half, half, half, P(), spread, spread, spread, half, P("wsh", None, None), half)
    out_specs = (rows, rows, spread, spread, spread, spread, spread)
    return jax.shard_map(on_device, mesh=mesh, in_specs=in_specs, out_specs=out_specs, check_vma=False)
```

```python
from types import SimpleNamespace

import jax
import jax.numpy as jnp
from jax import lax
from jax.experimental import pallas as pl
from jax.experimental.pallas import tpu as pltpu
from jax.sharding import PartitionSpec as P

D = 1024
HEADS = 16
FF = 4096
HEAD_DIM = 64
ROT = 16
ADAPTERS = 8
RANK = 16
STEP = 8
COLS = 8 * D + 2 * FF
CB = 512
NB = COLS // CB
WIDE = 512
W_CUT = 2048
HALF = FF // 2 // CB
QUERIES, KEYS = 512, 512

A_QKV, A_OUT, A_UP, A_DOWN = 0, 1, 2, 3
B_QKV, B_OUT, B_UP, B_DOWN = 7, 10, 11, 15

epsilon = 1e-05
adapter_scale = 8.0
rope_base = 10000.0
learn_rate = 0.02
beta_first = 0.5
beta_second = 0.5
weight_decay = 0.01
adam_epsilon = 1e-08
masked_value = -1e30

bf16 = jnp.bfloat16
f32 = jnp.float32

HBM = pl.BlockSpec(memory_space=pltpu.HBM)


def dot_nn(a, b):
    return jnp.dot(a, b, preferred_element_type=f32)


def dot_nt(a, b):
    return lax.dot_general(a, b, (((1,), (1,)), ((), ())), preferred_element_type=f32)


def dot_tn(a, b):
    return lax.dot_general(a, b, (((0,), (0,)), ((), ())), preferred_element_type=f32)


def shape(dims, dtype=bf16):
    return jax.ShapeDtypeStruct(tuple(dims), dtype)


def cut(index, width=D):
    return slice(index * width, (index + 1) * width)


class Stage:
    def __init__(self, loads, scalar, raw, out, targets):
        self.loads = loads
        self.scalar = scalar
        self.raw = raw
        self.out = out
        self.targets = targets
        self.waited = set()
        self.pending = []

    def __getattr__(self, name):
        buffer, copy = self.loads[name]
        if name not in self.waited:
            self.waited.add(name)
            copy.wait()
        return buffer

    def start(self, *ends):
        copy = pltpu.make_async_copy(*ends)
        copy.start()
        self.pending.append(copy)

    def store(self, buffer, at=None, into=None, sem=0):
        target, sems = self.targets[id(buffer)]
        if at is not None and into is None:
            into, sem = at, at
        source = buffer if at is None else buffer.at[at]
        self.start(source, target if into is None else target.at[into], sems.at[sem])


def staged(body, loads, results, raws=None, scalars=None, scratch=(), parts=None, micros=2, inside=None, alias=None):
    raws, scalars, parts, inside, alias = raws or {}, scalars or {}, parts or {}, inside or {}, alias or {}
    raw_list, raw_tree = jax.tree.flatten(raws)

    def kernel(*refs):
        refs = list(refs)

        def take(count):
            head = refs[:count]
            del refs[:count]
            return head

        scalar_from, load_from = take(len(scalars)), take(len(loads))
        raw = jax.tree.unflatten(raw_tree, take(len(raw_list)))
        targets = take(len(results))
        scalar_to, load_to, out = take(len(scalars)), take(len(loads)), take(len(results))
        (sems,) = take(1)
        out_sems = take(len(results))
        moves = [
            pltpu.make_async_copy(source, buffer, sems.at[i])
            for i, (source, buffer) in enumerate(zip(scalar_from + load_from, scalar_to + load_to))
        ]
        for move in moves:
            move.start()
        for move in moves[: len(scalars)]:
            move.wait()
        stage = Stage(
            dict(zip(loads, zip(load_to, moves[len(scalars) :]))),
            SimpleNamespace(**dict(zip(scalars, scalar_to))),
            SimpleNamespace(**raw),
            SimpleNamespace(**dict(zip(results, out))),
            {id(buffer): ends for buffer, ends in zip(out, zip(targets, out_sems))},
        )
        body(stage, *refs)
        for name in loads:
            getattr(stage, name)
        for copy in stage.pending:
            copy.wait()

    raw_names = list(raws)
    made = pl.pallas_call(
        kernel,
        out_shape=tuple(results.values()),
        in_specs=[HBM] * (len(scalars) + len(loads) + len(raw_list)),
        out_specs=(HBM,) * len(results),
        scratch_shapes=[pltpu.SMEM(a.shape, a.dtype) for a in scalars.values()]
        + [pltpu.VMEM(a.shape, a.dtype) for a in loads.values()]
        + [pltpu.VMEM(inside.get(n, s.shape), s.dtype) for n, s in results.items()]
        + [pltpu.SemaphoreType.DMA((len(loads) + len(scalars) + 1,))]
        + [pltpu.SemaphoreType.DMA((parts.get(n, 1),)) for n in results]
        + list(scratch),
        compiler_params=pltpu.CompilerParams(vmem_limit_bytes=64 * 1024 * 1024),
        input_output_aliases={
            len(scalars) + len(loads) + raw_names.index(a): list(results).index(b) for a, b in alias.items()
        },
        cost_estimate=pl.CostEstimate(flops=int(micros * 1.15e9), bytes_accessed=1024, transcendentals=0),
        name=body.__name__,
    )(*scalars.values(), *loads.values(), *raw_list)
    return SimpleNamespace(**dict(zip(results, made)))


def normalize(values):
    center = values - jnp.mean(values, axis=-1, keepdims=True)
    spread = jnp.mean(center * center, axis=-1, keepdims=True)
    scale = lax.rsqrt(spread + epsilon)
    return center * scale, scale


def give_adapters(stage):
    give = stage.out.give
    for a in range(ADAPTERS):
        give[cut(a, RANK), :] = stage.adapters[a].astype(bf16)
    row = lax.broadcasted_iota(jnp.int32, (RANK, give.shape[1]), 0)
    lane = lax.broadcasted_iota(jnp.int32, (RANK, give.shape[1]), 1)
    choice = jnp.zeros((RANK, give.shape[1]), f32)
    for j in range(stage.scalar.chosen.shape[1]):
        for a in range(ADAPTERS):
            choice = jnp.where((row == j) & (lane == a), stage.scalar.chosen[0, j, a].astype(f32), choice)
    give[ADAPTERS * RANK :, :] = choice.astype(bf16)
    stage.store(give)


def layer_norms(stage):
    out = stage.out
    normed, _ = normalize(stage.tok[...].astype(f32))
    gain, shift = stage.gain, stage.shift
    half = pl.multiple_of((1 - lax.axis_index("wsh")) * (D // 2), D // 2)
    for i, buffer in enumerate((out.attn, out.mlp)):
        buffer[...] = (normed * gain[i : i + 1, :] + shift[i : i + 1, :]).astype(bf16)
        out.give[:, cut(i, D // 2)] = buffer[:, pl.ds(half, D // 2)]
    stage.store(out.give)
    stage.store(out.attn)
    stage.store(out.mlp)


def tables(stage, sem):
    order, starts, out = stage.scalar.order, stage.scalar.starts, stage.out
    source = stage.raw.up
    copy = pltpu.make_async_copy(source.at[own_part(source, 4), hidden_columns(HALF)], out.up, sem)
    copy.start()
    rows, lanes = out.tab.shape[1:]
    ndoc = starts.shape[1]
    ctx = lax.axis_index("ctx")
    half = rows // 2

    def positions(dims, axis):
        index = lax.broadcasted_iota(jnp.int32, dims, axis)
        block = jnp.where(index < half, order[0, 2 * ctx], order[0, 2 * ctx + 1])
        return block * half + index % half

    pos = positions((rows, lanes), 0)
    start = jnp.zeros((rows, lanes), jnp.int32)
    for j in range(1, ndoc):
        start = jnp.where(pos >= starts[0, j], starts[0, j], start)
    lane = lax.broadcasted_iota(jnp.int32, (rows, lanes), 1) % HEAD_DIM
    frequency = jnp.ones((rows, lanes), f32)
    for i in range(1, ROT // 2):
        frequency = jnp.where(lane % (ROT // 2) == i, rope_base ** (-2.0 * i / ROT), frequency)
    angle = (pos - start).astype(f32) * frequency
    sine = jnp.sin(angle)
    out.tab[0] = jnp.where(lane < ROT, jnp.cos(angle), 1.0)
    out.tab[1] = jnp.where(lane < ROT // 2, -sine, 0.0)
    out.tab[2] = jnp.where((lane >= ROT // 2) & (lane < ROT), sine, 0.0)
    stage.store(out.tab)

    def used(dims, row_axis):
        pos = positions(dims, row_axis)
        doc = lax.broadcasted_iota(jnp.int32, dims, 1 - row_axis) // RANK
        held = jnp.zeros(dims, jnp.int32)
        for j in range(1, ndoc):
            held = jnp.where(pos >= starts[0, j], j, held)
        return (held == doc).astype(f32)

    out.mask[...] = used(out.mask.shape, 0)
    out.mask_t[...] = used(out.mask_t.shape, 1)
    stage.store(out.mask)
    stage.store(out.mask_t)
    copy.wait()
    stage.store(out.up)


def choose_adapters(stage):
    adapters, given = stage.adapters, stage.given
    rows = stage.out.rows
    target, sems = stage.targets[id(rows)]
    columns = adapters.shape[2]
    wsh = lax.axis_index("wsh")
    for j in range(rows.shape[0] // RANK):
        index = 0
        for a in range(1, ADAPTERS):
            index = index + a * stage.scalar.chosen[0, j, a]
        start = pl.multiple_of(index * RANK, RANK)
        own_at = pl.multiple_of(wsh * columns, 128)
        other_at = pl.multiple_of((1 - wsh) * columns, 128)
        rows[cut(j, RANK), pl.ds(own_at, columns)] = adapters[index].astype(bf16)
        rows[cut(j, RANK), pl.ds(other_at, columns)] = given[pl.ds(start, RANK), :]
    for i in range(target.shape[0]):
        stage.start(rows, target.at[i], sems.at[i])


def part_orders(share):
    ctx = lax.axis_index("ctx")
    if share == 2:
        return ctx % 2, 1 - ctx % 2
    mine = ctx % 2 * 2 + ctx // 2 % 2
    return mine, mine ^ 1, mine ^ 2, mine ^ 3


def rows_at(first, count):
    return pl.ds(pl.multiple_of(first, count), count)


def own_part(weight, share):
    rows = weight.shape[0] // share
    return rows_at(part_orders(share)[0] * rows, rows)


def place_weights(own, chunks, target, sems, first=0):
    half = own.shape[0]
    own_half = lax.axis_index("wsh")
    copies = [pltpu.make_async_copy(own, target.at[rows_at(own_half * half, half), :], sems.at[first])]
    for column, source_column, width, parts in chunks:
        rows = half // len(parts)
        for order, part in zip(part_orders(len(parts)), parts):
            copies.append(
                pltpu.make_async_copy(
                    part.at[:, source_column : source_column + width],
                    target.at[rows_at((1 - own_half) * half + order * rows, rows), column : column + width],
                    sems.at[first + len(copies)],
                )
            )
    for copy in copies:
        copy.start()
    return copies


def turn(values, tab, sign):
    left = pltpu.roll(values, 120, 1)
    right = pltpu.roll(values, 8, 1)
    return values * tab[0] + sign * (left * tab[1] + right * tab[2])


def swap_halves(first, second):
    low = lax.broadcasted_iota(jnp.int32, first.shape, 1) < HEAD_DIM
    one = jnp.where(low, first, pltpu.roll(second, HEAD_DIM, 1))
    two = jnp.where(low, pltpu.roll(first, HEAD_DIM, 1), second)
    return one, two


def both_streams(stage, side=0):
    half = pl.multiple_of(lax.axis_index("wsh") * (D // 2), D // 2)
    return jnp.concatenate([stage.h[:, pl.ds(half, D // 2)], stage.given[:, cut(side, D // 2)]], axis=0)


def weight_columns(source, first, weights, sems):
    copies = []
    for n in range(weights.shape[0]):
        copies.append(
            pltpu.make_async_copy(source.at[:, first + n * WIDE : first + (n + 1) * WIDE], weights.at[n], sems.at[n])
        )
        copies[-1].start()
    return copies


def partial_qk(stage, weights, sems):
    copies = weight_columns(stage.raw.qkv, 0, weights, sems)
    both = both_streams(stage)
    rows = both.shape[0] // 2
    for n, copy in enumerate(copies):
        copy.wait()
        part = dot_nn(both, weights[n])
        stage.out.give[:, cut(n, WIDE)] = part[rows:].astype(bf16)
        stage.out.kept[n] = part[:rows]
    stage.store(stage.out.give)
    stage.store(stage.out.kept)


def partial_vg(stage, weights, out_rows, sems):
    copies = weight_columns(stage.raw.qkv, 2 * D, weights, sems)
    out_copy = pltpu.make_async_copy(stage.raw.out, out_rows, sems.at[len(copies)])
    out_copy.start()
    both = both_streams(stage)
    rows = both.shape[0] // 2
    for n, copy in enumerate(copies):
        copy.wait()
        part = dot_nn(both, weights[n])
        stage.out.give[:, cut(n, WIDE)] = part[rows:].astype(bf16)
        stage.out.kept[n] = part[:rows]
    grads = jnp.concatenate([stage.grad[...], stage.grad_given[...]], axis=0)
    out_copy.wait()
    part = dot_nt(grads, out_rows[...])
    stage.out.give[:, D:] = part[rows:].astype(bf16)
    stage.store(stage.out.give)
    stage.out.kept[D // WIDE] = part[:rows]
    stage.store(stage.out.kept)


def queries_keys(stage):
    low, mask, bias, tab, kept, given = stage.low, stage.mask[...], stage.bias, stage.tab, stage.kept, stage.given
    inner = (dot_nt(stage.h[...], low[A_QKV]) * mask).astype(bf16)
    stage.out.inner[...] = inner
    stage.store(stage.out.inner)
    grad_inner = (adapter_scale * dot_nt(stage.grad[...], low[B_OUT]) * mask).astype(bf16)
    stage.out.grad_inner[...] = grad_inner
    stage.store(stage.out.grad_inner)
    steps = D // WIDE
    for n in range(steps):
        sides = []
        for kind in range(2):
            at = cut(kind * steps + n, WIDE)
            part = kept[kind * steps + n] + given[:, at].astype(f32) + bias[:, at]
            sides.append(part + adapter_scale * dot_nn(inner, low[B_QKV + kind][:, cut(n, WIDE)]))
        for pair in range(WIDE // 128):
            query = turn(sides[0][:, cut(pair, 128)], tab, 1.0) * HEAD_DIM**-0.5
            key = turn(sides[1][:, cut(pair, 128)], tab, 1.0)
            head = n * WIDE // HEAD_DIM + 2 * pair
            for i, both in enumerate(swap_halves(query, key)):
                stage.out.send[head + i] = both.astype(bf16)
    stage.store(stage.out.send, into=(slice(None), 0))
    base, kept, wsh = stage.out.base, stage.kept_vg, lax.axis_index("wsh")
    for n in range(steps):
        base[n] = kept[n] + bias[:, 2 * D + n * WIDE : 2 * D + (n + 1) * WIDE]
        base[n] += adapter_scale * dot_nn(inner, low[B_QKV + 2][:, cut(n, WIDE)])
        base[steps + n] = jnp.where(wsh == n, kept[steps], 0.0) + dot_nn(grad_inner, low[A_OUT][:, cut(n, WIDE)])
    stage.store(base)


def values_grads(stage):
    base, given = stage.base, stage.given
    steps = D // WIDE
    wsh = lax.axis_index("wsh")
    for n in range(steps):
        value = base[n] + given[:, cut(n, WIDE)].astype(f32)
        grad = base[steps + n] + jnp.where(wsh == n, 0.0, given[:, D:].astype(f32))
        for pair in range(WIDE // 128):
            head = n * WIDE // HEAD_DIM + 2 * pair
            for i, both in enumerate(swap_halves(value[:, cut(pair, 128)], grad[:, cut(pair, 128)])):
                stage.out.send[head + i] = both.astype(bf16)
    stage.store(stage.out.send, into=(slice(None), 1))


def attention(stage, xt, dks, dvs, ks, vs, aq, s_scr, e_scr):
    order = stage.scalar.order
    rows = aq.shape[0]
    blocks = order.shape[1]
    half = rows // blocks
    hd = HEAD_DIM
    x = stage.arrived
    per = x.shape[2] // half
    for i in range(blocks):
        start = pl.multiple_of(order[0, i] * half, half)
        for side in range(2):
            aq[pl.ds(start, half), cut(side, 2 * hd)] = x[i // per, side, cut(i % per, half), :]
    for t in range(rows // KEYS):
        part = aq[cut(t, KEYS), :]
        ks[cut(t, KEYS), :] = part[:, hd : 2 * hd]
        vs[cut(t, KEYS), :] = part[:, 2 * hd : 3 * hd]
        xt[:, cut(t, KEYS)] = part.T
    dks[...] = jnp.zeros_like(dks)
    dvs[...] = jnp.zeros_like(dvs)
    later = lax.broadcasted_iota(jnp.int32, (KEYS, QUERIES), 0) - lax.broadcasted_iota(jnp.int32, (KEYS, QUERIES), 1)
    for b in range(rows // QUERIES):
        at = cut(b, QUERIES)
        q_t = xt[0:hd, at]
        g_t = xt[3 * hd : 4 * hd, at]
        tiles = [(cut(t, KEYS), b * QUERIES - t * KEYS) for t in range(-(-(b + 1) * QUERIES // KEYS))]
        top = jnp.full((8, QUERIES), masked_value, f32)
        for part, ahead in tiles:
            s = dot_nn(ks[part, :], q_t)
            if ahead < KEYS - 1:
                s = jnp.where(later <= ahead, s, masked_value)
            s_scr[part, :] = s
            top = jnp.maximum(top, jnp.max(s.reshape(KEYS // 8, 8, QUERIES), axis=0))
        top = jnp.max(top, axis=0, keepdims=True)
        total = jnp.zeros((8, QUERIES), f32)
        att = jnp.zeros((hd, QUERIES), f32)
        for part, _ in tiles:
            e = jnp.exp(s_scr[part, :] - top)
            total = total + jnp.sum(e.reshape(KEYS // 8, 8, QUERIES), axis=0)
            e = e.astype(bf16)
            e_scr[part, :] = e
            att = att + dot_nn(xt[2 * hd : 3 * hd, part], e)
        inverse = 1.0 / jnp.sum(total, axis=0, keepdims=True)
        att = att * inverse
        g_f = g_t.astype(f32)
        delta = jnp.sum(g_f * att, axis=0, keepdims=True) * inverse
        g_n = (g_f * inverse).astype(bf16)
        dq = jnp.zeros((hd, QUERIES), f32)
        for part, _ in tiles:
            e = e_scr[part, :]
            dp = dot_nn(vs[part, :], g_n)
            ds = (e.astype(f32) * (dp - delta)).astype(bf16)
            dq = dq + dot_nn(xt[hd : 2 * hd, part], ds)
            dks[part, :] += dot_nt(ds, q_t)
            dvs[part, :] += dot_nt(e, g_n)
        both = jnp.concatenate([att, dq * hd**-0.5], axis=0)
        aq[at, 0 : 2 * hd] = both.T.astype(bf16)
    for t in range(rows // KEYS):
        aq[cut(t, KEYS), 2 * hd : 3 * hd] = dks[cut(t, KEYS), :].astype(bf16)
        aq[cut(t, KEYS), 3 * hd :] = dvs[cut(t, KEYS), :].astype(bf16)
    for i in range(blocks):
        start = pl.multiple_of(order[0, i] * half, half)
        stage.out.back[cut(i, half), :] = aq[pl.ds(start, half), :]
    stage.store(stage.out.back)


def attention_one_document(order, arrived):
    rows = arrived.shape[0] * arrived.shape[2]
    hd = HEAD_DIM
    return staged(
        attention,
        dict(arrived=arrived),
        dict(back=shape((rows, 4 * hd))),
        scalars=dict(order=order),
        scratch=[
            pltpu.VMEM((4 * hd, rows), bf16),
            pltpu.VMEM((rows, hd), f32),
            pltpu.VMEM((rows, hd), f32),
            pltpu.VMEM((rows, hd), bf16),
            pltpu.VMEM((rows, hd), bf16),
            pltpu.VMEM((rows, 4 * hd), bf16),
            pltpu.VMEM((rows, QUERIES), f32),
            pltpu.VMEM((rows, QUERIES), bf16),
        ],
        micros=17,
    ).back


def attention_documents(arrived, pos, doc, groups, first_row):
    rows = arrived.shape[0] * arrived.shape[2]
    hd = HEAD_DIM
    qk, vg = (arrived[:, side].reshape(rows, 2 * hd) for side in range(2))
    q, k, v, g = qk[:, :hd], qk[:, hd:], vg[:, :hd], vg[:, hd:]
    if groups is not None:
        both = lax.all_gather(jnp.concatenate([k, v], 1), "ctx", axis=0, tiled=True, axis_index_groups=groups)
        k, v = both[:, :hd], both[:, hd:]
    step = 512
    my_pos = lax.dynamic_slice_in_dim(pos, first_row, rows)
    my_doc = lax.dynamic_slice_in_dim(doc, first_row, rows)

    def one(sums, item):
        q_b, g_b, pos_b, doc_b = item
        scores = dot_nt(q_b, k)
        allowed = (doc_b[:, None] == doc[None, :]) & (pos[None, :] <= pos_b[:, None])
        scores = jnp.where(allowed, scores, masked_value)
        top = jnp.max(scores, axis=1, keepdims=True)
        weights = jnp.exp(scores - top)
        weights = weights / jnp.sum(weights, axis=1, keepdims=True)
        weights_low = weights.astype(bf16)
        att = dot_nn(weights_low, v)
        delta = jnp.sum(g_b.astype(f32) * att, axis=1, keepdims=True)
        ds = (weights * (dot_nt(g_b, v) - delta)).astype(bf16)
        dq = dot_nn(ds, k) * hd**-0.5
        sums = (sums[0] + dot_tn(ds, q_b), sums[1] + dot_tn(weights_low, g_b))
        return sums, jnp.concatenate([att, dq], 1).astype(bf16)

    zero = jnp.zeros((k.shape[0], hd), f32)
    split = lambda a: a.reshape((rows // step, step) + a.shape[1:])
    sums, att_dq = lax.scan(one, (zero, zero), tuple(map(split, (q, g, my_pos, my_doc))))
    sums = jnp.concatenate(sums, 1)
    if groups is not None:
        sums = lax.psum_scatter(sums, "ctx", scatter_dimension=0, tiled=True, axis_index_groups=groups)
    return jnp.concatenate([att_dq.reshape(rows, 2 * hd), sums.astype(bf16)], axis=1)


def swapped(rows):
    half = rows.shape[0] // 2
    return jnp.concatenate([rows[half:], rows[:half]], axis=0)


def hidden_block(j):
    wsh = lax.axis_index("wsh")
    return (wsh if j < HALF else 1 - wsh) * HALF + j % HALF


def hidden_columns(j):
    return pl.ds(pl.multiple_of(hidden_block(j // HALF * HALF) * CB, HALF * CB), HALF * CB)


def up_blocks(source, weights, sems, order):
    copies = {}
    for j in order:
        first = pl.multiple_of(hidden_block(j) * CB, CB)
        copies[j] = pltpu.make_async_copy(source.at[:, pl.ds(first, CB)], weights.at[j], sems.at[j])
        copies[j].start()
    return copies


def adapter_block(low, first, j):
    return low[first + hidden_block(j) // 2, :, cut(j % 2, CB)]


def mlp_up(stage, weights, sems):
    out = stage.out
    order = [*range(HALF, 2 * HALF), *range(HALF)]
    copies = up_blocks(stage.raw.up, weights, sems, order)
    both = both_streams(stage, 1)
    for j in order:
        copies[j].wait()
        part = dot_nn(both, weights[j])
        if j < HALF:
            out.kept[j] = part
        elif j == HALF:
            out.early[...] = part.astype(bf16)
            stage.store(out.early)
        else:
            out.late[:, cut(j - HALF - 1, CB)] = part.astype(bf16)
            if j == 2 * HALF - 1:
                stage.store(out.late)
    stage.store(out.kept)


def share_at(kind, j, rank):
    down, right = divmod(kind * HALF + j, HALF - 1)
    return cut(down, rank), cut(right, CB)


def mlp_share(stage, sems):
    out = stage.out
    qkv, weight = stage.raw.qkv, stage.raw.out
    mine = own_part(qkv, 4)
    copies = [
        pltpu.make_async_copy(weight.at[mine, :], out.first.at[:, :D], sems.at[0]),
        pltpu.make_async_copy(qkv.at[mine, :W_CUT], out.first.at[:, D:], sems.at[1]),
        pltpu.make_async_copy(qkv.at[mine, W_CUT:], out.second, sems.at[2]),
    ]
    for copy in copies:
        copy.start()
    share, low, mask = out.share, stage.low, stage.mask_t[...]
    rank, rows = mask.shape
    for j in range(HALF):
        share[share_at(0, j, rank)] = adapter_block(low, A_DOWN, HALF + j)
        share[share_at(1, j, rank)] = adapter_block(low, B_UP, HALF + j)
    inner = (dot_nt(low[A_UP], stage.h[...]) * mask).astype(bf16)
    back = (adapter_scale * dot_nt(low[B_DOWN], stage.grad[...]) * mask).astype(bf16)
    zero = jnp.zeros((rank, CB - 2 * rows), bf16)
    share[share_at(2, 0, rank)] = jnp.concatenate([inner, back, zero], axis=1)
    stage.store(share)
    out.products[...] = jnp.concatenate([inner, back], axis=1)
    stage.store(out.products)
    for copy in copies:
        copy.wait()
    for buffer in (out.first, out.second):
        stage.store(buffer)


def diagonal(one, two):
    zero = jnp.zeros_like(one)
    return jnp.concatenate([jnp.concatenate([one, zero], axis=1), jnp.concatenate([zero, two], axis=1)], axis=0)


def mlp_middle(stage, down_rows, up_rows, down_sems, up_sems):
    out, low = stage.out, stage.low
    copies = []
    for j in range(HALF):
        copies.append(pltpu.make_async_copy(stage.raw.down.at[cut(j, CB), :], down_rows.at[j], down_sems.at[j]))
        copies[-1].start()
    up_copies = place_weights(
        stage.raw.up.at[:, hidden_columns(0)], [(0, 0, HALF * CB, stage.raw.u)], up_rows, up_sems, 0
    )
    grads = jnp.concatenate([stage.grad[...], stage.grad_given[...]], axis=0)
    rows = grads.shape[0] // 2
    products, given = stage.products[...], stage.given
    rank = products.shape[0]
    other = given[share_at(2, 0, rank)]
    inner, back = (diagonal(products[:, cut(i, rows)], other[:, cut(i, rows)]) for i in range(2))
    sums = None
    grad_ups = []
    for j in range(HALF):
        at = cut(j, CB)
        a_both = jnp.concatenate([adapter_block(low, A_DOWN, j), given[share_at(0, j, rank)]], axis=0)
        b_both = jnp.concatenate([adapter_block(low, B_UP, j), given[share_at(1, j, rank)]], axis=0)
        part = stage.early[...] if j == 0 else stage.late[:, cut(j - 1, CB)]
        shift = pl.multiple_of(4 * D + hidden_block(j) * CB, CB)
        up = stage.kept[j] + swapped(part.astype(f32)) + stage.bias[:, pl.ds(shift, CB)]
        up = up + adapter_scale * dot_tn(inner, b_both)
        spread = 0.5 * (1.0 + lax.erf(up * (0.5**0.5)))
        hidden = (up * spread).astype(bf16)
        slope = spread + up * (jnp.exp(-0.5 * up * up) * (0.5 / jnp.pi) ** 0.5)
        copies[j].wait()
        down = down_rows[j]
        grad_hidden = dot_nt(grads, down) + dot_tn(back, a_both)
        grad_up = (grad_hidden * slope).astype(bf16)
        grad_ups.append(grad_up)
        parts = dot_nn(hidden, down), dot_nt(a_both, hidden), dot_nt(b_both, grad_up)
        sums = parts if sums is None else tuple(one + two for one, two in zip(sums, parts))
        a_grad = dot_nn(back, hidden).astype(bf16)
        b_grad = (adapter_scale * dot_nn(inner, grad_up)).astype(bf16)
        out.grads[j], out.grads[HALF + j] = a_grad[:rank], b_grad[:rank]
        out.pack[pack_at(0, j, rank)], out.pack[pack_at(1, j, rank)] = a_grad[rank:], b_grad[rank:]
    down, inner_down, gi_up = sums
    out.small[0], out.small[1] = inner_down[:rank, :rows], gi_up[:rank, :rows]
    out.pack[4 * rank : 5 * rank, :] = jnp.zeros((rank, D), bf16)
    out.pack[4 * rank : 5 * rank, 0:rows] = inner_down[rank:, rows:].astype(bf16)
    out.pack[4 * rank : 5 * rank, rows : 2 * rows] = gi_up[rank:, rows:].astype(bf16)
    for copy in up_copies:
        copy.wait()
    total = None
    for j in range(HALF):
        part = dot_nt(grad_ups[j], up_rows[:, cut(j, CB)])
        total = part if total is None else total + part
    out.pack[5 * rank :, :] = total[rows:].astype(bf16)
    stage.store(out.pack)
    out.kept[...] = total[:rows]
    out.rest[...] = down[rows:].astype(bf16)
    out.down[...] = down[:rows]
    for buffer in (out.small, out.grads, out.kept, out.rest, out.down):
        stage.store(buffer)


def pack_at(kind, j, rank):
    return pl.ds((2 * kind + j // 2) * rank, rank), cut(j % 2, CB)


def mlp_finish(stage):
    out, low, mask = stage.out, stage.low, stage.mask_t[...]
    rank, rows = mask.shape
    pack, small, wsh = stage.pack, stage.small, lax.axis_index("wsh")
    extra = pack[4 * rank : 5 * rank, :].astype(f32)
    inner_down = ((small[0] + extra[:, 0:rows]) * mask).astype(bf16)
    gi_up = (adapter_scale * (small[1] + extra[:, rows : 2 * rows]) * mask).astype(bf16)
    for j in range(HALF):
        for kind in range(2):
            out.flat[2 + kind * 2 * HALF + wsh * HALF + j] = stage.grads[kind * HALF + j]
            out.flat[2 + kind * 2 * HALF + (1 - wsh) * HALF + j] = pack[pack_at(kind, j, rank)]
    up_grad = dot_nn(gi_up, stage.h[...])
    down_grad = adapter_scale * dot_nn(inner_down, stage.grad[...])
    for i in range(2):
        out.flat[i] = up_grad[:, cut(i, CB)].astype(bf16)
        out.flat[18 + i] = down_grad[:, cut(i, CB)].astype(bf16)
    per = D // CB
    stage.store(out.flat, at=pl.ds(0, 10), into=pl.ds(A_UP * per, 10), sem=0)
    stage.store(out.flat, at=pl.ds(10, 10), into=pl.ds(B_UP * per, 10), sem=1)
    out.inner_down[...] = inner_down
    stage.store(out.inner_down)
    out.back[...] = stage.kept[...] + pack[5 * rank :, :].astype(f32) + dot_tn(gi_up, low[A_UP])
    stage.store(out.back)


def adapter_gradients(stage):
    arrived, tab = stage.arrived, stage.tab
    att, gq, flat = stage.out.att, stage.out.gq, stage.out.flat
    for pair in range(HEADS // 2):
        at = cut(pair, 128)
        one, two = arrived[2 * pair].astype(f32), arrived[2 * pair + 1].astype(f32)
        attended, query = swap_halves(one[:, :128], two[:, :128])
        key, value = swap_halves(one[:, 128:], two[:, 128:])
        att[:, at] = attended.astype(bf16)
        for kind, part in enumerate((turn(query, tab, -1.0), turn(key, tab, -1.0), value)):
            gq[:, kind * D + pair * 128 : kind * D + (pair + 1) * 128] = part.astype(bf16)
    stage.store(att)
    stage.store(gq)
    low, mask, h, grad = stage.low, stage.mask[...], stage.h, stage.grad
    inner_out = (dot_nt(att[...], low[A_OUT]) * mask).astype(bf16)
    stage.out.inner_out[...] = inner_out
    stage.store(stage.out.inner_out)
    gi = sum(dot_nt(gq[:, cut(i)], low[B_QKV + i]) for i in range(3))
    gi = (adapter_scale * gi * mask).astype(bf16)
    stage.out.gi[...] = gi
    stage.store(stage.out.gi)
    per = D // CB

    def put(block, value):
        place = block if block < A_UP else block - B_QKV + A_UP
        for i in range(per):
            flat[place * per + i] = value[:, cut(i, CB)].astype(bf16)

    put(A_QKV, dot_tn(gi, h[...]))
    put(A_OUT, dot_tn(stage.grad_inner[...], att[...]))
    put(B_OUT, adapter_scale * dot_tn(inner_out, grad[...]))
    for i in range(3):
        put(B_QKV + i, adapter_scale * dot_tn(stage.inner[...], gq[:, cut(i)]))
    first, rest = A_UP * per, (B_UP - B_QKV) * per
    stage.store(flat, at=pl.ds(0, first), into=pl.ds(0, first), sem=0)
    stage.store(flat, at=pl.ds(first, rest), into=pl.ds(B_QKV * per, rest), sem=1)


def first_outputs(stage, wq, wo, sems):
    raw, low, bias = stage.raw, stage.low, stage.bias
    o_copies = place_weights(raw.out, [(0, 0, D, raw.v)], wo, sems)
    q_copies = place_weights(raw.qkv.at[:, :W_CUT], [(0, D, W_CUT, raw.v)], wq, sems, 5)
    att, inner_out, inner_down = stage.att[...], stage.inner_out[...], stage.inner_down[...]
    for copy in o_copies:
        copy.wait()
    for n in range(D // WIDE):
        at = cut(n, WIDE)
        shift = n * WIDE
        part = dot_nn(att, wo[:, at]) + bias[:, 3 * D + shift : 3 * D + shift + WIDE]
        part = part + adapter_scale * dot_nn(inner_out, low[B_OUT][:, at])
        mlp = stage.down[:, at] + bias[:, 4 * D + FF + shift : 4 * D + FF + shift + WIDE]
        mlp = mlp + adapter_scale * dot_tn(inner_down, low[B_DOWN][:, at])
        stage.out.block[:, at] = part + stage.tok[:, at].astype(f32) + mlp
    stage.store(stage.out.block)
    for copy in q_copies:
        copy.wait()
    stage.out.grad_h[...] = dot_nt(stage.gq[:, :W_CUT], wq[...]) + dot_nn(stage.gi[...], low[A_QKV])
    stage.store(stage.out.grad_h)


def last_outputs(stage, wq, sems):
    raw, gain, out = stage.raw, stage.gain, stage.out
    copies = place_weights(raw.qkv.at[:, W_CUT:], [(0, 0, 3 * D - W_CUT, raw.w)], wq, sems)
    normed, scale = normalize(stage.tok[...].astype(f32))
    out.block[...] = (stage.block[...] + stage.rest[...].astype(f32)).astype(bf16)
    stage.store(out.block)
    for copy in copies:
        copy.wait()
    grad_h = stage.grad_h[...] + dot_nt(stage.gq[:, W_CUT:], wq[...])
    grad_n = grad_h * gain[0:1, :] + stage.back[...] * gain[1:2, :]
    grad_v = grad_n - jnp.mean(grad_n, axis=-1, keepdims=True) - normed * jnp.mean(grad_n * normed, axis=-1, keepdims=True)
    out.tokens[...] = stage.grad[...].astype(f32) + scale * grad_v
    stage.store(out.tokens)


def adamw(stage):
    chosen, parts, out = stage.scalar.chosen, stage.parts, stage.out
    given, wsh = stage.given, lax.axis_index("wsh")
    sums = []
    for stream in range(2):
        total = parts[stream].astype(f32)
        for source in range(stream + 2, parts.shape[0], 2):
            total = total + parts[source].astype(f32)
        sums.append(total)
    ndoc = sums[0].shape[0] // RANK
    for a in range(ADAPTERS):
        grad = None
        for stream in range(2):
            for j in range(ndoc):
                own = chosen[0, j, a].astype(f32)
                other = given[ADAPTERS * RANK + j : ADAPTERS * RANK + j + 1, a : a + 1].astype(f32)
                term = jnp.where(wsh == stream, own, other) * sums[stream][cut(j, RANK), :]
                grad = term if grad is None else grad + term
        new_first = beta_first * stage.first[a] + (1.0 - beta_first) * grad
        new_second = beta_second * stage.second[a] + (1.0 - beta_second) * grad * grad
        first_hat = new_first / (1.0 - beta_first**STEP)
        second_hat = new_second / (1.0 - beta_second**STEP)
        old = stage.adapters[a]
        new = old - learn_rate * (first_hat / (jnp.sqrt(second_hat) + adam_epsilon) + weight_decay * old)
        for buffer, value in (
            (out.grad, grad),
            (out.new, new),
            (out.first, new_first),
            (out.second, new_second),
            (out.low, new.astype(bf16)),
        ):
            buffer[a] = value
            stage.store(buffer, a)


def stream_layout(order_row, starts_row, rows, total_rows, half_dev):
    slot = rows // half_dev
    picked = (slot[:, None] == jnp.arange(order_row.shape[0], dtype=jnp.int32)[None, :]).astype(jnp.int32)
    pos = jnp.sum(picked * order_row[None, :], axis=1) * half_dev + rows % half_dev
    finish = jnp.concatenate([starts_row[1:], jnp.full((1,), total_rows, jnp.int32)])
    inside = ((pos[:, None] >= starts_row[None, :]) & (pos[:, None] < finish[None, :])).astype(jnp.int32)
    doc = jnp.sum(inside * jnp.arange(starts_row.shape[0], dtype=jnp.int32)[None, :], axis=1)
    place = pos - jnp.sum(inside * starts_row[None, :], axis=1)
    return pos, doc, place, inside


def tie(first, *others):
    return lax.optimization_barrier((first,) + others)[0]


def on_device(
    tokens,
    out_cotangent,
    norm_gains,
    norm_biases,
    qkv_weight,
    out_weight,
    up_weight,
    down_weight,
    proj_biases,
    adapters,
    first_moment,
    second_moment,
    doc_starts,
    doc_adapter,
    block_order,
):
    n_ctx = lax.axis_size("ctx")
    n_dev = n_ctx * lax.axis_size("wsh")
    ctx = lax.axis_index("ctx")
    wsh = lax.axis_index("wsh")
    tok_dev = tokens.shape[1]
    half_dev = tok_dev // 2
    total_rows = tok_dev * n_ctx
    ndoc = doc_starts.shape[1]
    rank = ndoc * RANK
    columns = adapters.shape[2]
    tok, grad = tokens[0], out_cotangent[0]
    bias = proj_biases[None, :]

    def to_y(a, name):
        with jax.named_scope("y_" + name):
            return lax.ppermute(a, "wsh", [(0, 1), (1, 0)])

    def to_x(a, name):
        with jax.named_scope("x_" + name):
            return lax.ppermute(a, "ctx", [(i, i ^ 2) for i in range(n_ctx)])

    def to_core(a, name):
        with jax.named_scope("c_" + name):
            return lax.ppermute(a, "ctx", [(i, i ^ 1) for i in range(n_ctx)])

    give = staged(
        give_adapters,
        dict(adapters=adapters),
        dict(give=shape(((ADAPTERS + 1) * RANK, columns))),
        scalars=dict(chosen=doc_adapter),
    ).give
    adapters_given = to_y(give, "adapters")
    normed = staged(
        layer_norms,
        dict(tok=tie(tok, give), gain=norm_gains, shift=norm_biases),
        dict(attn=shape(tok.shape), mlp=shape(tok.shape), give=shape((tok_dev, D))),
    )
    h_attn, h_mlp = normed.attn, normed.mlp
    given = to_y(normed.give, "h")
    grad_given = to_y(tie(grad, normed.give), "grad")
    chosen_rows = staged(
        choose_adapters,
        dict(adapters=adapters, given=tie(adapters_given, h_attn)),
        dict(rows=shape((n_ctx, rank, 2 * columns))),
        scalars=dict(chosen=doc_adapter),
        parts=dict(rows=n_ctx),
        inside=dict(rows=(rank, 2 * columns)),
    ).rows
    low = lax.all_to_all(chosen_rows, "ctx", 0, 0, tiled=True)
    if n_ctx != HEADS:
        low = low.reshape(COLS // D, n_ctx // HEADS, rank, 2 * columns).transpose(0, 2, 1, 3).reshape(COLS // D, rank, D)

    both = staged(
        partial_qk,
        dict(h=h_attn, given=tie(given, chosen_rows)),
        dict(give=shape((tok_dev, 2 * D)), kept=shape((2 * D // WIDE, tok_dev, WIDE), f32)),
        raws=dict(qkv=qkv_weight),
        scratch=[pltpu.VMEM((2 * D // WIDE, D // 2, WIDE), bf16), pltpu.SemaphoreType.DMA((2 * D // WIDE,))],
        micros=3,
    )
    kept_qk, give_qk = both.kept, both.give
    given_qk = to_y(give_qk, "qk")
    both = staged(
        partial_vg,
        dict(h=tie(h_attn, give_qk), given=given, grad=grad, grad_given=grad_given),
        dict(give=shape((tok_dev, 3 * D // 2)), kept=shape((D // WIDE + 1, tok_dev, WIDE), f32)),
        raws=dict(qkv=qkv_weight, out=out_weight),
        scratch=[
            pltpu.VMEM((D // WIDE, D // 2, WIDE), bf16),
            pltpu.VMEM((D // 2, D), bf16),
            pltpu.SemaphoreType.DMA((D // WIDE + 1,)),
        ],
        micros=3,
    )
    given_vg = to_y(both.give, "vg")
    table = staged(
        tables,
        {},
        dict(tab=shape((3, tok_dev, 128), f32), mask=shape((tok_dev, rank), f32), mask_t=shape((rank, tok_dev), f32), up=shape((D // 8, HALF * CB))),
        raws=dict(up=up_weight),
        scalars=dict(order=tie(block_order, both.give), starts=doc_starts),
        scratch=[pltpu.SemaphoreType.DMA],
        micros=0.1,
    )
    tab, mask, mask_t = table.tab, table.mask, table.mask_t
    up = staged(
        mlp_up,
        dict(h=tie(h_mlp, both.give), given=given),
        dict(
            early=shape((2 * tok_dev, CB)),
            late=shape((2 * tok_dev, (HALF - 1) * CB)),
            kept=shape((HALF, 2 * tok_dev, CB), f32),
        ),
        raws=dict(up=up_weight),
        scratch=[pltpu.VMEM((2 * HALF, D // 2, CB), bf16), pltpu.SemaphoreType.DMA((2 * HALF,))],
        micros=0.1,
    )
    heads = shape((HEADS, 2, tok_dev, 2 * HEAD_DIM))
    one = (HEADS, tok_dev, 2 * HEAD_DIM)
    made = staged(
        queries_keys,
        dict(
            h=tie(h_attn, up.kept),
            grad=grad,
            low=low,
            mask=mask,
            bias=bias,
            tab=tab,
            kept=kept_qk,
            given=given_qk,
            kept_vg=both.kept,
        ),
        dict(
            inner=shape((tok_dev, rank)),
            grad_inner=shape((tok_dev, rank)),
            send=heads,
            base=shape((2 * D // WIDE, tok_dev, WIDE), f32),
        ),
        inside=dict(send=one),
        micros=0.1,
    )
    inner_qkv, grad_inner_out = made.inner, made.grad_inner
    made = staged(
        values_grads,
        dict(base=made.base, given=given_vg),
        dict(send=heads),
        raws=dict(send=made.send),
        inside=dict(send=one),
        alias=dict(send="send"),
        micros=3,
    )
    parts = n_ctx // HEADS
    near = None if parts == 1 else [[g * HEADS + i for i in range(HEADS)] for g in range(parts)]

    def exchange(a):
        return lax.all_to_all(a, "ctx", 0, 0, tiled=True, axis_index_groups=near)

    shared = staged(
        mlp_share,
        dict(h=h_mlp, grad=grad, low=low, mask_t=mask_t),
        dict(
            share=shape((3 * rank, (HALF - 1) * CB)),
            products=shape((rank, 2 * tok_dev)),
            first=shape((D // 8, D + W_CUT)),
            second=shape((D // 8, 3 * D - W_CUT)),
        ),
        raws=dict(qkv=qkv_weight, out=out_weight),
        scratch=[pltpu.SemaphoreType.DMA((3,))],
    )

    def quarters(y, x, name, *after):
        return [y, x, to_core(tie(y, *after), name + "y"), to_core(tie(x, *after), name + "x")]

    u_y = to_y(table.up, "u")
    early_given = to_y(up.early, "early")
    u_x = to_x(tie(u_y, shared.products), "u")
    late_given = to_y(up.late, "late")
    share_given = to_y(shared.share, "share")
    arrived = tie(exchange(tie(made.send, early_given)), u_y)
    if parts == 1 and ndoc == 1:
        done = attention_one_document(block_order, arrived)
    else:
        all_pos, all_doc, _, _ = stream_layout(
            block_order[0], doc_starts[0], jnp.arange(total_rows, dtype=jnp.int32), total_rows, half_dev
        )
        far = None if parts == 1 else [[g * HEADS + i for g in range(parts)] for i in range(HEADS)]
        done = attention_documents(arrived, all_pos, all_doc, far, ctx // HEADS * HEADS * tok_dev)
    back = exchange(tie(done.reshape(HEADS, tok_dev, 4 * HEAD_DIM), u_x, late_given, share_given))
    v_y = to_y(tie(shared.first, done), "v")
    middle = staged(
        mlp_middle,
        dict(
            kept=up.kept,
            early=tie(early_given, done),
            late=late_given,
            given=share_given,
            grad=grad,
            grad_given=grad_given,
            low=low,
            bias=bias,
            products=shared.products,
        ),
        dict(
            pack=shape((5 * rank + tok_dev, D)),
            small=shape((2, rank, tok_dev), f32),
            grads=shape((2 * HALF, rank, CB)),
            kept=shape((tok_dev, D), f32),
            rest=shape((tok_dev, D)),
            down=shape((tok_dev, D), f32),
        ),
        raws=dict(down=down_weight, up=up_weight, u=quarters(u_y, u_x, "u", done)),
        scratch=[
            pltpu.VMEM((HALF, CB, D), bf16),
            pltpu.VMEM((D, HALF * CB), bf16),
            pltpu.SemaphoreType.DMA((HALF,)),
            pltpu.SemaphoreType.DMA((5,)),
        ],
        micros=0.1,
    )
    pack_given = to_y(middle.pack, "pack")
    v_x = to_x(tie(v_y, middle.pack), "v")
    w_y = to_y(tie(shared.second, v_y, middle.pack), "w")
    rest_given = to_y(tie(middle.rest, pack_given), "rest")
    tail = staged(
        adapter_gradients,
        dict(
            arrived=back,
            tab=tab,
            low=low,
            mask=mask,
            h=h_attn,
            grad=grad,
            inner=inner_qkv,
            grad_inner=grad_inner_out,
        ),
        dict(
            att=shape((tok_dev, D)),
            gq=shape((tok_dev, 3 * D)),
            inner_out=shape((tok_dev, rank)),
            gi=shape((tok_dev, rank)),
            flat=shape((NB, rank, CB)),
        ),
        inside=dict(flat=(12, rank, CB)),
        parts=dict(flat=2),
        micros=0.1,
    )
    mlp = staged(
        mlp_finish,
        dict(
            small=middle.small,
            grads=middle.grads,
            pack=pack_given,
            kept=middle.kept,
            h=h_mlp,
            grad=grad,
            low=low,
            mask_t=mask_t,
        ),
        dict(inner_down=shape((rank, tok_dev)), back=shape((tok_dev, D), f32), flat=shape((NB, rank, CB))),
        raws=dict(flat=tail.flat),
        inside=dict(flat=(20, rank, CB)),
        alias=dict(flat="flat"),
        parts=dict(flat=2),
        micros=0.1,
    )
    flat = mlp.flat
    if columns != CB:
        flat = flat.reshape(NB, rank, CB // columns, columns).transpose(0, 2, 1, 3).reshape(n_dev, rank, columns)
    shares = lax.all_to_all(tie(flat, w_y), ("ctx", "wsh"), 0, 0, tiled=True)
    v_parts = quarters(v_y, v_x, "v", tail.att)
    w_x = to_x(tie(w_y, flat), "w")
    firsts = staged(
        first_outputs,
        dict(
            tok=tok,
            att=tail.att,
            gq=tail.gq,
            inner_out=tail.inner_out,
            gi=tail.gi,
            low=low,
            bias=bias,
            down=middle.down,
            inner_down=mlp.inner_down,
        ),
        dict(block=shape((tok_dev, D), f32), grad_h=shape((tok_dev, D), f32)),
        raws=dict(qkv=qkv_weight, out=out_weight, v=v_parts),
        scratch=[pltpu.VMEM((D, W_CUT), bf16), pltpu.VMEM((D, D), bf16), pltpu.SemaphoreType.DMA((10,))],
        micros=0.1,
    )
    ends = staged(
        last_outputs,
        dict(
            tok=tok,
            grad=grad,
            gain=norm_gains,
            gq=tail.gq,
            back=mlp.back,
            rest=rest_given,
            block=firsts.block,
            grad_h=firsts.grad_h,
        ),
        dict(block=shape((tok_dev, D)), tokens=shape((tok_dev, D), f32)),
        raws=dict(qkv=qkv_weight, w=quarters(w_y, w_x, "w", firsts.block, rest_given)),
        scratch=[pltpu.VMEM((D, 3 * D - W_CUT), bf16), pltpu.SemaphoreType.DMA((5,))],
        micros=0.1,
    )
    full = shape(adapters.shape, f32)
    new = staged(
        adamw,
        dict(adapters=adapters, first=first_moment, second=second_moment, parts=shares, given=adapters_given),
        dict(grad=full, new=full, first=full, second=full, low=shape(adapters.shape)),
        scalars=dict(chosen=doc_adapter),
        parts=dict(grad=ADAPTERS, new=ADAPTERS, first=ADAPTERS, second=ADAPTERS, low=ADAPTERS),
    )
    return (ends.block[None], ends.tokens[None], new.grad, new.new, new.first, new.second, new.low)


def solution(mesh):
    spread = P(None, None, ("ctx", "wsh"))
    rows = P("wsh", "ctx", None)
    half = P("wsh", None)
    in_specs = (rows, rows, P(), P(), half, half, half, half, P(), spread, spread, spread, half, P("wsh", None, None), half)
    out_specs = (rows, rows, spread, spread, spread, spread, spread)
    return jax.shard_map(on_device, mesh=mesh, in_specs=in_specs, out_specs=out_specs, check_vma=False)
```

```python
from types import SimpleNamespace

import jax
import jax.numpy as jnp
from jax import lax
from jax.experimental import pallas as pl
from jax.experimental.pallas import tpu as pltpu
from jax.sharding import PartitionSpec as P

D = 1024
HEADS = 16
FF = 4096
HEAD_DIM = 64
ROT = 16
ADAPTERS = 8
RANK = 16
STEP = 8
COLS = 8 * D + 2 * FF
CB = 512
NB = COLS // CB
WIDE = 512
W_CUT = 2048
HALF = FF // 2 // CB
QUERIES, KEYS = 512, 512

A_QKV, A_OUT, A_UP, A_DOWN = 0, 1, 2, 3
B_QKV, B_OUT, B_UP, B_DOWN = 7, 10, 11, 15

epsilon = 1e-05
adapter_scale = 8.0
rope_base = 10000.0
learn_rate = 0.02
beta_first = 0.5
beta_second = 0.5
weight_decay = 0.01
adam_epsilon = 1e-08
masked_value = -1e30

bf16 = jnp.bfloat16
f32 = jnp.float32

HBM = pl.BlockSpec(memory_space=pltpu.HBM)


def dot_nn(a, b):
    return jnp.dot(a, b, preferred_element_type=f32)


def dot_nt(a, b):
    return lax.dot_general(a, b, (((1,), (1,)), ((), ())), preferred_element_type=f32)


def dot_tn(a, b):
    return lax.dot_general(a, b, (((0,), (0,)), ((), ())), preferred_element_type=f32)


def shape(dims, dtype=bf16):
    return jax.ShapeDtypeStruct(tuple(dims), dtype)


def cut(index, width=D):
    return slice(index * width, (index + 1) * width)


class Stage:
    def __init__(self, loads, scalar, raw, out, targets):
        self.loads = loads
        self.scalar = scalar
        self.raw = raw
        self.out = out
        self.targets = targets
        self.waited = set()
        self.pending = []

    def __getattr__(self, name):
        buffer, copy = self.loads[name]
        if name not in self.waited:
            self.waited.add(name)
            copy.wait()
        return buffer

    def start(self, *ends):
        copy = pltpu.make_async_copy(*ends)
        copy.start()
        self.pending.append(copy)

    def store(self, buffer, at=None, into=None, sem=0):
        target, sems = self.targets[id(buffer)]
        if at is not None and into is None:
            into, sem = at, at
        source = buffer if at is None else buffer.at[at]
        self.start(source, target if into is None else target.at[into], sems.at[sem])


def staged(body, loads, results, raws=None, scalars=None, scratch=(), parts=None, micros=2, inside=None, alias=None):
    raws, scalars, parts, inside, alias = raws or {}, scalars or {}, parts or {}, inside or {}, alias or {}
    raw_list, raw_tree = jax.tree.flatten(raws)

    def kernel(*refs):
        refs = list(refs)

        def take(count):
            head = refs[:count]
            del refs[:count]
            return head

        scalar_from, load_from = take(len(scalars)), take(len(loads))
        raw = jax.tree.unflatten(raw_tree, take(len(raw_list)))
        targets = take(len(results))
        scalar_to, load_to, out = take(len(scalars)), take(len(loads)), take(len(results))
        (sems,) = take(1)
        out_sems = take(len(results))
        moves = [
            pltpu.make_async_copy(source, buffer, sems.at[i])
            for i, (source, buffer) in enumerate(zip(scalar_from + load_from, scalar_to + load_to))
        ]
        for move in moves:
            move.start()
        for move in moves[: len(scalars)]:
            move.wait()
        stage = Stage(
            dict(zip(loads, zip(load_to, moves[len(scalars) :]))),
            SimpleNamespace(**dict(zip(scalars, scalar_to))),
            SimpleNamespace(**raw),
            SimpleNamespace(**dict(zip(results, out))),
            {id(buffer): ends for buffer, ends in zip(out, zip(targets, out_sems))},
        )
        body(stage, *refs)
        for name in loads:
            getattr(stage, name)
        for copy in stage.pending:
            copy.wait()

    raw_names = list(raws)
    made = pl.pallas_call(
        kernel,
        out_shape=tuple(results.values()),
        in_specs=[HBM] * (len(scalars) + len(loads) + len(raw_list)),
        out_specs=(HBM,) * len(results),
        scratch_shapes=[pltpu.SMEM(a.shape, a.dtype) for a in scalars.values()]
        + [pltpu.VMEM(a.shape, a.dtype) for a in loads.values()]
        + [pltpu.VMEM(inside.get(n, s.shape), s.dtype) for n, s in results.items()]
        + [pltpu.SemaphoreType.DMA((len(loads) + len(scalars) + 1,))]
        + [pltpu.SemaphoreType.DMA((parts.get(n, 1),)) for n in results]
        + list(scratch),
        compiler_params=pltpu.CompilerParams(vmem_limit_bytes=64 * 1024 * 1024),
        input_output_aliases={
            len(scalars) + len(loads) + raw_names.index(a): list(results).index(b) for a, b in alias.items()
        },
        cost_estimate=pl.CostEstimate(flops=int(micros * 1.15e9), bytes_accessed=1024, transcendentals=0),
        name=body.__name__,
    )(*scalars.values(), *loads.values(), *raw_list)
    return SimpleNamespace(**dict(zip(results, made)))


def normalize(values):
    center = values - jnp.mean(values, axis=-1, keepdims=True)
    spread = jnp.mean(center * center, axis=-1, keepdims=True)
    scale = lax.rsqrt(spread + epsilon)
    return center * scale, scale


def give_adapters(stage):
    give = stage.out.give
    for a in range(ADAPTERS):
        give[cut(a, RANK), :] = stage.adapters[a].astype(bf16)
    row = lax.broadcasted_iota(jnp.int32, (RANK, give.shape[1]), 0)
    lane = lax.broadcasted_iota(jnp.int32, (RANK, give.shape[1]), 1)
    choice = jnp.zeros((RANK, give.shape[1]), f32)
    for j in range(stage.scalar.chosen.shape[1]):
        for a in range(ADAPTERS):
            choice = jnp.where((row == j) & (lane == a), stage.scalar.chosen[0, j, a].astype(f32), choice)
    give[ADAPTERS * RANK :, :] = choice.astype(bf16)
    stage.store(give)


def layer_norms(stage):
    out = stage.out
    normed, _ = normalize(stage.tok[...].astype(f32))
    gain, shift = stage.gain, stage.shift
    half = pl.multiple_of((1 - lax.axis_index("wsh")) * (D // 2), D // 2)
    for i, buffer in enumerate((out.attn, out.mlp)):
        buffer[...] = (normed * gain[i : i + 1, :] + shift[i : i + 1, :]).astype(bf16)
        out.give[:, cut(i, D // 2)] = buffer[:, pl.ds(half, D // 2)]
    stage.store(out.give)
    stage.store(out.attn)
    stage.store(out.mlp)


def tables(stage, sem):
    order, starts, out = stage.scalar.order, stage.scalar.starts, stage.out
    source = stage.raw.up
    copy = pltpu.make_async_copy(source.at[own_part(source, 4), hidden_columns(HALF)], out.up, sem)
    copy.start()
    rows, lanes = out.tab.shape[1:]
    ndoc = starts.shape[1]
    ctx = lax.axis_index("ctx")
    half = rows // 2

    def positions(dims, axis):
        index = lax.broadcasted_iota(jnp.int32, dims, axis)
        block = jnp.where(index < half, order[0, 2 * ctx], order[0, 2 * ctx + 1])
        return block * half + index % half

    pos = positions((rows, lanes), 0)
    start = jnp.zeros((rows, lanes), jnp.int32)
    for j in range(1, ndoc):
        start = jnp.where(pos >= starts[0, j], starts[0, j], start)
    lane = lax.broadcasted_iota(jnp.int32, (rows, lanes), 1) % HEAD_DIM
    frequency = jnp.ones((rows, lanes), f32)
    for i in range(1, ROT // 2):
        frequency = jnp.where(lane % (ROT // 2) == i, rope_base ** (-2.0 * i / ROT), frequency)
    angle = (pos - start).astype(f32) * frequency
    sine = jnp.sin(angle)
    out.tab[0] = jnp.where(lane < ROT, jnp.cos(angle), 1.0)
    out.tab[1] = jnp.where(lane < ROT // 2, -sine, 0.0)
    out.tab[2] = jnp.where((lane >= ROT // 2) & (lane < ROT), sine, 0.0)
    stage.store(out.tab)

    def used(dims, row_axis):
        pos = positions(dims, row_axis)
        doc = lax.broadcasted_iota(jnp.int32, dims, 1 - row_axis) // RANK
        held = jnp.zeros(dims, jnp.int32)
        for j in range(1, ndoc):
            held = jnp.where(pos >= starts[0, j], j, held)
        return (held == doc).astype(f32)

    out.mask[...] = used(out.mask.shape, 0)
    out.mask_t[...] = used(out.mask_t.shape, 1)
    stage.store(out.mask)
    stage.store(out.mask_t)
    copy.wait()
    stage.store(out.up)


def choose_adapters(stage):
    adapters, given = stage.adapters, stage.given
    rows = stage.out.rows
    target, sems = stage.targets[id(rows)]
    columns = adapters.shape[2]
    wsh = lax.axis_index("wsh")
    for j in range(rows.shape[0] // RANK):
        index = 0
        for a in range(1, ADAPTERS):
            index = index + a * stage.scalar.chosen[0, j, a]
        start = pl.multiple_of(index * RANK, RANK)
        own_at = pl.multiple_of(wsh * columns, 128)
        other_at = pl.multiple_of((1 - wsh) * columns, 128)
        rows[cut(j, RANK), pl.ds(own_at, columns)] = adapters[index].astype(bf16)
        rows[cut(j, RANK), pl.ds(other_at, columns)] = given[pl.ds(start, RANK), :]
    for i in range(target.shape[0]):
        stage.start(rows, target.at[i], sems.at[i])


def part_orders(share):
    ctx = lax.axis_index("ctx")
    if share == 2:
        return ctx % 2, 1 - ctx % 2
    mine = ctx % 2 * 2 + ctx // 2 % 2
    return mine, mine ^ 1, mine ^ 2, mine ^ 3


def rows_at(first, count):
    return pl.ds(pl.multiple_of(first, count), count)


def own_part(weight, share):
    rows = weight.shape[0] // share
    return rows_at(part_orders(share)[0] * rows, rows)


def place_weights(own, chunks, target, sems, first=0):
    half = own.shape[0]
    own_half = lax.axis_index("wsh")
    copies = [pltpu.make_async_copy(own, target.at[rows_at(own_half * half, half), :], sems.at[first])]
    for column, source_column, width, parts in chunks:
        rows = half // len(parts)
        for order, part in zip(part_orders(len(parts)), parts):
            copies.append(
                pltpu.make_async_copy(
                    part.at[:, source_column : source_column + width],
                    target.at[rows_at((1 - own_half) * half + order * rows, rows), column : column + width],
                    sems.at[first + len(copies)],
                )
            )
    for copy in copies:
        copy.start()
    return copies


def turn(values, tab, sign):
    left = pltpu.roll(values, 120, 1)
    right = pltpu.roll(values, 8, 1)
    return values * tab[0] + sign * (left * tab[1] + right * tab[2])


def swap_halves(first, second):
    low = lax.broadcasted_iota(jnp.int32, first.shape, 1) < HEAD_DIM
    one = jnp.where(low, first, pltpu.roll(second, HEAD_DIM, 1))
    two = jnp.where(low, pltpu.roll(first, HEAD_DIM, 1), second)
    return one, two


def both_streams(stage, side=0):
    half = pl.multiple_of(lax.axis_index("wsh") * (D // 2), D // 2)
    return jnp.concatenate([stage.h[:, pl.ds(half, D // 2)], stage.given[:, cut(side, D // 2)]], axis=0)


def weight_columns(source, first, weights, sems):
    copies = []
    for n in range(weights.shape[0]):
        copies.append(
            pltpu.make_async_copy(source.at[:, first + n * WIDE : first + (n + 1) * WIDE], weights.at[n], sems.at[n])
        )
        copies[-1].start()
    return copies


def partial_qk(stage, weights, sems):
    copies = weight_columns(stage.raw.qkv, 0, weights, sems)
    both = both_streams(stage)
    rows = both.shape[0] // 2
    for n, copy in enumerate(copies):
        copy.wait()
        part = dot_nn(both, weights[n])
        at = (slice(None), cut(n, WIDE))
        stage.out.give[at] = part[rows:].astype(bf16)
        stage.store(stage.out.give, at=at, into=at, sem=n)
        stage.out.kept[n] = part[:rows]
        stage.store(stage.out.kept, n)


def partial_vg(stage, weights, out_rows, sems):
    copies = weight_columns(stage.raw.qkv, 2 * D, weights, sems)
    out_copy = pltpu.make_async_copy(stage.raw.out, out_rows, sems.at[len(copies)])
    out_copy.start()
    both = both_streams(stage)
    rows = both.shape[0] // 2
    for n, copy in enumerate(copies):
        copy.wait()
        part = dot_nn(both, weights[n])
        at = (slice(None), cut(n, WIDE))
        stage.out.give[at] = part[rows:].astype(bf16)
        stage.store(stage.out.give, at=at, into=at, sem=n)
        stage.out.kept[n] = part[:rows]
        stage.store(stage.out.kept, n)
    grads = jnp.concatenate([stage.grad[...], stage.grad_given[...]], axis=0)
    out_copy.wait()
    part = dot_nt(grads, out_rows[...])
    at = (slice(None), slice(D, D + WIDE))
    stage.out.give[at] = part[rows:].astype(bf16)
    stage.store(stage.out.give, at=at, into=at, sem=D // WIDE)
    stage.out.kept[D // WIDE] = part[:rows]
    stage.store(stage.out.kept, D // WIDE)


def queries_keys(stage):
    low, mask, bias, tab, kept, given = stage.low, stage.mask[...], stage.bias, stage.tab, stage.kept, stage.given
    inner = (dot_nt(stage.h[...], low[A_QKV]) * mask).astype(bf16)
    stage.out.inner[...] = inner
    stage.store(stage.out.inner)
    grad_inner = (adapter_scale * dot_nt(stage.grad[...], low[B_OUT]) * mask).astype(bf16)
    stage.out.grad_inner[...] = grad_inner
    stage.store(stage.out.grad_inner)
    steps = D // WIDE
    for n in range(steps):
        sides = []
        for kind in range(2):
            at = cut(kind * steps + n, WIDE)
            part = kept[kind * steps + n] + given[:, at].astype(f32) + bias[:, at]
            sides.append(part + adapter_scale * dot_nn(inner, low[B_QKV + kind][:, cut(n, WIDE)]))
        for pair in range(WIDE // 128):
            query = turn(sides[0][:, cut(pair, 128)], tab, 1.0) * HEAD_DIM**-0.5
            key = turn(sides[1][:, cut(pair, 128)], tab, 1.0)
            head = n * WIDE // HEAD_DIM + 2 * pair
            for i, both in enumerate(swap_halves(query, key)):
                stage.out.send[head + i] = both.astype(bf16)
    stage.store(stage.out.send, into=(slice(None), 0))
    base, kept, wsh = stage.out.base, stage.kept_vg, lax.axis_index("wsh")
    for n in range(steps):
        base[n] = kept[n] + bias[:, 2 * D + n * WIDE : 2 * D + (n + 1) * WIDE]
        base[n] += adapter_scale * dot_nn(inner, low[B_QKV + 2][:, cut(n, WIDE)])
        base[steps + n] = jnp.where(wsh == n, kept[steps], 0.0) + dot_nn(grad_inner, low[A_OUT][:, cut(n, WIDE)])
    stage.store(base)


def values_grads(stage):
    base, given = stage.base, stage.given
    steps = D // WIDE
    wsh = lax.axis_index("wsh")
    for n in range(steps):
        value = base[n] + given[:, cut(n, WIDE)].astype(f32)
        grad = base[steps + n] + jnp.where(wsh == n, 0.0, given[:, D:].astype(f32))
        for pair in range(WIDE // 128):
            head = n * WIDE // HEAD_DIM + 2 * pair
            for i, both in enumerate(swap_halves(value[:, cut(pair, 128)], grad[:, cut(pair, 128)])):
                stage.out.send[head + i] = both.astype(bf16)
        heads = pl.ds(n * WIDE // HEAD_DIM, WIDE // HEAD_DIM)
        stage.store(stage.out.send, at=heads, into=(heads, 1), sem=n)


def attention(stage, xt, dks, dvs, ks, vs, aq, s_scr, e_scr):
    order = stage.scalar.order
    rows = aq.shape[0]
    blocks = order.shape[1]
    half = rows // blocks
    hd = HEAD_DIM
    x = stage.arrived
    per = x.shape[2] // half
    for i in range(blocks):
        start = pl.multiple_of(order[0, i] * half, half)
        for side in range(2):
            aq[pl.ds(start, half), cut(side, 2 * hd)] = x[i // per, side, cut(i % per, half), :]
    for t in range(rows // KEYS):
        part = aq[cut(t, KEYS), :]
        ks[cut(t, KEYS), :] = part[:, hd : 2 * hd]
        vs[cut(t, KEYS), :] = part[:, 2 * hd : 3 * hd]
        xt[:, cut(t, KEYS)] = part.T
    dks[...] = jnp.zeros_like(dks)
    dvs[...] = jnp.zeros_like(dvs)
    later = lax.broadcasted_iota(jnp.int32, (KEYS, QUERIES), 0) - lax.broadcasted_iota(jnp.int32, (KEYS, QUERIES), 1)
    for b in range(rows // QUERIES):
        at = cut(b, QUERIES)
        q_t = xt[0:hd, at]
        g_t = xt[3 * hd : 4 * hd, at]
        tiles = [(cut(t, KEYS), b * QUERIES - t * KEYS) for t in range(-(-(b + 1) * QUERIES // KEYS))]
        top = jnp.full((8, QUERIES), masked_value, f32)
        for part, ahead in tiles:
            s = dot_nn(ks[part, :], q_t)
            if ahead < KEYS - 1:
                s = jnp.where(later <= ahead, s, masked_value)
            s_scr[part, :] = s
            top = jnp.maximum(top, jnp.max(s.reshape(KEYS // 8, 8, QUERIES), axis=0))
        top = jnp.max(top, axis=0, keepdims=True)
        total = jnp.zeros((8, QUERIES), f32)
        att = jnp.zeros((hd, QUERIES), f32)
        for part, _ in tiles:
            e = jnp.exp(s_scr[part, :] - top)
            total = total + jnp.sum(e.reshape(KEYS // 8, 8, QUERIES), axis=0)
            e = e.astype(bf16)
            e_scr[part, :] = e
            att = att + dot_nn(xt[2 * hd : 3 * hd, part], e)
        inverse = 1.0 / jnp.sum(total, axis=0, keepdims=True)
        att = att * inverse
        g_f = g_t.astype(f32)
        delta = jnp.sum(g_f * att, axis=0, keepdims=True) * inverse
        g_n = (g_f * inverse).astype(bf16)
        dq = jnp.zeros((hd, QUERIES), f32)
        for part, _ in tiles:
            e = e_scr[part, :]
            dp = dot_nn(vs[part, :], g_n)
            ds = (e.astype(f32) * (dp - delta)).astype(bf16)
            dq = dq + dot_nn(xt[hd : 2 * hd, part], ds)
            dks[part, :] += dot_nt(ds, q_t)
            dvs[part, :] += dot_nt(e, g_n)
        both = jnp.concatenate([att, dq * hd**-0.5], axis=0)
        aq[at, 0 : 2 * hd] = both.T.astype(bf16)
    for t in range(rows // KEYS):
        aq[cut(t, KEYS), 2 * hd : 3 * hd] = dks[cut(t, KEYS), :].astype(bf16)
        aq[cut(t, KEYS), 3 * hd :] = dvs[cut(t, KEYS), :].astype(bf16)
    for i in range(blocks):
        start = pl.multiple_of(order[0, i] * half, half)
        stage.out.back[cut(i, half), :] = aq[pl.ds(start, half), :]
    stage.store(stage.out.back)


def attention_one_document(order, arrived):
    rows = arrived.shape[0] * arrived.shape[2]
    hd = HEAD_DIM
    return staged(
        attention,
        dict(arrived=arrived),
        dict(back=shape((rows, 4 * hd))),
        scalars=dict(order=order),
        scratch=[
            pltpu.VMEM((4 * hd, rows), bf16),
            pltpu.VMEM((rows, hd), f32),
            pltpu.VMEM((rows, hd), f32),
            pltpu.VMEM((rows, hd), bf16),
            pltpu.VMEM((rows, hd), bf16),
            pltpu.VMEM((rows, 4 * hd), bf16),
            pltpu.VMEM((rows, QUERIES), f32),
            pltpu.VMEM((rows, QUERIES), bf16),
        ],
        micros=17,
    ).back


def attention_documents(arrived, pos, doc, groups, first_row):
    rows = arrived.shape[0] * arrived.shape[2]
    hd = HEAD_DIM
    qk, vg = (arrived[:, side].reshape(rows, 2 * hd) for side in range(2))
    q, k, v, g = qk[:, :hd], qk[:, hd:], vg[:, :hd], vg[:, hd:]
    if groups is not None:
        both = lax.all_gather(jnp.concatenate([k, v], 1), "ctx", axis=0, tiled=True, axis_index_groups=groups)
        k, v = both[:, :hd], both[:, hd:]
    step = 512
    my_pos = lax.dynamic_slice_in_dim(pos, first_row, rows)
    my_doc = lax.dynamic_slice_in_dim(doc, first_row, rows)

    def one(sums, item):
        q_b, g_b, pos_b, doc_b = item
        scores = dot_nt(q_b, k)
        allowed = (doc_b[:, None] == doc[None, :]) & (pos[None, :] <= pos_b[:, None])
        scores = jnp.where(allowed, scores, masked_value)
        top = jnp.max(scores, axis=1, keepdims=True)
        weights = jnp.exp(scores - top)
        weights = weights / jnp.sum(weights, axis=1, keepdims=True)
        weights_low = weights.astype(bf16)
        att = dot_nn(weights_low, v)
        delta = jnp.sum(g_b.astype(f32) * att, axis=1, keepdims=True)
        ds = (weights * (dot_nt(g_b, v) - delta)).astype(bf16)
        dq = dot_nn(ds, k) * hd**-0.5
        sums = (sums[0] + dot_tn(ds, q_b), sums[1] + dot_tn(weights_low, g_b))
        return sums, jnp.concatenate([att, dq], 1).astype(bf16)

    zero = jnp.zeros((k.shape[0], hd), f32)
    split = lambda a: a.reshape((rows // step, step) + a.shape[1:])
    sums, att_dq = lax.scan(one, (zero, zero), tuple(map(split, (q, g, my_pos, my_doc))))
    sums = jnp.concatenate(sums, 1)
    if groups is not None:
        sums = lax.psum_scatter(sums, "ctx", scatter_dimension=0, tiled=True, axis_index_groups=groups)
    return jnp.concatenate([att_dq.reshape(rows, 2 * hd), sums.astype(bf16)], axis=1)


def swapped(rows):
    half = rows.shape[0] // 2
    return jnp.concatenate([rows[half:], rows[:half]], axis=0)


def hidden_block(j):
    wsh = lax.axis_index("wsh")
    return (wsh if j < HALF else 1 - wsh) * HALF + j % HALF


def hidden_columns(j):
    return pl.ds(pl.multiple_of(hidden_block(j // HALF * HALF) * CB, HALF * CB), HALF * CB)


def up_blocks(source, weights, sems, order):
    copies = {}
    for j in order:
        first = pl.multiple_of(hidden_block(j) * CB, CB)
        copies[j] = pltpu.make_async_copy(source.at[:, pl.ds(first, CB)], weights.at[j], sems.at[j])
        copies[j].start()
    return copies


def adapter_block(low, first, j):
    return low[first + hidden_block(j) // 2, :, cut(j % 2, CB)]


def mlp_up(stage, weights, sems):
    out = stage.out
    order = [*range(HALF, 2 * HALF), *range(HALF)]
    copies = up_blocks(stage.raw.up, weights, sems, order)
    both = both_streams(stage, 1)
    for j in order:
        copies[j].wait()
        part = dot_nn(both, weights[j])
        if j < HALF:
            out.kept[j] = part
        elif j == HALF:
            out.early[...] = part.astype(bf16)
            stage.store(out.early)
        else:
            out.late[:, cut(j - HALF - 1, CB)] = part.astype(bf16)
            if j == 2 * HALF - 1:
                stage.store(out.late, into=pl.ds(0, part.shape[0]))
    stage.store(out.kept)


def share_at(kind, j, rank, rows):
    down, right = divmod(kind * HALF + j, HALF - 1)
    return pl.ds(rows + down * rank, rank), cut(right, CB)


def mlp_share(stage, sems):
    out = stage.out
    qkv, weight = stage.raw.qkv, stage.raw.out
    mine = own_part(qkv, 4)
    copies = [
        pltpu.make_async_copy(weight.at[mine, :], out.first.at[:, :D], sems.at[0]),
        pltpu.make_async_copy(qkv.at[mine, :W_CUT], out.first.at[:, D:], sems.at[1]),
        pltpu.make_async_copy(qkv.at[mine, W_CUT:], out.second, sems.at[2]),
    ]
    for copy in copies:
        copy.start()
    share, low, mask = out.late, stage.low, stage.mask_t[...]
    rank, rows = mask.shape
    for j in range(HALF):
        share[share_at(0, j, rank, 0)] = adapter_block(low, A_DOWN, HALF + j)
        share[share_at(1, j, rank, 0)] = adapter_block(low, B_UP, HALF + j)
    inner = (dot_nt(low[A_UP], stage.h[...]) * mask).astype(bf16)
    back = (adapter_scale * dot_nt(low[B_DOWN], stage.grad[...]) * mask).astype(bf16)
    zero = jnp.zeros((rank, CB - 2 * rows), bf16)
    share[share_at(2, 0, rank, 0)] = jnp.concatenate([inner, back, zero], axis=1)
    stage.store(share, into=pl.ds(2 * rows, 3 * rank))
    out.products[...] = jnp.concatenate([inner, back], axis=1)
    stage.store(out.products)
    for copy in copies:
        copy.wait()
    for buffer in (out.first, out.second):
        stage.store(buffer)


def diagonal(one, two):
    zero = jnp.zeros_like(one)
    return jnp.concatenate([jnp.concatenate([one, zero], axis=1), jnp.concatenate([zero, two], axis=1)], axis=0)


def mlp_middle(stage, down_rows, up_rows, down_sems, up_sems):
    out, low = stage.out, stage.low
    copies = []
    for j in range(HALF):
        copies.append(pltpu.make_async_copy(stage.raw.down.at[cut(j, CB), :], down_rows.at[j], down_sems.at[j]))
        copies[-1].start()
    up_copies = place_weights(
        stage.raw.up.at[:, hidden_columns(0)], [(0, 0, HALF * CB, stage.raw.u)], up_rows, up_sems, 0
    )
    grads = jnp.concatenate([stage.grad[...], stage.grad_given[...]], axis=0)
    rows = grads.shape[0] // 2
    products, late = stage.products[...], stage.late
    rank = products.shape[0]
    other = late[share_at(2, 0, rank, 2 * rows)]
    inner, back = (diagonal(products[:, cut(i, rows)], other[:, cut(i, rows)]) for i in range(2))
    sums = None
    grad_ups = []
    for j in range(HALF):
        at = cut(j, CB)
        a_both = jnp.concatenate([adapter_block(low, A_DOWN, j), late[share_at(0, j, rank, 2 * rows)]], axis=0)
        b_both = jnp.concatenate([adapter_block(low, B_UP, j), late[share_at(1, j, rank, 2 * rows)]], axis=0)
        part = stage.early[...] if j == 0 else late[: 2 * rows, cut(j - 1, CB)]
        shift = pl.multiple_of(4 * D + hidden_block(j) * CB, CB)
        up = stage.kept[j] + swapped(part.astype(f32)) + stage.bias[:, pl.ds(shift, CB)]
        up = up + adapter_scale * dot_tn(inner, b_both)
        spread = 0.5 * (1.0 + lax.erf(up * (0.5**0.5)))
        hidden = (up * spread).astype(bf16)
        slope = spread + up * (jnp.exp(-0.5 * up * up) * (0.5 / jnp.pi) ** 0.5)
        copies[j].wait()
        down = down_rows[j]
        grad_hidden = dot_nt(grads, down) + dot_tn(back, a_both)
        grad_up = (grad_hidden * slope).astype(bf16)
        grad_ups.append(grad_up)
        parts = dot_nn(hidden, down), dot_nt(a_both, hidden), dot_nt(b_both, grad_up)
        sums = parts if sums is None else tuple(one + two for one, two in zip(sums, parts))
        a_grad = dot_nn(back, hidden).astype(bf16)
        b_grad = (adapter_scale * dot_nn(inner, grad_up)).astype(bf16)
        out.grads[j], out.grads[HALF + j] = a_grad[:rank], b_grad[:rank]
        out.pack[pack_at(0, j, rank)], out.pack[pack_at(1, j, rank)] = a_grad[rank:], b_grad[rank:]
    down, inner_down, gi_up = sums
    out.small[0], out.small[1] = inner_down[:rank, :rows], gi_up[:rank, :rows]
    out.pack[4 * rank : 5 * rank, :] = jnp.zeros((rank, D), bf16)
    out.pack[4 * rank : 5 * rank, 0:rows] = inner_down[rank:, rows:].astype(bf16)
    out.pack[4 * rank : 5 * rank, rows : 2 * rows] = gi_up[rank:, rows:].astype(bf16)
    for copy in up_copies:
        copy.wait()
    total = None
    for j in range(HALF):
        part = dot_nt(grad_ups[j], up_rows[:, cut(j, CB)])
        total = part if total is None else total + part
    out.pack[5 * rank :, :] = total[rows:].astype(bf16)
    stage.store(out.pack)
    out.kept[...] = total[:rows]
    out.rest[...] = down[rows:].astype(bf16)
    out.down[...] = down[:rows]
    for buffer in (out.small, out.grads, out.kept, out.rest, out.down):
        stage.store(buffer)


def pack_at(kind, j, rank):
    return pl.ds((2 * kind + j // 2) * rank, rank), cut(j % 2, CB)


def mlp_finish(stage):
    out, low, mask = stage.out, stage.low, stage.mask_t[...]
    rank, rows = mask.shape
    pack, small, wsh = stage.pack, stage.small, lax.axis_index("wsh")
    extra = pack[4 * rank : 5 * rank, :].astype(f32)
    inner_down = ((small[0] + extra[:, 0:rows]) * mask).astype(bf16)
    gi_up = (adapter_scale * (small[1] + extra[:, rows : 2 * rows]) * mask).astype(bf16)
    for j in range(HALF):
        for kind in range(2):
            out.flat[2 + kind * 2 * HALF + wsh * HALF + j] = stage.grads[kind * HALF + j]
            out.flat[2 + kind * 2 * HALF + (1 - wsh) * HALF + j] = pack[pack_at(kind, j, rank)]
    up_grad = dot_nn(gi_up, stage.h[...])
    down_grad = adapter_scale * dot_nn(inner_down, stage.grad[...])
    for i in range(2):
        out.flat[i] = up_grad[:, cut(i, CB)].astype(bf16)
        out.flat[18 + i] = down_grad[:, cut(i, CB)].astype(bf16)
    per = D // CB
    stage.store(out.flat, at=pl.ds(0, 10), into=pl.ds(A_UP * per, 10), sem=0)
    stage.store(out.flat, at=pl.ds(10, 10), into=pl.ds(B_UP * per, 10), sem=1)
    out.inner_down[...] = inner_down
    stage.store(out.inner_down)
    out.back[...] = stage.kept[...] + pack[5 * rank :, :].astype(f32) + dot_tn(gi_up, low[A_UP])
    stage.store(out.back)


def adapter_gradients(stage):
    arrived, tab = stage.arrived, stage.tab
    att, gq, flat = stage.out.att, stage.out.gq, stage.out.flat
    for pair in range(HEADS // 2):
        at = cut(pair, 128)
        one, two = arrived[2 * pair].astype(f32), arrived[2 * pair + 1].astype(f32)
        attended, query = swap_halves(one[:, :128], two[:, :128])
        key, value = swap_halves(one[:, 128:], two[:, 128:])
        att[:, at] = attended.astype(bf16)
        for kind, part in enumerate((turn(query, tab, -1.0), turn(key, tab, -1.0), value)):
            gq[:, kind * D + pair * 128 : kind * D + (pair + 1) * 128] = part.astype(bf16)
    stage.store(att)
    stage.store(gq)
    low, mask, h, grad = stage.low, stage.mask[...], stage.h, stage.grad
    inner_out = (dot_nt(att[...], low[A_OUT]) * mask).astype(bf16)
    stage.out.inner_out[...] = inner_out
    stage.store(stage.out.inner_out)
    gi = sum(dot_nt(gq[:, cut(i)], low[B_QKV + i]) for i in range(3))
    gi = (adapter_scale * gi * mask).astype(bf16)
    stage.out.gi[...] = gi
    stage.store(stage.out.gi)
    per = D // CB

    def put(block, value):
        place = block if block < A_UP else block - B_QKV + A_UP
        for i in range(per):
            flat[place * per + i] = value[:, cut(i, CB)].astype(bf16)

    put(A_QKV, dot_tn(gi, h[...]))
    put(A_OUT, dot_tn(stage.grad_inner[...], att[...]))
    put(B_OUT, adapter_scale * dot_tn(inner_out, grad[...]))
    for i in range(3):
        put(B_QKV + i, adapter_scale * dot_tn(stage.inner[...], gq[:, cut(i)]))
    first, rest = A_UP * per, (B_UP - B_QKV) * per
    stage.store(flat, at=pl.ds(0, first), into=pl.ds(0, first), sem=0)
    stage.store(flat, at=pl.ds(first, rest), into=pl.ds(B_QKV * per, rest), sem=1)


def first_outputs(stage, wq, wo, sems):
    raw, low, bias = stage.raw, stage.low, stage.bias
    o_copies = place_weights(raw.out, [(0, 0, D, raw.v)], wo, sems)
    q_copies = place_weights(raw.qkv.at[:, :W_CUT], [(0, D, W_CUT, raw.v)], wq, sems, 5)
    att, inner_out, inner_down = stage.att[...], stage.inner_out[...], stage.inner_down[...]
    for copy in o_copies:
        copy.wait()
    for n in range(D // WIDE):
        at = cut(n, WIDE)
        shift = n * WIDE
        part = dot_nn(att, wo[:, at]) + bias[:, 3 * D + shift : 3 * D + shift + WIDE]
        part = part + adapter_scale * dot_nn(inner_out, low[B_OUT][:, at])
        mlp = stage.down[:, at] + bias[:, 4 * D + FF + shift : 4 * D + FF + shift + WIDE]
        mlp = mlp + adapter_scale * dot_tn(inner_down, low[B_DOWN][:, at])
        stage.out.block[:, at] = part + stage.tok[:, at].astype(f32) + mlp
    stage.store(stage.out.block)
    for copy in q_copies:
        copy.wait()
    stage.out.grad_h[...] = dot_nt(stage.gq[:, :W_CUT], wq[...]) + dot_nn(stage.gi[...], low[A_QKV])
    stage.store(stage.out.grad_h)


def last_outputs(stage, wq, sems):
    raw, gain, out = stage.raw, stage.gain, stage.out
    copies = place_weights(raw.qkv.at[:, W_CUT:], [(0, 0, 3 * D - W_CUT, raw.w)], wq, sems)
    normed, scale = normalize(stage.tok[...].astype(f32))
    out.block[...] = (stage.block[...] + stage.rest[...].astype(f32)).astype(bf16)
    stage.store(out.block)
    for copy in copies:
        copy.wait()
    grad_h = stage.grad_h[...] + dot_nt(stage.gq[:, W_CUT:], wq[...])
    grad_n = grad_h * gain[0:1, :] + stage.back[...] * gain[1:2, :]
    grad_v = grad_n - jnp.mean(grad_n, axis=-1, keepdims=True) - normed * jnp.mean(grad_n * normed, axis=-1, keepdims=True)
    out.tokens[...] = stage.grad[...].astype(f32) + scale * grad_v
    stage.store(out.tokens)


def adamw(stage):
    chosen, parts, out = stage.scalar.chosen, stage.parts, stage.out
    given, wsh = stage.given, lax.axis_index("wsh")
    sums = []
    for stream in range(2):
        total = parts[stream].astype(f32)
        for source in range(stream + 2, parts.shape[0], 2):
            total = total + parts[source].astype(f32)
        sums.append(total)
    ndoc = sums[0].shape[0] // RANK
    for a in range(ADAPTERS):
        grad = None
        for stream in range(2):
            for j in range(ndoc):
                own = chosen[0, j, a].astype(f32)
                other = given[ADAPTERS * RANK + j : ADAPTERS * RANK + j + 1, a : a + 1].astype(f32)
                term = jnp.where(wsh == stream, own, other) * sums[stream][cut(j, RANK), :]
                grad = term if grad is None else grad + term
        new_first = beta_first * stage.first[a] + (1.0 - beta_first) * grad
        new_second = beta_second * stage.second[a] + (1.0 - beta_second) * grad * grad
        first_hat = new_first / (1.0 - beta_first**STEP)
        second_hat = new_second / (1.0 - beta_second**STEP)
        old = stage.adapters[a]
        new = old - learn_rate * (first_hat / (jnp.sqrt(second_hat) + adam_epsilon) + weight_decay * old)
        for buffer, value in (
            (out.grad, grad),
            (out.new, new),
            (out.first, new_first),
            (out.second, new_second),
            (out.low, new.astype(bf16)),
        ):
            buffer[a] = value
            stage.store(buffer, a)


def stream_layout(order_row, starts_row, rows, total_rows, half_dev):
    slot = rows // half_dev
    picked = (slot[:, None] == jnp.arange(order_row.shape[0], dtype=jnp.int32)[None, :]).astype(jnp.int32)
    pos = jnp.sum(picked * order_row[None, :], axis=1) * half_dev + rows % half_dev
    finish = jnp.concatenate([starts_row[1:], jnp.full((1,), total_rows, jnp.int32)])
    inside = ((pos[:, None] >= starts_row[None, :]) & (pos[:, None] < finish[None, :])).astype(jnp.int32)
    doc = jnp.sum(inside * jnp.arange(starts_row.shape[0], dtype=jnp.int32)[None, :], axis=1)
    place = pos - jnp.sum(inside * starts_row[None, :], axis=1)
    return pos, doc, place, inside


def tie(first, *others):
    return lax.optimization_barrier((first,) + others)[0]


def on_device(
    tokens,
    out_cotangent,
    norm_gains,
    norm_biases,
    qkv_weight,
    out_weight,
    up_weight,
    down_weight,
    proj_biases,
    adapters,
    first_moment,
    second_moment,
    doc_starts,
    doc_adapter,
    block_order,
):
    n_ctx = lax.axis_size("ctx")
    n_dev = n_ctx * lax.axis_size("wsh")
    ctx = lax.axis_index("ctx")
    wsh = lax.axis_index("wsh")
    tok_dev = tokens.shape[1]
    half_dev = tok_dev // 2
    total_rows = tok_dev * n_ctx
    ndoc = doc_starts.shape[1]
    rank = ndoc * RANK
    columns = adapters.shape[2]
    tok, grad = tokens[0], out_cotangent[0]
    bias = proj_biases[None, :]

    def to_y(a, name):
        with jax.named_scope("y_" + name):
            return lax.ppermute(a, "wsh", [(0, 1), (1, 0)])

    def to_x(a, name):
        with jax.named_scope("x_" + name):
            return lax.ppermute(a, "ctx", [(i, i ^ 2) for i in range(n_ctx)])

    def to_core(a, name):
        with jax.named_scope("c_" + name):
            return lax.ppermute(a, "ctx", [(i, i ^ 1) for i in range(n_ctx)])

    give = staged(
        give_adapters,
        dict(adapters=adapters),
        dict(give=shape(((ADAPTERS + 1) * RANK, columns))),
        scalars=dict(chosen=doc_adapter),
    ).give
    adapters_given = to_y(give, "adapters")
    normed = staged(
        layer_norms,
        dict(tok=tie(tok, give), gain=norm_gains, shift=norm_biases),
        dict(attn=shape(tok.shape), mlp=shape(tok.shape), give=shape((tok_dev, D))),
    )
    h_attn, h_mlp = normed.attn, normed.mlp
    given = to_y(normed.give, "h")
    grad_given = to_y(tie(grad, normed.give), "grad")
    chosen_rows = staged(
        choose_adapters,
        dict(adapters=adapters, given=tie(adapters_given, h_attn)),
        dict(rows=shape((n_ctx, rank, 2 * columns))),
        scalars=dict(chosen=doc_adapter),
        parts=dict(rows=n_ctx),
        inside=dict(rows=(rank, 2 * columns)),
    ).rows
    low = lax.all_to_all(chosen_rows, "ctx", 0, 0, tiled=True)
    if n_ctx != HEADS:
        low = low.reshape(COLS // D, n_ctx // HEADS, rank, 2 * columns).transpose(0, 2, 1, 3).reshape(COLS // D, rank, D)

    both = staged(
        partial_qk,
        dict(h=h_attn, given=tie(given, chosen_rows)),
        dict(give=shape((tok_dev, 2 * D)), kept=shape((2 * D // WIDE, tok_dev, WIDE), f32)),
        raws=dict(qkv=qkv_weight),
        scratch=[pltpu.VMEM((2 * D // WIDE, D // 2, WIDE), bf16), pltpu.SemaphoreType.DMA((2 * D // WIDE,))],
        parts=dict(give=2 * D // WIDE, kept=2 * D // WIDE),
        micros=3,
    )
    kept_qk, give_qk = both.kept, both.give
    given_qk = to_y(give_qk, "qk")
    both = staged(
        partial_vg,
        dict(h=tie(h_attn, give_qk), given=given, grad=grad, grad_given=grad_given),
        dict(give=shape((tok_dev, 3 * D // 2)), kept=shape((D // WIDE + 1, tok_dev, WIDE), f32)),
        raws=dict(qkv=qkv_weight, out=out_weight),
        scratch=[
            pltpu.VMEM((D // WIDE, D // 2, WIDE), bf16),
            pltpu.VMEM((D // 2, D), bf16),
            pltpu.SemaphoreType.DMA((D // WIDE + 1,)),
        ],
        parts=dict(give=D // WIDE + 1, kept=D // WIDE + 1),
        micros=3,
    )
    given_vg = to_y(both.give, "vg")
    table = staged(
        tables,
        {},
        dict(tab=shape((3, tok_dev, 128), f32), mask=shape((tok_dev, rank), f32), mask_t=shape((rank, tok_dev), f32), up=shape((D // 8, HALF * CB))),
        raws=dict(up=up_weight),
        scalars=dict(order=tie(block_order, both.give), starts=doc_starts),
        scratch=[pltpu.SemaphoreType.DMA],
        micros=0.1,
    )
    tab, mask, mask_t = table.tab, table.mask, table.mask_t
    up = staged(
        mlp_up,
        dict(h=tie(h_mlp, both.give), given=given),
        dict(
            early=shape((2 * tok_dev, CB)),
            late=shape((2 * tok_dev + 3 * rank, (HALF - 1) * CB)),
            kept=shape((HALF, 2 * tok_dev, CB), f32),
        ),
        raws=dict(up=up_weight),
        inside=dict(late=(2 * tok_dev, (HALF - 1) * CB)),
        scratch=[pltpu.VMEM((2 * HALF, D // 2, CB), bf16), pltpu.SemaphoreType.DMA((2 * HALF,))],
        micros=0.1,
    )
    heads = shape((HEADS, 2, tok_dev, 2 * HEAD_DIM))
    one = (HEADS, tok_dev, 2 * HEAD_DIM)
    made = staged(
        queries_keys,
        dict(
            h=tie(h_attn, up.kept),
            grad=grad,
            low=low,
            mask=mask,
            bias=bias,
            tab=tab,
            kept=kept_qk,
            given=given_qk,
            kept_vg=both.kept,
        ),
        dict(
            inner=shape((tok_dev, rank)),
            grad_inner=shape((tok_dev, rank)),
            send=heads,
            base=shape((2 * D // WIDE, tok_dev, WIDE), f32),
        ),
        inside=dict(send=one),
        micros=0.1,
    )
    inner_qkv, grad_inner_out = made.inner, made.grad_inner
    made = staged(
        values_grads,
        dict(base=made.base, given=given_vg),
        dict(send=heads),
        raws=dict(send=made.send),
        inside=dict(send=one),
        alias=dict(send="send"),
        parts=dict(send=D // WIDE),
        micros=3,
    )
    parts = n_ctx // HEADS
    near = None if parts == 1 else [[g * HEADS + i for i in range(HEADS)] for g in range(parts)]

    def exchange(a):
        return lax.all_to_all(a, "ctx", 0, 0, tiled=True, axis_index_groups=near)

    shared = staged(
        mlp_share,
        dict(h=h_mlp, grad=grad, low=low, mask_t=mask_t),
        dict(
            late=shape(up.late.shape),
            products=shape((rank, 2 * tok_dev)),
            first=shape((D // 8, D + W_CUT)),
            second=shape((D // 8, 3 * D - W_CUT)),
        ),
        raws=dict(late=up.late, qkv=qkv_weight, out=out_weight),
        inside=dict(late=(3 * rank, (HALF - 1) * CB)),
        alias=dict(late="late"),
        scratch=[pltpu.SemaphoreType.DMA((3,))],
    )

    def quarters(y, x, name, *after):
        return [y, x, to_core(tie(y, *after), name + "y"), to_core(tie(x, *after), name + "x")]

    u_y = to_y(table.up, "u")
    early_given = to_y(up.early, "early")
    u_x = to_x(tie(u_y, shared.products), "u")
    late_given = to_y(shared.late, "late")
    arrived = tie(exchange(made.send), u_y, early_given)
    if parts == 1 and ndoc == 1:
        done = attention_one_document(block_order, arrived)
    else:
        all_pos, all_doc, _, _ = stream_layout(
            block_order[0], doc_starts[0], jnp.arange(total_rows, dtype=jnp.int32), total_rows, half_dev
        )
        far = None if parts == 1 else [[g * HEADS + i for g in range(parts)] for i in range(HEADS)]
        done = attention_documents(arrived, all_pos, all_doc, far, ctx // HEADS * HEADS * tok_dev)
    back = exchange(tie(done.reshape(HEADS, tok_dev, 4 * HEAD_DIM), u_x, late_given))
    v_y = to_y(tie(shared.first, done), "v")
    middle = staged(
        mlp_middle,
        dict(
            kept=up.kept,
            early=tie(early_given, done),
            late=late_given,
            grad=grad,
            grad_given=grad_given,
            low=low,
            bias=bias,
            products=shared.products,
        ),
        dict(
            pack=shape((5 * rank + tok_dev, D)),
            small=shape((2, rank, tok_dev), f32),
            grads=shape((2 * HALF, rank, CB)),
            kept=shape((tok_dev, D), f32),
            rest=shape((tok_dev, D)),
            down=shape((tok_dev, D), f32),
        ),
        raws=dict(down=down_weight, up=up_weight, u=quarters(u_y, u_x, "u", done)),
        scratch=[
            pltpu.VMEM((HALF, CB, D), bf16),
            pltpu.VMEM((D, HALF * CB), bf16),
            pltpu.SemaphoreType.DMA((HALF,)),
            pltpu.SemaphoreType.DMA((5,)),
        ],
        micros=0.1,
    )
    pack_given = to_y(middle.pack, "pack")
    v_x = to_x(tie(v_y, middle.pack), "v")
    w_y = to_y(tie(shared.second, v_y, middle.pack), "w")
    rest_given = to_y(tie(middle.rest, pack_given), "rest")
    tail = staged(
        adapter_gradients,
        dict(
            arrived=back,
            tab=tab,
            low=low,
            mask=mask,
            h=h_attn,
            grad=grad,
            inner=inner_qkv,
            grad_inner=grad_inner_out,
        ),
        dict(
            att=shape((tok_dev, D)),
            gq=shape((tok_dev, 3 * D)),
            inner_out=shape((tok_dev, rank)),
            gi=shape((tok_dev, rank)),
            flat=shape((NB, rank, CB)),
        ),
        inside=dict(flat=(12, rank, CB)),
        parts=dict(flat=2),
        micros=0.1,
    )
    mlp = staged(
        mlp_finish,
        dict(
            small=middle.small,
            grads=middle.grads,
            pack=pack_given,
            kept=middle.kept,
            h=h_mlp,
            grad=grad,
            low=low,
            mask_t=mask_t,
        ),
        dict(inner_down=shape((rank, tok_dev)), back=shape((tok_dev, D), f32), flat=shape((NB, rank, CB))),
        raws=dict(flat=tail.flat),
        inside=dict(flat=(20, rank, CB)),
        alias=dict(flat="flat"),
        parts=dict(flat=2),
        micros=0.1,
    )
    flat = mlp.flat
    if columns != CB:
        flat = flat.reshape(NB, rank, CB // columns, columns).transpose(0, 2, 1, 3).reshape(n_dev, rank, columns)
    shares = lax.all_to_all(tie(flat, w_y), ("ctx", "wsh"), 0, 0, tiled=True)
    v_parts = quarters(v_y, v_x, "v", tail.att)
    w_x = to_x(tie(w_y, flat), "w")
    firsts = staged(
        first_outputs,
        dict(
            tok=tok,
            att=tail.att,
            gq=tail.gq,
            inner_out=tail.inner_out,
            gi=tail.gi,
            low=low,
            bias=bias,
            down=middle.down,
            inner_down=mlp.inner_down,
        ),
        dict(block=shape((tok_dev, D), f32), grad_h=shape((tok_dev, D), f32)),
        raws=dict(qkv=qkv_weight, out=out_weight, v=v_parts),
        scratch=[pltpu.VMEM((D, W_CUT), bf16), pltpu.VMEM((D, D), bf16), pltpu.SemaphoreType.DMA((10,))],
        micros=0.1,
    )
    ends = staged(
        last_outputs,
        dict(
            tok=tok,
            grad=grad,
            gain=norm_gains,
            gq=tail.gq,
            back=mlp.back,
            rest=rest_given,
            block=firsts.block,
            grad_h=firsts.grad_h,
        ),
        dict(block=shape((tok_dev, D)), tokens=shape((tok_dev, D), f32)),
        raws=dict(qkv=qkv_weight, w=quarters(w_y, w_x, "w", firsts.block, rest_given)),
        scratch=[pltpu.VMEM((D, 3 * D - W_CUT), bf16), pltpu.SemaphoreType.DMA((5,))],
        micros=0.1,
    )
    full = shape(adapters.shape, f32)
    new = staged(
        adamw,
        dict(adapters=adapters, first=first_moment, second=second_moment, parts=shares, given=adapters_given),
        dict(grad=full, new=full, first=full, second=full, low=shape(adapters.shape)),
        scalars=dict(chosen=doc_adapter),
        parts=dict(grad=ADAPTERS, new=ADAPTERS, first=ADAPTERS, second=ADAPTERS, low=ADAPTERS),
    )
    return (ends.block[None], ends.tokens[None], new.grad, new.new, new.first, new.second, new.low)


def solution(mesh):
    spread = P(None, None, ("ctx", "wsh"))
    rows = P("wsh", "ctx", None)
    half = P("wsh", None)
    in_specs = (rows, rows, P(), P(), half, half, half, half, P(), spread, spread, spread, half, P("wsh", None, None), half)
    out_specs = (rows, rows, spread, spread, spread, spread, spread)
    return jax.shard_map(on_device, mesh=mesh, in_specs=in_specs, out_specs=out_specs, check_vma=False)
```
